128 devices in a mesh: row: 8 (over z_lo, y), col: 16 (over x, z_hi, core).
Axes of the slice: x: 4, y: 4, z: 4 (z_hi: 2, z_lo: 2; z = z_hi * 2 + z_lo), core: 2. Of those that a mesh axis runs over, the one named last changes fastest.
Arguments:
- x_input: bfloat16 [64, 2048, 256], P('row', 'col'), may hold values from -70 to 70
- grad_output: bfloat16 [64, 2048, 256], P('row', 'col'), may hold values from -6 to 6
- in_scale: float32 [256], replicated, may hold values from 0.5 to 2
- in_shift: float32 [256], replicated, may hold values from -3 to 3
- w_expand: bfloat16 [256, 1024], replicated, may hold values from -0.375 to 0.375
- dw_kernel: float32 [9, 1024], replicated, may hold values from -2 to 2
- w_project: bfloat16 [1024, 256], replicated, may hold values from -0.1875 to 0.1875
- gain_block: float32 [256], replicated, may hold values from 0.5 to 2
- w_qkv_block: bfloat16 [256, 768], replicated, may hold values from -0.375 to 0.375
- w_out_block: bfloat16 [256, 256], replicated, may hold values from -0.375 to 0.375
- bias_block: float32 [8, 225], replicated, may hold values from -3 to 330
- gain_grid: float32 [256], replicated, may hold values from 0.5 to 2
- w_qkv_grid: bfloat16 [256, 768], replicated, may hold values from -0.375 to 0.375
- w_out_grid: bfloat16 [256, 256], replicated, may hold values from -0.375 to 0.375
- bias_grid: float32 [8, 225], replicated, may hold values from -3 to 330
Outputs:
- grad_input: bfloat16 [64, 2048, 256], P('row', 'col')
- grad_expand: float32 [256, 1024], replicated
- grad_kernel: float32 [9, 1024], replicated
- grad_project: float32 [1024, 256], replicated
- grad_qkv_block: float32 [256, 768], replicated
- grad_out_block: float32 [256, 256], replicated
- grad_qkv_grid: float32 [256, 768], replicated
- grad_out_grid: float32 [256, 256], replicated
The draws below stay inside these ranges and needn't reach their ends.
All inputs are finite; a program needn't handle non-finite values.
Results may differ from the reference program's by a relative error of at most 0.02.
Values may be sent and summed in bfloat16 or wider, within the bound.
No kernel may reach another device: no remote copies, remote signals or barrier semaphores. Data moves between devices by JAX's collectives and lax.ppermute only.
A program may use at most 128 MiB of HBM per device.

```python
import math
import jax
import jax.numpy as jnp
from jax import lax

D = 256
E = 1024
HEADS = 8
SLAB_ROWS = 64
SLAB_COLS = 2048


def draw_x_input(key, part):
    key = jax.random.fold_in(key, 7)
    key_base, key_rows, key_cols = jax.random.split(key, 3)
    row_scale = 10.0 ** jax.random.uniform(key_rows, (SLAB_ROWS, SLAB_COLS, 1), jnp.float32, -0.5, 0.5)
    col_scale = 10.0 ** jax.random.uniform(key_cols, (D,), jnp.float32, -0.5, 0.5)
    values = jnp.clip(jax.random.normal(key_base, (SLAB_ROWS, SLAB_COLS, D), jnp.float32), -4.0, 4.0)
    return (values * row_scale * col_scale).astype(jnp.bfloat16)


def draw_bias_block(key, part):
    key = jax.random.fold_in(key, 21)
    key_base = jax.random.fold_in(key, 0)
    return jnp.clip(jax.random.normal(key_base, (HEADS, 225), jnp.float32), -3.0, 3.0)


def draw_bias_grid(key, part):
    key = jax.random.fold_in(key, 33)
    key_base = jax.random.fold_in(key, 0)
    return jnp.clip(jax.random.normal(key_base, (HEADS, 225), jnp.float32), -3.0, 3.0)


def levels(key, extent, cuts, least, top_value):
    gain = 1.0
    for dim, blocks in cuts:
        steps = jax.random.uniform(jax.random.fold_in(jax.random.fold_in(key, 6), dim), (blocks,), jnp.float32, least / len(cuts), top_value / len(cuts))
        gain = gain * jnp.repeat(jnp.exp(steps), extent[dim] // blocks).reshape((-1,) + (1,) * (len(extent) - 1 - dim))
    return gain


def centred(stream_key, dims, deviation, bound, cuts=(), kind=jnp.bfloat16):
    factor_of = levels(stream_key, dims, cuts, -0.22, 0.18) if cuts else 1.0
    values = jax.random.normal(stream_key, dims, jnp.float32) * deviation * factor_of
    return jnp.minimum(jnp.maximum(values, -bound), bound).astype(kind)


def setup_inputs(seed: int = 0) -> dict:
    splits = jax.random.split(jax.random.key(seed), 16)
    x_input = draw_x_input(jax.random.fold_in(splits[15], 71), 0)
    grad_output = centred(splits[1], (SLAB_ROWS, SLAB_COLS, D), 1.0, 6.0, ((0, 8), (1, 16)))
    in_scale = jnp.clip(jnp.exp(jax.random.uniform(splits[2], (D,), jnp.float32, math.log(0.5), math.log(2.0))), 0.5, 2.0)
    in_shift = centred(splits[3], (D,), 0.5, 3.0, (), jnp.float32)
    w_expand = centred(splits[4], (D, E), D ** -0.5, 0.375)
    dw_kernel = centred(splits[5], (9, E), 9 ** -0.5, 2.0, (), jnp.float32)
    w_project = centred(splits[6], (E, D), E ** -0.5, 0.1875)
    gain_block = jnp.clip(jnp.exp(jax.random.uniform(splits[7], (D,), jnp.float32, math.log(0.5), math.log(2.0))), 0.5, 2.0)
    w_qkv_block = centred(splits[8], (D, 3 * D), D ** -0.5, 0.375)
    w_out_block = centred(splits[9], (D, D), D ** -0.5, 0.375)
    bias_block = draw_bias_block(jax.random.fold_in(splits[15], 71), 0)
    gain_grid = jnp.clip(jnp.exp(jax.random.uniform(splits[11], (D,), jnp.float32, math.log(0.5), math.log(2.0))), 0.5, 2.0)
    w_qkv_grid = centred(splits[12], (D, 3 * D), D ** -0.5, 0.375)
    w_out_grid = centred(splits[13], (D, D), D ** -0.5, 0.375)
    bias_grid = draw_bias_grid(jax.random.fold_in(splits[15], 71), 0)
    return dict(x_input=x_input, grad_output=grad_output, in_scale=in_scale, in_shift=in_shift, w_expand=w_expand, dw_kernel=dw_kernel, w_project=w_project, gain_block=gain_block, w_qkv_block=w_qkv_block, w_out_block=w_out_block, bias_block=bias_block, gain_grid=gain_grid, w_qkv_grid=w_qkv_grid, w_out_grid=w_out_grid, bias_grid=bias_grid)


EPSILON = 1e-05

def settle(values):
    return lax.optimization_barrier(values)

def project(left_side, matrix):
    return lax.dot_general(left_side, matrix, (((left_side.ndim - 1,), (0,)), ((), ())), preferred_element_type=jnp.float32)

def project_back(left_side, matrix):
    return lax.dot_general(left_side, matrix, (((left_side.ndim - 1,), (1,)), ((), ())), preferred_element_type=jnp.float32)

def outer_total(left_side, right_side):
    leading = tuple(range(left_side.ndim - 1))
    return lax.dot_general(left_side, right_side, ((leading, leading), ((), ())), preferred_element_type=jnp.float32)

def gelu_slope(values):
    return jax.jvp(jax.nn.gelu, (values,), (jnp.ones_like(values),))[1]

def normalize(values, gain_vec):
    average = lax.optimization_barrier(jnp.mean(values, axis=-1, keepdims=True))
    centered = values - average
    spread = lax.optimization_barrier(jnp.mean(centered * centered, axis=-1, keepdims=True))
    return centered * lax.rsqrt(spread + EPSILON) * gain_vec

def layer_norm(values, gain_vec):
    return normalize(values.astype(jnp.float32), gain_vec).astype(jnp.bfloat16)

def norm_backward(values, gain_vec, grad_normed):
    _, pullback = jax.vjp(lambda inputs: normalize(inputs, gain_vec), values.astype(jnp.float32))
    return pullback(grad_normed.astype(jnp.float32))[0]

def bias_full(bias_table):
    position = jnp.arange(64, dtype=jnp.int32)
    pos_row = position // 8
    pos_col = position % 8
    relative = (pos_row[:, None] - pos_row[None, :] + 7) * 15 + (pos_col[:, None] - pos_col[None, :] + 7)
    onehot = (relative[:, :, None] == jnp.arange(225, dtype=jnp.int32)[None, None, :]).astype(jnp.float32)
    return jnp.einsum('pqr,hr->hpq', onehot, bias_table, precision=lax.Precision.HIGHEST)

def attend_core(query_part, key_part, value_part, bias_cube):
    query_part, key_part, value_part = settle((query_part, key_part, value_part))
    groups, places, features = query_part.shape
    head_size = features // HEADS
    query_heads = query_part.astype(jnp.float32).reshape(groups, places, HEADS, head_size)
    key_heads = key_part.astype(jnp.float32).reshape(groups, places, HEADS, head_size)
    value_heads = value_part.astype(jnp.float32).reshape(groups, places, HEADS, head_size)
    scores = jnp.einsum('gphd,gqhd->ghpq', query_heads, key_heads, precision=lax.Precision.HIGHEST) * head_size ** (-0.5) + bias_cube[None]
    weights = settle(jax.nn.softmax(scores, axis=-1).astype(jnp.bfloat16))
    mixture = jnp.einsum('ghpq,gqhd->gphd', weights.astype(jnp.float32), value_heads, precision=lax.Precision.HIGHEST)
    return mixture.reshape(groups, places, features).astype(jnp.bfloat16)

def attend_front(normed, w_qkv):
    features = normed.shape[-1]
    joined = project(normed, w_qkv)
    return (joined[..., :features].astype(jnp.bfloat16), joined[..., features:2 * features].astype(jnp.bfloat16), joined[..., 2 * features:].astype(jnp.bfloat16))

def attend_grads(normed, query_part, key_part, value_part, grad_out, w_qkv, w_out, bias_cube):
    mixture, pullback = jax.vjp(lambda a_part, b_part, c_part: attend_core(a_part, b_part, c_part, bias_cube), query_part, key_part, value_part)
    total_out = outer_total(mixture, grad_out)
    grad_mixture = project_back(grad_out, w_out).astype(jnp.bfloat16)
    grad_query, grad_key, grad_value = pullback(grad_mixture)
    grad_joined = jnp.concatenate([grad_query, grad_key, grad_value], axis=-1)
    total_qkv = outer_total(normed, grad_joined)
    grad_normed = project_back(grad_joined, w_qkv).astype(jnp.bfloat16)
    return (grad_normed, total_qkv, total_out)

def to_windows(tile_cells):
    tile_rows, tile_cols, channels = tile_cells.shape
    return tile_cells.reshape(tile_rows // 8, 8, tile_cols // 8, 8, channels).transpose(0, 2, 1, 3, 4).reshape(-1, 64, channels)

def from_windows(windows, tile_rows, tile_cols):
    channels = windows.shape[-1]
    return windows.reshape(tile_rows // 8, tile_cols // 8, 8, 8, channels).transpose(0, 2, 1, 3, 4).reshape(tile_rows, tile_cols, channels)

def expand_front(row_block, inside, in_scale, in_shift, w_expand):
    shifted = (row_block.astype(jnp.float32) * in_scale + in_shift).astype(jnp.bfloat16)
    preact = project(shifted, w_expand)
    lifted = jnp.where(inside, jax.nn.gelu(preact), 0.0).astype(jnp.bfloat16)
    return (shifted, preact, settle(lifted))

def depthwise(padded, kernel, row_count, col_count):
    summed = jnp.zeros((row_count, col_count, padded.shape[-1]), jnp.float32)
    for offset in range(9):
        row_off, col_off = (offset // 3, offset % 3)
        summed = summed + kernel[offset] * padded[row_off:row_off + row_count, col_off:col_off + col_count].astype(jnp.float32)
    return summed

def depthwise_back(padded, kernel, row_count, col_count):
    summed = jnp.zeros((row_count, col_count, padded.shape[-1]), jnp.float32)
    for offset in range(9):
        row_off, col_off = (offset // 3, offset % 3)
        summed = summed + kernel[offset] * padded[2 - row_off:2 - row_off + row_count, 2 - col_off:2 - col_off + col_count].astype(jnp.float32)
    return summed

def kernel_grad(padded, grad_inner, row_count, col_count):
    grad_values = grad_inner.astype(jnp.float32)
    return jnp.stack([lax.optimization_barrier(jnp.sum(padded[offset // 3:offset // 3 + row_count, offset % 3:offset % 3 + col_count].astype(jnp.float32) * grad_values, axis=(0, 1))) for offset in range(9)])

def reference(x_input, grad_output, in_scale, in_shift, w_expand, dw_kernel, w_project, gain_block, w_qkv_block, w_out_block, bias_block, gain_grid, w_qkv_grid, w_out_grid, bias_grid):
    slab_rows, slab_cols, features = x_input.shape
    expanded = w_expand.shape[1]
    band_rows = 8
    band_count = slab_rows // band_rows
    band_ids = jnp.arange(band_count, dtype=jnp.int32)
    padded_input = jnp.pad(x_input, ((2, 2), (1, 1), (0, 0)))
    col_ids = jnp.arange(slab_cols + 2, dtype=jnp.int32)
    col_inside = (col_ids >= 1) & (col_ids <= slab_cols)
    block_cube = bias_full(bias_block)
    grid_cube = bias_full(bias_grid)
    empty_carry = jnp.zeros((), jnp.float32)

    def front_rows(first_row, row_count):
        row_block = lax.dynamic_slice_in_dim(padded_input, first_row, row_count, 0)
        global_row = first_row - 2 + jnp.arange(row_count, dtype=jnp.int32)
        inside = ((global_row >= 0) & (global_row < slab_rows))[:, None, None] & col_inside[None, :, None]
        return expand_front(row_block, inside, in_scale, in_shift, w_expand)

    def forward_band(totals, band_index):
        first_row = (band_index * band_rows).astype(jnp.int32)
        lifted = front_rows(first_row + 1, band_rows + 2)[2]
        convolved = depthwise(lifted, dw_kernel, band_rows, slab_cols)
        second = jax.nn.gelu(convolved).astype(jnp.bfloat16)
        base_rows = lax.dynamic_slice_in_dim(x_input, first_row, band_rows, 0)
        return (totals, (base_rows.astype(jnp.float32) + project(second, w_project)).astype(jnp.bfloat16))
    section_one = lax.scan(forward_band, empty_carry, band_ids)[1]
    section_one = settle(section_one.reshape(slab_rows, slab_cols, features))

    def block_band(totals, band_index):
        first_row = (band_index * band_rows).astype(jnp.int32)
        row_block = lax.dynamic_slice_in_dim(section_one, first_row, band_rows, 0)
        windows = to_windows(layer_norm(row_block, gain_block))
        projected = attend_front(windows, w_qkv_block)
        attended = project(attend_core(projected[0], projected[1], projected[2], block_cube), w_out_block)
        return (totals, (row_block.astype(jnp.float32) + from_windows(attended, band_rows, slab_cols)).astype(jnp.bfloat16))
    section_two = lax.scan(block_band, empty_carry, band_ids)[1]
    section_two = settle(section_two.reshape(slab_rows, slab_cols, features))
    normed_grid = layer_norm(section_two, gain_grid)
    step_rows = slab_rows // 8
    step_cols = slab_cols // 8
    grid_normed = normed_grid.reshape(8, step_rows, 8, step_cols, features).transpose(1, 3, 0, 2, 4).reshape(step_rows, step_cols, 64, features)
    grid_grads = grad_output.reshape(8, step_rows, 8, step_cols, features).transpose(1, 3, 0, 2, 4).reshape(step_rows, step_cols, 64, features)

    def grid_step(totals, pieces):
        normed, grad_out = pieces
        projected = attend_front(normed, w_qkv_grid)
        grad_normed, total_qkv, total_out = attend_grads(normed, projected[0], projected[1], projected[2], grad_out, w_qkv_grid, w_out_grid, grid_cube)
        return ((totals[0] + total_qkv, totals[1] + total_out), grad_normed)
    zero_totals = (jnp.zeros((features, 3 * features), jnp.float32), jnp.zeros((features, features), jnp.float32))
    grid_totals, grad_grid = lax.scan(grid_step, zero_totals, (grid_normed, grid_grads))
    grad_normed_grid = grad_grid.reshape(step_rows, step_cols, 8, 8, features).transpose(2, 0, 3, 1, 4).reshape(slab_rows, slab_cols, features)
    grad_normed_grid = settle(grad_normed_grid)
    grad_section_two = settle((grad_output.astype(jnp.float32) + norm_backward(section_two, gain_grid, grad_normed_grid)).astype(jnp.bfloat16))

    def block_back(totals, band_index):
        first_row = (band_index * band_rows).astype(jnp.int32)
        row_block = lax.dynamic_slice_in_dim(section_one, first_row, band_rows, 0)
        grad_block = lax.dynamic_slice_in_dim(grad_section_two, first_row, band_rows, 0)
        windows = to_windows(layer_norm(row_block, gain_block))
        projected = attend_front(windows, w_qkv_block)
        grad_normed, total_qkv, total_out = attend_grads(windows, projected[0], projected[1], projected[2], to_windows(grad_block), w_qkv_block, w_out_block, block_cube)
        grad_rows = settle(from_windows(grad_normed, band_rows, slab_cols))
        result = (grad_block.astype(jnp.float32) + norm_backward(row_block, gain_block, grad_rows)).astype(jnp.bfloat16)
        return ((totals[0] + total_qkv, totals[1] + total_out), result)
    block_totals, grad_section_one = lax.scan(block_back, zero_totals, band_ids)
    grad_section_one = settle(grad_section_one.reshape(slab_rows, slab_cols, features))
    padded_grad = jnp.pad(grad_section_one, ((1, 1), (0, 0), (0, 0)))

    def conv_back(totals, band_index):
        first_row = (band_index * band_rows).astype(jnp.int32)
        shifted, preact, lifted = front_rows(first_row, band_rows + 4)
        convolved = depthwise(lifted, dw_kernel, band_rows + 2, slab_cols)
        grad_rows = lax.dynamic_slice_in_dim(padded_grad, first_row, band_rows + 2, 0)
        through = project_back(grad_rows, w_project)
        grad_inner = settle((through * gelu_slope(convolved)).astype(jnp.bfloat16))
        padded_inner = jnp.pad(grad_inner, ((0, 0), (1, 1), (0, 0)))
        grad_lifted = depthwise_back(padded_inner, dw_kernel, band_rows, slab_cols)
        core_preact = preact[2:band_rows + 2, 1:slab_cols + 1]
        grad_preact = (grad_lifted * gelu_slope(core_preact)).astype(jnp.bfloat16)
        core_shifted = shifted[2:band_rows + 2, 1:slab_cols + 1]
        second = jax.nn.gelu(convolved[1:band_rows + 1]).astype(jnp.bfloat16)
        grad_middle = grad_rows[1:band_rows + 1]
        total_project = outer_total(second, grad_middle)
        total_kernel = kernel_grad(lifted[1:band_rows + 3], grad_inner[1:band_rows + 1], band_rows, slab_cols)
        total_expand = outer_total(core_shifted, grad_preact)
        returned = project_back(grad_preact, w_expand)
        result = (grad_middle.astype(jnp.float32) + returned * in_scale).astype(jnp.bfloat16)
        return ((totals[0] + total_expand, totals[1] + total_kernel, totals[2] + total_project), result)
    conv_zero = (jnp.zeros((features, expanded), jnp.float32), jnp.zeros((9, expanded), jnp.float32), jnp.zeros((expanded, features), jnp.float32))
    conv_totals, grad_input = lax.scan(conv_back, conv_zero, band_ids)
    grad_input = grad_input.reshape(slab_rows, slab_cols, features)
    factor = (slab_rows * slab_cols) ** (-0.5)
    return (grad_input, conv_totals[0] * factor, conv_totals[1] * factor, conv_totals[2] * factor, block_totals[0] * factor, block_totals[1] * factor, grid_totals[0] * factor, grid_totals[1] * factor)
```

```python
import jax
import jax.numpy as jnp
from jax import lax
from jax.experimental import pallas as pl
from jax.experimental.pallas import tpu as pltpu
from jax.sharding import Mesh
from jax.sharding import PartitionSpec as P

F32 = jnp.float32
BF16 = jnp.bfloat16
EPSILON = 1e-05
HEADS = 8
HEAD = 32
SCALE = HEAD ** (-0.5)
ROWS = 8
COLS = 128
TOKENS = ROWS * COLS
D = 256
E = 1024
BLOCKS = E // 128
LEFT = 8
WIDE = COLS + 2 * LEFT
GELU_1 = 0.7978845608028654
GELU_3 = 0.044715 * GELU_1


def dot(left, right, left_dim, right_dim):
    return lax.dot_general(
        left, right, (((left_dim,), (right_dim,)), ((), ())), preferred_element_type=F32
    )


def gelu_pair(values):
    square = values * values
    half = 0.5 + 0.5 * jnp.tanh(values * (GELU_1 + GELU_3 * square))
    value = values * half
    slope = half + value * (1.0 - half) * (2.0 * GELU_1 + (6.0 * GELU_3) * square)
    return value, slope


def norm_parts(values):
    centered = values - jnp.mean(values, axis=-1, keepdims=True)
    spread = jnp.mean(centered * centered, axis=-1, keepdims=True)
    inverse = lax.rsqrt(spread + EPSILON)
    return centered * inverse, inverse


def norm_back(values, gain, grad):
    unit, inverse = norm_parts(values)
    scaled = grad * gain
    mean_grad = jnp.mean(scaled, axis=-1, keepdims=True)
    mean_unit = jnp.mean(scaled * unit, axis=-1, keepdims=True)
    return inverse * (scaled - mean_grad - unit * mean_unit)


def four_windows(cells):
    return jnp.concatenate(
        [cells[:, 8 * m : 8 * m + 8, :].reshape(64, D) for m in range(4)], axis=0
    )


def from_four_windows(tokens):
    return jnp.concatenate(
        [tokens[64 * m : 64 * m + 64].reshape(8, 8, D) for m in range(4)], axis=1
    )


def make_bias(rows_ref, bias_ref):
    for head in range(HEADS):
        rows = rows_ref[head]
        for a_k in range(8):
            start = 8 * (7 - a_k)
            bias_ref[
                head // 4, 8 * a_k : 8 * a_k + 8, 64 * (head % 4) : 64 * (head % 4) + 64
            ] = rows[:, start : start + 64]


def stacked(part, heads_mask):
    return jnp.concatenate([part] * 4, axis=0) * heads_mask


def pick(product):
    lane = lax.broadcasted_iota(jnp.int32, (64, 128), 1)
    low = jnp.where(lane < 32, product[0:64], product[64:128])
    high = jnp.where(lane < 96, product[128:192], product[192:256])
    return jnp.where(lane < 64, low, high)


def softmax_keys(scores):
    shifted = jnp.exp(scores - jnp.max(scores, axis=0, keepdims=True))
    return shifted * (1.0 / jnp.sum(shifted, axis=0, keepdims=True))


def half_of(joined, part, half, group):
    start = part * D + half * 128
    return joined[64 * group : 64 * group + 64, start : start + 128]


def attend(joined, bias_ref, heads_mask, group, half):
    query = half_of(joined, 0, half, group)
    key = half_of(joined, 1, half, group)
    value = half_of(joined, 2, half, group)
    query_stack = stacked(query, heads_mask)
    probs = softmax_keys(dot(key, query_stack, 1, 1) * SCALE + bias_ref[half])
    mixture = pick(dot(probs.astype(BF16), value, 0, 0)).astype(BF16)
    return probs, mixture


def attend_back(joined, probs, grad_mix, heads_mask, group, half):
    query = half_of(joined, 0, half, group)
    key = half_of(joined, 1, half, group)
    value = half_of(joined, 2, half, group)
    query_stack = stacked(query, heads_mask)
    grad_stack = stacked(grad_mix, heads_mask)
    grad_weights = dot(value, grad_stack, 1, 1).astype(BF16).astype(F32)
    centre = jnp.sum(grad_weights * probs, axis=0, keepdims=True)
    grad_scores = (probs * (grad_weights - centre) * SCALE).astype(BF16)
    grad_value = dot(probs.astype(BF16), grad_stack, 1, 0).astype(BF16)
    grad_key = dot(grad_scores, query_stack, 1, 0).astype(BF16)
    grad_query = pick(dot(grad_scores, key, 0, 0)).astype(BF16)
    return grad_query, grad_key, grad_value


def heads_mask_of():
    row = lax.broadcasted_iota(jnp.int32, (256, 128), 0) // 64
    lane = lax.broadcasted_iota(jnp.int32, (256, 128), 1) // HEAD
    return jnp.where(row == lane, 1.0, 0.0).astype(BF16)


def attention_totals(total_ref, normed_ref, grad_joined_ref, mixture_ref, grad_ref):
    for part in range(3):
        total = dot(normed_ref[...], grad_joined_ref[:, D * part : D * part + D], 0, 0)
        for k in range(2):
            start = 256 * (2 * part + k)
            total_ref[start : start + 256, :] = total[:, 128 * k : 128 * k + 128]
    total = dot(mixture_ref[...], grad_ref[...], 0, 0)
    for k in range(2):
        total_ref[1536 + 256 * k : 1792 + 256 * k, :] = total[:, 128 * k : 128 * k + 128]


def front_kernel(
    edge_ref,
    x_ref,
    top_ref,
    bottom_ref,
    side_ref,
    scale_ref,
    shift_ref,
    w_expand_ref,
    dw_ref,
    w_project_ref,
    gain_block_ref,
    w_qkv_ref,
    w_out_ref,
    rows_ref,
    gain_grid_ref,
    lifted_ref,
    slope_pre_ref,
    second_ref,
    slope_conv_ref,
    section_one_ref,
    section_two_ref,
    normed_grid_ref,
    normed_block_ref,
    joined_ref,
    probs_ref,
    mixture_ref,
    pad,
    cells,
    outcome,
    bias,
):
    make_bias(rows_ref, bias)
    heads_mask = heads_mask_of()

    def shifted_of(tokens):
        return (tokens.astype(F32) * scale_ref[...] + shift_ref[...]).astype(BF16)

    for source, row, flag in ((top_ref, 0, edge_ref[0]), (bottom_ref, 9, edge_ref[1])):
        shifted = shifted_of(source[...])
        for pair in range(4):
            value, _ = gelu_pair(dot(shifted, w_expand_ref[:, 256 * pair : 256 * pair + 256], 1, 0))
            value = value.astype(BF16).astype(F32) * flag
            for k in range(2):
                pad[2 * pair + k, row, LEFT : LEFT + COLS, :] = value[:, 128 * k : 128 * k + 128]
    shifted = shifted_of(side_ref[...])
    place = lax.broadcasted_iota(jnp.int32, (32, 1), 0)
    flags = jnp.where(place < 16, edge_ref[2], edge_ref[3])
    flags = flags * jnp.where(place % 16 == 0, edge_ref[0], 1.0)
    flags = flags * jnp.where(place % 16 == 9, edge_ref[1], 1.0)
    for pair in range(4):
        value, _ = gelu_pair(dot(shifted, w_expand_ref[:, 256 * pair : 256 * pair + 256], 1, 0))
        value = value.astype(BF16).astype(F32) * flags
        for k in range(2):
            for row in range(10):
                part = value[:, 128 * k : 128 * k + 128]
                pad[2 * pair + k, row, LEFT - 1 : LEFT, :] = part[row : row + 1]
                pad[2 * pair + k, row, LEFT + COLS : LEFT + COLS + 1, :] = part[16 + row : 17 + row]

    @pl.loop(0, ROWS)
    def _(row):
        here = pl.ds(pl.multiple_of(row * COLS, COLS), COLS)
        shifted = shifted_of(x_ref[here, :])
        for pair in range(4):
            value, slope = gelu_pair(
                dot(shifted, w_expand_ref[:, 256 * pair : 256 * pair + 256], 1, 0)
            )
            value = value.astype(BF16)
            slope = slope.astype(BF16)
            for k in range(2):
                lanes = slice(128 * k, 128 * k + 128)
                lifted_ref[2 * pair + k, here, :] = value[:, lanes]
                slope_pre_ref[2 * pair + k, here, :] = slope[:, lanes]
                pad[2 * pair + k, row + 1, LEFT : LEFT + COLS, :] = value[:, lanes].astype(F32)

    @pl.loop(0, BLOCKS)
    def _(block):
        taps = [
            dw_ref[t : t + 1, pl.ds(pl.multiple_of(block * 128, 128), 128)] for t in range(9)
        ]

        @pl.loop(0, ROWS)
        def _(row):
            for chunk in range(4):
                summed = None
                for t in range(9):
                    start = LEFT - 1 + t % 3 + 32 * chunk
                    term = taps[t] * pad[block, row + t // 3, start : start + 32, :]
                    summed = term if summed is None else summed + term
                value, slope = gelu_pair(summed)
                here = pl.ds(pl.multiple_of(row * COLS + 32 * chunk, 32), 32)
                second_ref[block, here, :] = value.astype(BF16)
                slope_conv_ref[block, here, :] = slope.astype(BF16)

    @pl.loop(0, 4)
    def _(part):
        here = pl.ds(pl.multiple_of(part * 256, 256), 256)
        summed = x_ref[here, :].astype(F32)
        for pair in range(4):
            joined = jnp.concatenate(
                [second_ref[2 * pair, here, :], second_ref[2 * pair + 1, here, :]], axis=1
            )
            summed = summed + dot(joined, w_project_ref[256 * pair : 256 * pair + 256, :], 1, 0)
        section_one = summed.astype(BF16)
        section_one_ref[here, :] = section_one
        cells[pl.ds(part * 2, 2)] = section_one.astype(F32).reshape(2, COLS, D)

    @pl.loop(0, 4)
    def _(part):
        here = pl.ds(pl.multiple_of(part * 256, 256), 256)
        columns = pl.ds(pl.multiple_of(part * 32, 32), 32)
        section_one = four_windows(cells[:, columns, :])
        normed = (norm_parts(section_one)[0] * gain_block_ref[...]).astype(BF16)
        normed_block_ref[here, :] = normed
        joined = dot(normed, w_qkv_ref[...], 1, 0).astype(BF16)
        joined_ref[here, :] = joined
        mixtures = []
        for group in range(4):
            halves = []
            for half in range(2):
                probs, mixture = attend(joined, bias, heads_mask, group, half)
                probs_ref[part * 8 + group * 2 + half] = probs
                halves.append(mixture)
            mixtures.append(jnp.concatenate(halves, axis=1))
        mixture = jnp.concatenate(mixtures, axis=0)
        mixture_ref[here, :] = mixture
        section_two = (section_one + dot(mixture, w_out_ref[...], 1, 0)).astype(BF16).astype(F32)
        cells[:, columns, :] = from_four_windows(section_two)
        normed = norm_parts(section_two)[0] * gain_grid_ref[...]
        outcome[:, columns, :] = from_four_windows(normed)

    section_two_ref[...] = cells[...].reshape(TOKENS, D).astype(BF16)
    normed_grid_ref[...] = outcome[...].reshape(TOKENS, D).astype(BF16)


def grid_kernel(
    normed_ref,
    grad_ref,
    w_qkv_ref,
    w_out_ref,
    rows_ref,
    grad_normed_ref,
    total_ref,
    bias,
    mixture_ref,
    grad_joined_ref,
):
    make_bias(rows_ref, bias)
    heads_mask = heads_mask_of()

    @pl.loop(0, 4)
    def _(part):
        here = pl.ds(pl.multiple_of(part * 256, 256), 256)
        joined = dot(normed_ref[here, :], w_qkv_ref[...], 1, 0).astype(BF16)
        grad_mix = dot(grad_ref[here, :], w_out_ref[...], 1, 1).astype(BF16)
        mixtures = []
        grads = []
        for group in range(4):
            halves = []
            pieces = []
            for half in range(2):
                probs, mixture = attend(joined, bias, heads_mask, group, half)
                halves.append(mixture)
                grad_half = half_of(grad_mix, 0, half, group)
                pieces.append(attend_back(joined, probs, grad_half, heads_mask, group, half))
            mixtures.append(jnp.concatenate(halves, axis=1))
            grads.append(
                jnp.concatenate([pieces[half][k] for k in range(3) for half in range(2)], axis=1)
            )
        mixture_ref[here, :] = jnp.concatenate(mixtures, axis=0)
        grad_joined = jnp.concatenate(grads, axis=0)
        grad_joined_ref[here, :] = grad_joined
        grad_normed_ref[here, :] = dot(grad_joined, w_qkv_ref[...], 1, 1).astype(BF16)

    attention_totals(total_ref, normed_ref, grad_joined_ref, mixture_ref, grad_ref)


def block_kernel(
    returned_ref,
    grad_output_ref,
    section_two_ref,
    section_one_ref,
    normed_block_ref,
    joined_ref,
    probs_ref,
    mixture_ref,
    second_ref,
    slope_conv_ref,
    gain_grid_ref,
    gain_block_ref,
    w_qkv_ref,
    w_out_ref,
    w_project_ref,
    grad_one_ref,
    inner_ref,
    total_ref,
    cells,
    base,
    grad_windows_ref,
    grad_joined_ref,
):
    heads_mask = heads_mask_of()

    @pl.loop(0, ROWS)
    def _(row):
        here = pl.ds(pl.multiple_of(row * COLS, COLS), COLS)
        grad = grad_output_ref[here, :].astype(F32) + norm_back(
            section_two_ref[here, :].astype(F32),
            gain_grid_ref[...],
            returned_ref[here, :].astype(F32),
        )
        cells[row] = grad.astype(BF16).astype(F32)
        base[row] = section_one_ref[here, :].astype(F32)

    @pl.loop(0, 4)
    def _(part):
        here = pl.ds(pl.multiple_of(part * 256, 256), 256)
        columns = pl.ds(pl.multiple_of(part * 32, 32), 32)
        grad_two = four_windows(cells[:, columns, :])
        grad_windows = grad_two.astype(BF16)
        grad_windows_ref[here, :] = grad_windows
        joined = joined_ref[here, :]
        grad_mix = dot(grad_windows, w_out_ref[...], 1, 1).astype(BF16)
        grads = []
        for group in range(4):
            pieces = []
            for half in range(2):
                probs = probs_ref[part * 8 + group * 2 + half]
                grad_half = half_of(grad_mix, 0, half, group)
                pieces.append(attend_back(joined, probs, grad_half, heads_mask, group, half))
            grads.append(
                jnp.concatenate([pieces[half][k] for k in range(3) for half in range(2)], axis=1)
            )
        grad_joined = jnp.concatenate(grads, axis=0)
        grad_joined_ref[here, :] = grad_joined
        grad_normed = dot(grad_joined, w_qkv_ref[...], 1, 1).astype(BF16).astype(F32)
        section_one = four_windows(base[:, columns, :])
        grad_one = grad_two + norm_back(section_one, gain_block_ref[...], grad_normed)
        cells[:, columns, :] = from_four_windows(grad_one)

    @pl.loop(0, ROWS)
    def _(row):
        here = pl.ds(pl.multiple_of(row * COLS, COLS), COLS)
        grad_one = cells[row].astype(BF16)
        grad_one_ref[here, :] = grad_one
        for pair in range(4):
            through = dot(grad_one, w_project_ref[256 * pair : 256 * pair + 256, :], 1, 1)
            for k in range(2):
                block = 2 * pair + k
                slope = slope_conv_ref[block, here, :].astype(F32)
                inner = through[:, 128 * k : 128 * k + 128] * slope
                inner_ref[block, here, :] = inner.astype(BF16)

    attention_totals(total_ref, normed_block_ref, grad_joined_ref, mixture_ref, grad_windows_ref)
    for block in range(BLOCKS):
        total = dot(second_ref[block], grad_one_ref[...], 0, 0)
        for k in range(2):
            start = 2048 + 1024 * k + 128 * block
            total_ref[start : start + 128, :] = total[:, 128 * k : 128 * k + 128]


def back_kernel(
    x_ref,
    lifted_ref,
    slope_pre_ref,
    inner_ref,
    grad_one_ref,
    top_ref,
    bottom_ref,
    side_ref,
    scale_ref,
    shift_ref,
    w_expand_ref,
    dw_ref,
    grad_input_ref,
    total_expand_ref,
    total_kernel_ref,
    pad,
    preact_ref,
    shifted_ref,
):
    for block in range(BLOCKS):
        pad[block, 0, LEFT : LEFT + COLS, :] = top_ref[block].astype(F32)
        pad[block, 9, LEFT : LEFT + COLS, :] = bottom_ref[block].astype(F32)
        side = side_ref[block].astype(F32)
        for row in range(10):
            pad[block, row, LEFT - 1 : LEFT, :] = side[row : row + 1]
            pad[block, row, LEFT + COLS : LEFT + COLS + 1, :] = side[16 + row : 17 + row]

    @pl.loop(0, BLOCKS)
    def _(block):
        taps = [
            dw_ref[t : t + 1, pl.ds(pl.multiple_of(block * 128, 128), 128)] for t in range(9)
        ]

        @pl.loop(0, ROWS)
        def _(row):
            here = pl.ds(pl.multiple_of(row * COLS, COLS), COLS)
            pad[block, row + 1, LEFT : LEFT + COLS, :] = inner_ref[block, here, :].astype(F32)

        def step(row, totals):
            totals = list(totals)
            for chunk in range(4):
                here = pl.ds(pl.multiple_of(row * COLS + 32 * chunk, 32), 32)
                lifted = lifted_ref[block, here, :].astype(F32)
                summed = None
                for t in range(9):
                    start = LEFT + 1 - t % 3 + 32 * chunk
                    cells = pad[block, row + 2 - t // 3, start : start + 32, :]
                    term = taps[t] * cells
                    summed = term if summed is None else summed + term
                    totals[t] = totals[t] + jnp.sum((lifted * cells).reshape(4, 8, 128), axis=0)
                grad = summed * slope_pre_ref[block, here, :].astype(F32)
                preact_ref[block, here, :] = grad.astype(BF16)
            return tuple(totals)

        totals = lax.fori_loop(0, ROWS, step, (jnp.zeros((8, 128), F32),) * 9)
        for t in range(9):
            total_kernel_ref[t, pl.ds(block, 1), :] = jnp.sum(totals[t], axis=0, keepdims=True)

    @pl.loop(0, 4)
    def _(part):
        here = pl.ds(pl.multiple_of(part * 256, 256), 256)
        summed = jnp.zeros((256, D), F32)
        for pair in range(4):
            joined = jnp.concatenate(
                [preact_ref[2 * pair, here, :], preact_ref[2 * pair + 1, here, :]], axis=1
            )
            summed = summed + dot(joined, w_expand_ref[:, 256 * pair : 256 * pair + 256], 1, 1)
        grad_one = grad_one_ref[here, :].astype(F32)
        grad_input_ref[here, :] = (grad_one + summed * scale_ref[...]).astype(BF16)
        shifted_ref[here, :] = (
            x_ref[here, :].astype(F32) * scale_ref[...] + shift_ref[...]
        ).astype(BF16)

    for pair in range(4):
        joined = jnp.concatenate([preact_ref[2 * pair], preact_ref[2 * pair + 1]], axis=1)
        total = dot(shifted_ref[...], joined, 0, 0)
        for k in range(2):
            start = 256 * (2 * pair + k)
            total_expand_ref[start : start + 256, :] = total[:, 128 * k : 128 * k + 128]


VMEM = pl.BlockSpec(memory_space=pltpu.VMEM)
SMEM = pl.BlockSpec(memory_space=pltpu.SMEM)
PARAMS = pltpu.CompilerParams(vmem_limit_bytes=60 * 1024 * 1024)


def shape(dims, kind):
    return jax.ShapeDtypeStruct(dims, kind)


def call(kernel, ins, outs, scratch, smem_first=False):
    specs = [VMEM] * len(ins)
    if smem_first:
        specs[0] = SMEM
    return pl.pallas_call(
        kernel,
        out_shape=outs,
        in_specs=specs,
        out_specs=[VMEM] * len(outs),
        scratch_shapes=scratch,
        compiler_params=PARAMS,
    )(*ins)


def bias_rows(table):
    cube = table.reshape(HEADS, 15, 15)
    rows = jnp.stack([cube[:, :, 7 - e : 15 - e] for e in range(8)], axis=1)
    return jnp.pad(rows.reshape(HEADS, 8, 120), ((0, 0), (0, 0), (0, 8)))


CHUNKS = 64
CHUNK = 72
FACTOR = float((64 * 2048) ** (-0.5))


def pack_kernel(core_ref, block_ref, grid_ref, expand_ref, taps_ref, send_ref, keep_ref):
    core = core_ref[0]

    def low(index):
        return block_ref[64 * index : 64 * index + 64, :], jnp.zeros((8, 128), F32)

    def high(index):
        start = 64 * (index % 32)
        source = grid_ref if index < 32 else expand_ref
        tap = taps_ref[index] if index < 9 else jnp.zeros((8, 128), F32)
        return source[start : start + 64, :], tap

    def fill(kept, sent):
        for index in range(CHUNKS):
            keep_ref[index, :64, :], keep_ref[index, 64:, :] = kept(index)
            send_ref[index] = jnp.concatenate(sent(index), axis=0).astype(BF16)

    @pl.when(core == 0)
    def _():
        fill(low, high)

    @pl.when(core == 1)
    def _():
        fill(high, low)


def pair_kernel(keep_ref, got_ref, out_ref):
    for index in range(CHUNKS):
        out_ref[index] = (keep_ref[index] + got_ref[index].astype(F32)).astype(BF16)


def sum_kernel(got_ref, out_ref):
    def step(index, total):
        return total + got_ref[index].astype(F32)

    total = lax.fori_loop(0, CHUNKS, step, jnp.zeros((CHUNK, 128), F32), unroll=8)
    total = total.astype(BF16)
    for index in range(CHUNKS):
        out_ref[index] = total


def unpack_kernel(
    core_ref,
    mine_ref,
    other_ref,
    expand_ref,
    kernel_ref,
    project_ref,
    qkv_block_ref,
    out_block_ref,
    qkv_grid_ref,
    out_grid_ref,
):
    core = core_ref[0]

    def place(target, row, column, value):
        target[row : row + 64, column : column + 128] = value

    def fill(low_ref, high_ref):
        for index in range(CHUNKS):
            value = low_ref[index].astype(F32) * FACTOR
            start = 64 * index
            if start < 1536:
                place(qkv_block_ref, start % 256, start // 256 * 128, value[:64])
            elif start < 2048:
                place(out_block_ref, start % 256, (start - 1536) // 256 * 128, value[:64])
            else:
                place(project_ref, start % 1024, (start - 2048) // 1024 * 128, value[:64])
            value = high_ref[index].astype(F32) * FACTOR
            if start < 1536:
                place(qkv_grid_ref, start % 256, start // 256 * 128, value[:64])
            elif start < 2048:
                place(out_grid_ref, start % 256, (start - 1536) // 256 * 128, value[:64])
            else:
                place(expand_ref, start % 256, (start - 2048) // 256 * 128, value[:64])
            if index < 9:
                for block in range(BLOCKS):
                    kernel_ref[index : index + 1, 128 * block : 128 * block + 128] = value[
                        64 + block : 65 + block
                    ]

    @pl.when(core == 0)
    def _():
        fill(mine_ref, other_ref)

    @pl.when(core == 1)
    def _():
        fill(other_ref, mine_ref)


def beside_rows(first, last, fill_axis="row"):
    count = lax.axis_size(fill_axis)
    down = [(i, i + 1) for i in range(count - 1)]
    up = [(i + 1, i) for i in range(count - 1)]
    return lax.ppermute(last, fill_axis, down), lax.ppermute(first, fill_axis, up)


def beside_columns(first, last):
    axes = ("hi", "core")
    count = lax.axis_size("hi") * lax.axis_size("core")
    right = [(i, i + 1) for i in range(count - 1)]
    left = [(i + 1, i) for i in range(count - 1)]
    return lax.ppermute(last, axes, right), lax.ppermute(first, axes, left)


def across(values):
    return lax.all_to_all(values, ("row", "hi"), split_axis=0, concat_axis=0, tiled=True)


def sibling(values):
    return lax.ppermute(values, "core", [(0, 1), (1, 0)])


def shards(
    x_input,
    grad_output,
    in_scale,
    in_shift,
    w_expand,
    dw_kernel,
    w_project,
    gain_block,
    w_qkv_block,
    w_out_block,
    bias_block,
    gain_grid,
    w_qkv_grid,
    w_out_grid,
    bias_grid,
):
    row_index = lax.axis_index("row")
    core = lax.axis_index("core")
    col_index = lax.axis_index("hi") * 2 + core
    edge = jnp.stack(
        [
            row_index > 0,
            row_index < lax.axis_size("row") - 1,
            col_index > 0,
            col_index < lax.axis_size("hi") * 2 - 1,
        ]
    ).astype(F32)
    core_flag = core.reshape(1).astype(jnp.int32)
    scale = in_scale.reshape(1, D)
    shift = in_shift.reshape(1, D)
    gain_block = gain_block.reshape(1, D)
    gain_grid = gain_grid.reshape(1, D)
    rows_block = bias_rows(bias_block)
    rows_grid = bias_rows(bias_grid)

    x_top, x_bottom = beside_rows(x_input[0], x_input[ROWS - 1])
    ends = [
        jnp.concatenate([x_top[c : c + 1], x_input[:, c], x_bottom[c : c + 1]], axis=0)
        for c in (0, COLS - 1)
    ]
    ends = [jnp.pad(e, ((0, 6), (0, 0))) for e in ends]
    x_side = jnp.concatenate(beside_columns(ends[0], ends[1]), axis=0)
    x_flat = x_input.reshape(TOKENS, D)
    grad_flat = grad_output.reshape(TOKENS, D)
    hidden = shape((BLOCKS, TOKENS, 128), BF16)
    tokens = shape((TOKENS, D), BF16)
    (
        lifted,
        slope_pre,
        second,
        slope_conv,
        section_one,
        section_two,
        normed_grid,
        normed_block,
        joined,
        probs,
        mixture,
    ) = call(
        front_kernel,
        [
            edge,
            x_flat,
            x_top,
            x_bottom,
            x_side,
            scale,
            shift,
            w_expand,
            dw_kernel,
            w_project,
            gain_block,
            w_qkv_block,
            w_out_block,
            rows_block,
            gain_grid,
        ],
        [
            hidden,
            hidden,
            hidden,
            hidden,
            tokens,
            tokens,
            tokens,
            tokens,
            shape((TOKENS, 3 * D), BF16),
            shape((32, 64, 256), F32),
            tokens,
        ],
        [
            pltpu.VMEM((BLOCKS, ROWS + 2, WIDE, 128), F32),
            pltpu.VMEM((ROWS, COLS, D), F32),
            pltpu.VMEM((ROWS, COLS, D), F32),
            pltpu.VMEM((2, 64, 256), F32),
        ],
        smem_first=True,
    )

    sendable = jnp.stack(
        [normed_grid.reshape(64, 16, D), grad_flat.reshape(64, 16, D)], axis=1
    ).reshape(64, 32, D)
    got = across(sendable).reshape(64, 2, 16, D).transpose(1, 2, 0, 3).reshape(2, TOKENS, D)
    grad_groups, grid_total = call(
        grid_kernel,
        [got[0], got[1], w_qkv_grid, w_out_grid, rows_grid],
        [tokens, shape((2048, 128), F32)],
        [
            pltpu.VMEM((2, 64, 256), F32),
            pltpu.VMEM((TOKENS, D), BF16),
            pltpu.VMEM((TOKENS, 3 * D), BF16),
        ],
    )
    returned = across(grad_groups.reshape(16, 64, D).transpose(1, 0, 2)).reshape(TOKENS, D)

    grad_one, inner, block_total = call(
        block_kernel,
        [
            returned,
            grad_flat,
            section_two,
            section_one,
            normed_block,
            joined,
            probs,
            mixture,
            second,
            slope_conv,
            gain_grid,
            gain_block,
            w_qkv_block,
            w_out_block,
            w_project,
        ],
        [tokens, hidden, shape((4096, 128), F32)],
        [
            pltpu.VMEM((ROWS, COLS, D), F32),
            pltpu.VMEM((ROWS, COLS, D), F32),
            pltpu.VMEM((TOKENS, D), BF16),
            pltpu.VMEM((TOKENS, 3 * D), BF16),
        ],
    )

    cells = inner.reshape(BLOCKS, ROWS, COLS, 128)
    top, bottom = beside_rows(cells[:, 0], cells[:, ROWS - 1])
    ends = [
        jnp.concatenate([top[:, c : c + 1], cells[:, :, c], bottom[:, c : c + 1]], axis=1)
        for c in (0, COLS - 1)
    ]
    ends = [jnp.pad(e, ((0, 0), (0, 6), (0, 0))) for e in ends]
    side = jnp.concatenate(beside_columns(ends[0], ends[1]), axis=1)
    grad_input, expand_total, tap_total = call(
        back_kernel,
        [
            x_flat,
            lifted,
            slope_pre,
            inner,
            grad_one,
            top,
            bottom,
            side,
            scale,
            shift,
            w_expand,
            dw_kernel,
        ],
        [tokens, shape((2048, 128), F32), shape((9, BLOCKS, 128), F32)],
        [
            pltpu.VMEM((BLOCKS, ROWS + 2, WIDE, 128), F32),
            pltpu.VMEM((BLOCKS, TOKENS, 128), BF16),
            pltpu.VMEM((TOKENS, D), BF16),
        ],
    )

    parts = shape((CHUNKS, CHUNK, 128), BF16)
    sent, kept = call(
        pack_kernel,
        [core_flag, block_total, grid_total, expand_total, tap_total],
        [parts, shape((CHUNKS, CHUNK, 128), F32)],
        [],
        smem_first=True,
    )
    (paired,) = call(pair_kernel, [kept, sibling(sent)], [parts], [])
    (summed,) = call(sum_kernel, [across(paired)], [parts], [])
    mine = across(summed)
    totals = call(
        unpack_kernel,
        [core_flag, mine, sibling(mine)],
        [
            shape((D, E), F32),
            shape((9, E), F32),
            shape((E, D), F32),
            shape((D, 3 * D), F32),
            shape((D, D), F32),
            shape((D, 3 * D), F32),
            shape((D, D), F32),
        ],
        [],
        smem_first=True,
    )
    return (grad_input.reshape(ROWS, COLS, D), *totals)


def solution(mesh):
    split = Mesh(mesh.devices.reshape(8, 8, 2), ("row", "hi", "core"))
    tile = P("row", ("hi", "core"), None)
    return jax.shard_map(
        shards,
        mesh=split,
        in_specs=(tile, tile) + (P(),) * 13,
        out_specs=(tile,) + (P(),) * 7,
        check_vma=False,
    )
```

```python
import functools

import jax
import jax.numpy as jnp
from jax import lax
from jax.experimental import pallas as pl
from jax.experimental.pallas import tpu as pltpu
from jax.sharding import Mesh
from jax.sharding import PartitionSpec as P

F32 = jnp.float32
BF16 = jnp.bfloat16
EPSILON = 1e-05
HEADS = 8
HEAD = 32
SCALE = HEAD ** (-0.5)
ROWS = 8
COLS = 128
TOKENS = ROWS * COLS
D = 256
E = 1024
BLOCKS = E // 128
LEFT = 8
WIDE = COLS + 2 * LEFT
GELU_1 = 0.7978845608028654
GELU_3 = 0.044715 * GELU_1


def dot(left, right, left_dim, right_dim):
    return lax.dot_general(
        left, right, (((left_dim,), (right_dim,)), ((), ())), preferred_element_type=F32
    )


def gelu_pair(values):
    square = values * values
    half = 0.5 + 0.5 * jnp.tanh(values * (GELU_1 + GELU_3 * square))
    value = values * half
    slope = half + value * (1.0 - half) * (2.0 * GELU_1 + (6.0 * GELU_3) * square)
    return value, slope


def norm_parts(values):
    centered = values - jnp.mean(values, axis=-1, keepdims=True)
    spread = jnp.mean(centered * centered, axis=-1, keepdims=True)
    inverse = lax.rsqrt(spread + EPSILON)
    return centered * inverse, inverse


def norm_back(values, gain, grad):
    unit, inverse = norm_parts(values)
    scaled = grad * gain
    mean_grad = jnp.mean(scaled, axis=-1, keepdims=True)
    mean_unit = jnp.mean(scaled * unit, axis=-1, keepdims=True)
    return inverse * (scaled - mean_grad - unit * mean_unit)


def four_windows(cells):
    return jnp.concatenate(
        [cells[:, 8 * m : 8 * m + 8, :].reshape(64, D) for m in range(4)], axis=0
    )


def from_four_windows(tokens):
    return jnp.concatenate(
        [tokens[64 * m : 64 * m + 64].reshape(8, 8, D) for m in range(4)], axis=1
    )


def load_kernel(*refs):
    count = (len(refs) - 4) // 2
    sources, targets = refs[:count], refs[count : 2 * count]
    left_ref, right_ref, sems, ends = refs[2 * count :]
    copies = [
        pltpu.make_async_copy(source, target, sems.at[k])
        for k, (source, target) in enumerate(zip(sources, targets))
    ]
    for copy in copies:
        copy.start()
    copies[0].wait()
    x_ref = targets[0]
    for row in range(ROWS):
        ends[0, row : row + 1, :] = x_ref[row, 0:16, :].astype(F32)[0:1]
        ends[1, row : row + 1, :] = x_ref[row, COLS - 16 : COLS, :].astype(F32)[15:16]
    left_ref[...] = ends[0].astype(BF16)
    right_ref[...] = ends[1].astype(BF16)
    for copy in copies[1:]:
        copy.wait()


def with_corners(cells, left, right):
    rest = jnp.zeros((14, cells.shape[1]), F32)
    corners = jnp.concatenate([left, right, rest], axis=0).astype(BF16)
    return jnp.concatenate([cells, corners], axis=0)


def x_edge_kernel(x_ref, left_ref, right_ref, first_ref, last_ref):
    left = left_ref[...].astype(F32)
    right = right_ref[...].astype(F32)
    for row, target in ((0, first_ref), (ROWS - 1, last_ref)):
        target[...] = with_corners(x_ref[row], left[row : row + 1], right[row : row + 1])


def inner_edge_kernel(outer_ref, middle_ref, left_ref, right_ref, first_ref, last_ref):
    for block in range(BLOCKS):
        left = left_ref[block].astype(F32)
        right = right_ref[block].astype(F32)
        for row, target in ((0, first_ref), (ROWS - 1, last_ref)):
            cells = whole_row(outer_ref[block, row], middle_ref[block, row])
            target[block] = with_corners(cells, left[row : row + 1], right[row : row + 1])


def whole_row(outer, middle):
    axis = outer.ndim - 2
    first = lax.slice_in_dim(outer, 0, 32, axis=axis)
    last = lax.slice_in_dim(outer, 32, 64, axis=axis)
    return jnp.concatenate([first, middle, last], axis=axis)


def bias_kernel(block_ref, grid_ref, bias_block_ref, bias_grid_ref, table):
    source = lax.broadcasted_iota(jnp.int32, (256, 1024), 0)
    place = lax.broadcasted_iota(jnp.int32, (256, 1024), 1)
    wanted = 15 * (place % 128 // 8) + 7 + place % 8 - place // 128
    onehot = jnp.where(source == wanted, 1.0, 0.0).astype(BF16)
    table[...] = jnp.zeros((2 * HEADS, 256), F32)
    table[0:HEADS, 0:225] = block_ref[...]
    table[HEADS : 2 * HEADS, 0:225] = grid_ref[...]
    rest = table[...]
    spread = jnp.zeros((2 * HEADS, 1024), F32)
    for _ in range(3):
        part = rest.astype(BF16)
        spread = spread + dot(part, onehot, 1, 0)
        rest = rest - part.astype(F32)
    for which, bias_ref in enumerate((bias_block_ref, bias_grid_ref)):
        for head in range(HEADS):
            line = HEADS * which + head
            rows = jnp.concatenate(
                [spread[line : line + 1, 128 * e : 128 * e + 128] for e in range(8)], axis=0
            )
            for a_k in range(8):
                start = 8 * (7 - a_k)
                bias_ref[
                    head // 4, 8 * a_k : 8 * a_k + 8, 64 * (head % 4) : 64 * (head % 4) + 64
                ] = rows[:, start : start + 64]


def stacked(part, heads_mask):
    return jnp.concatenate([part] * 4, axis=0) * heads_mask


def pick(product):
    lane = lax.broadcasted_iota(jnp.int32, (64, 128), 1)
    low = jnp.where(lane < 32, product[0:64], product[64:128])
    high = jnp.where(lane < 96, product[128:192], product[192:256])
    return jnp.where(lane < 64, low, high)


def softmax_keys(scores):
    shifted = jnp.exp(scores - jnp.max(scores, axis=0, keepdims=True))
    return shifted * (1.0 / jnp.sum(shifted, axis=0, keepdims=True))


def half_of(joined, part, half, group):
    start = part * D + half * 128
    return joined[64 * group : 64 * group + 64, start : start + 128]


PAIRS = [(group, half) for group in range(4) for half in range(2)]


def quarter(parts):
    return jnp.concatenate(
        [jnp.concatenate(parts[2 * g : 2 * g + 2], axis=1) for g in range(4)], axis=0
    )


def attend(joined, bias_ref, heads_mask):
    scores = [
        dot(half_of(joined, 1, h, g), stacked(half_of(joined, 0, h, g), heads_mask), 1, 1)
        for g, h in PAIRS
    ]
    probs = [softmax_keys(s * SCALE + bias_ref[h]) for s, (_, h) in zip(scores, PAIRS)]
    products = [dot(p.astype(BF16), half_of(joined, 2, h, g), 0, 0) for p, (g, h) in zip(probs, PAIRS)]
    return probs, quarter([pick(p).astype(BF16) for p in products])


def attend_back(joined, probs, grad_mix, heads_mask):
    stacks = [stacked(half_of(grad_mix, 0, h, g), heads_mask) for g, h in PAIRS]
    grad_weights = [
        dot(half_of(joined, 2, h, g), stack, 1, 1).astype(BF16).astype(F32)
        for stack, (g, h) in zip(stacks, PAIRS)
    ]
    grad_values = [dot(p.astype(BF16), stack, 1, 0) for p, stack in zip(probs, stacks)]
    grad_scores = []
    for p, w in zip(probs, grad_weights):
        centre = jnp.sum(w * p, axis=0, keepdims=True)
        grad_scores.append((p * (w - centre) * SCALE).astype(BF16))
    grad_keys = [
        dot(s, stacked(half_of(joined, 0, h, g), heads_mask), 1, 0)
        for s, (g, h) in zip(grad_scores, PAIRS)
    ]
    grad_queries = [
        pick(dot(s, half_of(joined, 1, h, g), 0, 0)) for s, (g, h) in zip(grad_scores, PAIRS)
    ]
    return jnp.concatenate(
        [quarter(grad_queries), quarter(grad_keys), quarter(grad_values)], axis=1
    ).astype(BF16)


def heads_mask_of():
    row = lax.broadcasted_iota(jnp.int32, (256, 128), 0) // 64
    lane = lax.broadcasted_iota(jnp.int32, (256, 128), 1) // HEAD
    return jnp.where(row == lane, 1.0, 0.0).astype(BF16)


def attention_totals(total_ref, normed_ref, grad_joined_ref, mixture_ref, grad_ref):
    for part in range(3):
        total = dot(normed_ref[...], grad_joined_ref[:, D * part : D * part + D], 0, 0)
        for k in range(2):
            start = 256 * (2 * part + k)
            total_ref[start : start + 256, :] = total[:, 128 * k : 128 * k + 128]
    total = dot(mixture_ref[...], grad_ref[...], 0, 0)
    for k in range(2):
        total_ref[1536 + 256 * k : 1792 + 256 * k, :] = total[:, 128 * k : 128 * k + 128]


def front_kernel(
    x_ref,
    top_ref,
    bottom_ref,
    left_ref,
    right_ref,
    scale_ref,
    shift_ref,
    w_expand_ref,
    dw_ref,
    w_project_ref,
    gain_block_ref,
    w_qkv_ref,
    w_out_ref,
    bias,
    gain_grid_ref,
    grad_output_ref,
    lifted_out,
    slope_pre_out,
    second_out,
    slope_conv_ref,
    section_one_ref,
    section_two_ref,
    send_ref,
    normed_block_out,
    joined_ref,
    probs_ref,
    mixture_out,
    pad,
    cells,
    outcome,
    lifted_ref,
    slope_pre_ref,
    second_ref,
    normed_block_ref,
    mixture_ref,
    sems,
):
    stores = [
        pltpu.make_async_copy(source, target, sems.at[k])
        for k, (source, target) in enumerate(
            (
                (lifted_ref, lifted_out),
                (slope_pre_ref, slope_pre_out),
                (second_ref, second_out),
                (normed_block_ref, normed_block_out),
                (mixture_ref, mixture_out),
            )
        )
    ]
    send_ref[:, 16:32, :] = grad_output_ref[...].reshape(64, 16, D)
    heads_mask = heads_mask_of()
    row_index = lax.axis_index("row")
    col_index = 2 * lax.axis_index("hi") + lax.axis_index("core")
    inside = [
        jnp.where(flag, 1.0, 0.0).astype(F32)
        for flag in (row_index > 0, row_index < 7, col_index > 0, col_index < 15)
    ]

    def shifted_of(tokens):
        return (tokens.astype(F32) * scale_ref[...] + shift_ref[...]).astype(BF16)

    for source, row, flag in ((top_ref, 0, inside[0]), (bottom_ref, 9, inside[1])):
        shifted = shifted_of(source[...])
        for pair in range(4):
            value, _ = gelu_pair(dot(shifted, w_expand_ref[:, 256 * pair : 256 * pair + 256], 1, 0))
            value = value.astype(BF16).astype(F32) * flag
            for k in range(2):
                block = 2 * pair + k
                part = value[:, 128 * k : 128 * k + 128]
                pad[block, row, LEFT : LEFT + COLS, :] = part[:COLS]
                pad[block, row, LEFT - 1 : LEFT, :] = part[COLS : COLS + 1] * inside[2]
                pad[block, row, LEFT + COLS : LEFT + COLS + 1, :] = (
                    part[COLS + 1 : COLS + 2] * inside[3]
                )
    shifted = shifted_of(jnp.concatenate([left_ref[...], right_ref[...]], axis=0))
    place = lax.broadcasted_iota(jnp.int32, (16, 1), 0)
    flags = jnp.where(place < 8, inside[2], inside[3])
    for pair in range(4):
        value, _ = gelu_pair(dot(shifted, w_expand_ref[:, 256 * pair : 256 * pair + 256], 1, 0))
        value = value.astype(BF16).astype(F32) * flags
        for k in range(2):
            block = 2 * pair + k
            part = value[:, 128 * k : 128 * k + 128]
            for row in range(ROWS):
                pad[block, row + 1, LEFT - 1 : LEFT, :] = part[row : row + 1]
                pad[block, row + 1, LEFT + COLS : LEFT + COLS + 1, :] = part[8 + row : 9 + row]

    @pl.loop(0, ROWS)
    def _(row):
        here = pl.ds(pl.multiple_of(row * COLS, COLS), COLS)
        shifted = shifted_of(x_ref[row])
        for pair in range(4):
            value, slope = gelu_pair(
                dot(shifted, w_expand_ref[:, 256 * pair : 256 * pair + 256], 1, 0)
            )
            value = value.astype(BF16)
            slope = slope.astype(BF16)
            for k in range(2):
                lanes = slice(128 * k, 128 * k + 128)
                lifted_ref[2 * pair + k, here, :] = value[:, lanes]
                slope_pre_ref[2 * pair + k, here, :] = slope[:, lanes]
                pad[2 * pair + k, row + 1, LEFT : LEFT + COLS, :] = value[:, lanes].astype(F32)

    stores[0].start()
    stores[1].start()

    @pl.loop(0, BLOCKS)
    def _(block):
        taps = [
            dw_ref[t : t + 1, pl.ds(pl.multiple_of(block * 128, 128), 128)] for t in range(9)
        ]

        @pl.loop(0, ROWS)
        def _(row):
            for chunk in range(4):
                summed = None
                for t in range(9):
                    start = LEFT - 1 + t % 3 + 32 * chunk
                    term = taps[t] * pad[block, row + t // 3, start : start + 32, :]
                    summed = term if summed is None else summed + term
                value, slope = gelu_pair(summed)
                here = pl.ds(pl.multiple_of(row * COLS + 32 * chunk, 32), 32)
                second_ref[block, here, :] = value.astype(BF16)
                slope_conv_ref[block, here, :] = slope.astype(BF16)

    stores[2].start()

    @pl.loop(0, 4)
    def _(part):
        here = pl.ds(pl.multiple_of(part * 256, 256), 256)
        summed = x_ref[pl.ds(2 * part, 2)].reshape(256, D).astype(F32)
        for pair in range(4):
            joined = jnp.concatenate(
                [second_ref[2 * pair, here, :], second_ref[2 * pair + 1, here, :]], axis=1
            )
            summed = summed + dot(joined, w_project_ref[256 * pair : 256 * pair + 256, :], 1, 0)
        section_one = summed.astype(BF16)
        section_one_ref[pl.ds(2 * part, 2)] = section_one.reshape(2, COLS, D)
        cells[pl.ds(2 * part, 2)] = section_one.astype(F32).reshape(2, COLS, D)

    @pl.loop(0, 4)
    def _(part):
        here = pl.ds(pl.multiple_of(part * 256, 256), 256)
        columns = pl.ds(pl.multiple_of(part * 32, 32), 32)
        section_one = four_windows(cells[:, columns, :])
        normed = (norm_parts(section_one)[0] * gain_block_ref[...]).astype(BF16)
        normed_block_ref[here, :] = normed
        joined = dot(normed, w_qkv_ref[...], 1, 0).astype(BF16)
        joined_ref[here, :] = joined
        probs, mixture = attend(joined, bias, heads_mask)
        for index in range(8):
            probs_ref[part * 8 + index] = probs[index]
        mixture_ref[here, :] = mixture
        section_two = (section_one + dot(mixture, w_out_ref[...], 1, 0)).astype(BF16).astype(F32)
        cells[:, columns, :] = from_four_windows(section_two)
        normed = norm_parts(section_two)[0] * gain_grid_ref[...]
        outcome[:, columns, :] = from_four_windows(normed)

    stores[3].start()
    stores[4].start()
    send_ref[:, 0:16, :] = outcome[...].astype(BF16).reshape(64, 16, D)
    section_two_ref[...] = cells[...].astype(BF16)
    for copy in stores:
        copy.wait()


def grid_kernel(
    got_ref,
    w_qkv_ref,
    w_out_ref,
    bias,
    grad_normed_ref,
    total_ref,
    mixture_ref,
    grad_joined_ref,
):
    heads_mask = heads_mask_of()
    normed_ref = got_ref.at[0]
    grad_ref = got_ref.at[1]

    @pl.loop(0, 4)
    def _(part):
        here = pl.ds(pl.multiple_of(part * 256, 256), 256)
        joined = dot(normed_ref[here, :], w_qkv_ref[...], 1, 0).astype(BF16)
        grad_mix = dot(grad_ref[here, :], w_out_ref[...], 1, 1).astype(BF16)
        probs, mixture = attend(joined, bias, heads_mask)
        mixture_ref[here, :] = mixture
        grad_joined = attend_back(joined, probs, grad_mix, heads_mask)
        grad_joined_ref[here, :] = grad_joined
        grad_normed_ref[here, :] = dot(grad_joined, w_qkv_ref[...], 1, 1).astype(BF16)

    attention_totals(total_ref, normed_ref, grad_joined_ref, mixture_ref, grad_ref)


def block_kernel(
    parts,
    returned_ref,
    grad_output_ref,
    section_two_ref,
    section_one_ref,
    joined_ref,
    probs_ref,
    slope_conv_ref,
    gain_grid_ref,
    gain_block_ref,
    w_qkv_ref,
    w_out_ref,
    w_project_ref,
    normed_block_in,
    mixture_in,
    *rest,
):
    normed_block_ref, mixture_ref, sems = rest[-3:]
    if len(rest) == 9:
        before_ref = None
        grad_one_ref, inner_ref, total_ref, left_ref, right_ref, ends = rest[:-3]
    else:
        before_ref, grad_one_ref, inner_ref, total_ref = rest[:-3]
    fetches = []
    for index, part in enumerate(parts):
        for k, (source, target) in enumerate(
            ((normed_block_in, normed_block_ref), (mixture_in, mixture_ref))
        ):
            fetches.append(
                pltpu.make_async_copy(
                    source.at[pl.ds(256 * part, 256), :],
                    target.at[pl.ds(256 * index, 256), :],
                    sems.at[2 * index + k],
                )
            )
            fetches[-1].start()
    heads_mask = heads_mask_of()
    all_windows = []
    all_joined = []
    for index, part in enumerate(parts):
        here = slice(256 * part, 256 * part + 256)
        columns = slice(32 * part, 32 * part + 32)
        out_columns = slice(32 * index, 32 * index + 32)

        def windows_of(ref):
            return four_windows(ref[:, columns, :].astype(F32))

        grad_two = windows_of(grad_output_ref) + norm_back(
            windows_of(section_two_ref), gain_grid_ref[...], windows_of(returned_ref)
        )
        grad_windows = grad_two.astype(BF16)
        grad_two = grad_windows.astype(F32)
        joined = joined_ref[here, :]
        grad_mix = dot(grad_windows, w_out_ref[...], 1, 1).astype(BF16)
        probs = [probs_ref[part * 8 + k] for k in range(8)]
        grad_joined = attend_back(joined, probs, grad_mix, heads_mask)
        all_windows.append(grad_windows)
        all_joined.append(grad_joined)
        grad_normed = dot(grad_joined, w_qkv_ref[...], 1, 1).astype(BF16).astype(F32)
        grad_one = grad_two + norm_back(
            windows_of(section_one_ref), gain_block_ref[...], grad_normed
        )
        grad_one = from_four_windows(grad_one).astype(BF16)
        grad_one_ref[:, out_columns, :] = grad_one
        grad_one = grad_one.reshape(256, D)
        for pair in range(4):
            through = dot(grad_one, w_project_ref[256 * pair : 256 * pair + 256, :], 1, 1)
            for k in range(2):
                block = 2 * pair + k
                slope = slope_conv_ref[block, :, columns, :].astype(F32)
                inner = through[:, 128 * k : 128 * k + 128].reshape(ROWS, 32, 128) * slope
                inner_ref[block, :, out_columns, :] = inner.astype(BF16)
                if before_ref is None:
                    side, column = (0, 0) if part == 0 else (1, 31)
                    for row in range(ROWS):
                        ends[side, block, row : row + 1, :] = inner[row, column : column + 1]
    if before_ref is None:
        left_ref[...] = ends[0].astype(BF16)
        right_ref[...] = ends[1].astype(BF16)
    for copy in fetches:
        copy.wait()
    joined = jnp.concatenate(all_joined, axis=0)
    windows = jnp.concatenate(all_windows, axis=0)
    products = [
        (normed_block_ref, joined[:, D * part : D * part + D], 512 * part) for part in range(3)
    ]
    for left, right, start in products + [(mixture_ref, windows, 1536)]:
        total = dot(left[...], right, 0, 0)
        for k in range(2):
            place = slice(start + 256 * k, start + 256 * k + 256)
            value = total[:, 128 * k : 128 * k + 128]
            total_ref[place, :] = value if before_ref is None else before_ref[place, :] + value


def total_kernel(
    core_ref,
    outer_ref,
    middle_ref,
    second_in,
    block_total_ref,
    grid_total_ref,
    grad_one_ref,
    early_send_ref,
    early_keep_ref,
    total_ref,
    second_ref,
    sem,
):
    fetch = pltpu.make_async_copy(second_in, second_ref, sem)
    fetch.start()
    grad_one = whole_row(outer_ref[...], middle_ref[...])
    grad_one_ref[...] = grad_one
    grad_one = grad_one.reshape(TOKENS, D)
    total_ref[0:2048, :] = block_total_ref[...]
    total_ref[4096:6144, :] = grid_total_ref[...]
    fetch.wait()
    for pair in range(4):
        joined = jnp.concatenate([second_ref[2 * pair], second_ref[2 * pair + 1]], axis=1)
        total = dot(joined, grad_one, 0, 0)
        for k in range(2):
            start = 2048 + 1024 * k + 256 * pair
            total_ref[start : start + 256, :] = total[:, 128 * k : 128 * k + 128]
    own = pl.ds(pl.multiple_of(core_ref[0] * 3072, 3072), 3072)
    other = pl.ds(pl.multiple_of((1 - core_ref[0]) * 3072, 3072), 3072)
    early_keep_ref[...] = total_ref[own, :].astype(BF16)
    early_send_ref[...] = total_ref[other, :].astype(BF16)


def back_kernel(
    core_ref,
    x_ref,
    lifted_in,
    slope_pre_in,
    outer_ref,
    middle_ref,
    top_ref,
    bottom_ref,
    left_ref,
    right_ref,
    scale_ref,
    shift_ref,
    dw_ref,
    _,
    preact_ref,
    late_send_ref,
    late_keep_ref,
    pad,
    shifted_ref,
    total_ref,
    taps_ref,
    lifted_ref,
    slope_pre_ref,
    sems,
):
    def fetches(block):
        return [
            pltpu.make_async_copy(source.at[block], target.at[block], sems.at[block, k])
            for k, (source, target) in enumerate(
                ((lifted_in, lifted_ref), (slope_pre_in, slope_pre_ref))
            )
        ]

    for block in range(BLOCKS):
        for copy in fetches(block):
            copy.start()
    for block in range(BLOCKS):
        for source, row in ((top_ref, 0), (bottom_ref, 9)):
            cells = source[block].astype(F32)
            pad[block, row, LEFT : LEFT + COLS, :] = cells[:COLS]
            pad[block, row, LEFT - 1 : LEFT, :] = cells[COLS : COLS + 1]
            pad[block, row, LEFT + COLS : LEFT + COLS + 1, :] = cells[COLS + 1 : COLS + 2]
        left = left_ref[block].astype(F32)
        right = right_ref[block].astype(F32)
        for row in range(ROWS):
            pad[block, row + 1, LEFT - 1 : LEFT, :] = left[row : row + 1]
            pad[block, row + 1, LEFT + COLS : LEFT + COLS + 1, :] = right[row : row + 1]

    @pl.loop(0, BLOCKS)
    def _(block):
        for copy in fetches(block):
            copy.wait()
        taps = [
            dw_ref[t : t + 1, pl.ds(pl.multiple_of(block * 128, 128), 128)] for t in range(9)
        ]

        @pl.loop(0, ROWS)
        def _(row):
            cells = whole_row(outer_ref[block, row], middle_ref[block, row])
            pad[block, row + 1, LEFT : LEFT + COLS, :] = cells.astype(F32)

        def step(row, totals):
            totals = list(totals)
            for chunk in range(4):
                here = pl.ds(pl.multiple_of(row * COLS + 32 * chunk, 32), 32)
                lifted = lifted_ref[block, here, :].astype(F32)
                summed = None
                for t in range(9):
                    start = LEFT + 1 - t % 3 + 32 * chunk
                    cells = pad[block, row + 2 - t // 3, start : start + 32, :]
                    term = taps[t] * cells
                    summed = term if summed is None else summed + term
                    totals[t] = totals[t] + jnp.sum((lifted * cells).reshape(4, 8, 128), axis=0)
                grad = summed * slope_pre_ref[block, here, :].astype(F32)
                preact_ref[block, here, :] = grad.astype(BF16)
            return tuple(totals)

        totals = lax.fori_loop(0, ROWS, step, (jnp.zeros((8, 128), F32),) * 9)
        for t in range(9):
            taps_ref[t, pl.ds(block, 1), :] = jnp.sum(totals[t], axis=0, keepdims=True)

    shifted_ref[...] = (
        x_ref[...].reshape(TOKENS, D).astype(F32) * scale_ref[...] + shift_ref[...]
    ).astype(BF16)
    for pair in range(4):
        joined = jnp.concatenate([preact_ref[2 * pair], preact_ref[2 * pair + 1]], axis=1)
        total = dot(shifted_ref[...], joined, 0, 0)
        for k in range(2):
            start = 256 * (2 * pair + k)
            total_ref[start : start + 256, :] = total[:, 128 * k : 128 * k + 128]
    own = pl.ds(pl.multiple_of(core_ref[0] * 1024, 1024), 1024)
    other = pl.ds(pl.multiple_of((1 - core_ref[0]) * 1024, 1024), 1024)
    for target, rows in ((late_keep_ref, own), (late_send_ref, other)):
        large = total_ref[rows, :].reshape(CHUNKS, 16, 128)
        for index in range(CHUNKS):
            taps = taps_ref[index] if index < 9 else jnp.zeros((8, 128), F32)
            target[index] = jnp.concatenate([large[index], taps], axis=0).astype(BF16)


def input_kernel(preact_ref, grad_one_ref, w_expand_ref, scale_ref, grad_input_ref):
    for part in range(4):
        here = slice(256 * part, 256 * part + 256)
        summed = jnp.zeros((256, D), F32)
        for pair in range(4):
            joined = jnp.concatenate(
                [preact_ref[2 * pair, here, :], preact_ref[2 * pair + 1, here, :]], axis=1
            )
            summed = summed + dot(joined, w_expand_ref[:, 256 * pair : 256 * pair + 256], 1, 1)
        grad_one = grad_one_ref[2 * part : 2 * part + 2].reshape(256, D).astype(F32)
        grad_input_ref[here, :] = (grad_one + summed * scale_ref[...]).astype(BF16)


VMEM = pl.BlockSpec(memory_space=pltpu.VMEM)
SMEM = pl.BlockSpec(memory_space=pltpu.SMEM)
HBM = pl.BlockSpec(memory_space=pltpu.HBM)


def shape(dims, kind):
    return jax.ShapeDtypeStruct(dims, kind)


def call(kernel, ins, outs, scratch, smem=(), far=(), far_out=(), keep=(), limit=16, flops=10**9):
    ins = [pltpu.with_memory_space_constraint(x, pltpu.HBM) if k in far else x for k, x in enumerate(ins)]
    specs = [SMEM if k in smem else HBM if k in far else VMEM for k in range(len(ins))]
    return pl.pallas_call(
        kernel,
        out_shape=[
            pltpu.VMEM(o.shape, o.dtype)
            if k in keep
            else pltpu.HBM(o.shape, o.dtype)
            if k in far_out
            else o
            for k, o in enumerate(outs)
        ],
        in_specs=specs,
        out_specs=[HBM if k in far_out else VMEM for k in range(len(outs))],
        scratch_shapes=scratch,
        compiler_params=pltpu.CompilerParams(vmem_limit_bytes=limit * 1024 * 1024),
        cost_estimate=pl.CostEstimate(flops=flops, bytes_accessed=flops // 100, transcendentals=0),
    )(*ins)


CHUNKS = 64
CHUNK = 72
FACTOR = float((64 * 2048) ** (-0.5))


def pair_kernel(early_keep_ref, early_got_ref, late_keep_ref, late_got_ref, parts_ref):
    early = early_keep_ref[...].astype(F32) + early_got_ref[...].astype(F32)
    early = early.reshape(CHUNKS, 48, 128)
    late = late_keep_ref[...].astype(F32) + late_got_ref[...].astype(F32)
    parts_ref[...] = jnp.concatenate([early, late], axis=1).astype(BF16)


def sum_kernel(got_ref, out_ref):
    def step(index, total):
        return total + got_ref[index].astype(F32)

    total = lax.fori_loop(0, CHUNKS, step, jnp.zeros((CHUNK, 128), F32), unroll=8)
    total = total.astype(BF16)
    for index in range(CHUNKS):
        out_ref[index] = total


def unpack_kernel(
    core_ref,
    mine_ref,
    other_ref,
    expand_ref,
    kernel_ref,
    project_ref,
    qkv_block_ref,
    out_block_ref,
    qkv_grid_ref,
    out_grid_ref,
):
    core = core_ref[0]

    targets = (
        [(qkv_block_ref, 0, 128 * k, 256) for k in range(6)]
        + [(out_block_ref, 0, 128 * k, 256) for k in range(2)]
        + [(project_ref, 0, 128 * k, 1024) for k in range(2)]
        + [(qkv_grid_ref, 0, 128 * k, 256) for k in range(6)]
        + [(out_grid_ref, 0, 128 * k, 256) for k in range(2)]
    )
    early = [
        (target, first + start, column)
        for target, first, column, count in targets
        for start in range(0, count, 16)
    ]

    def fill(low_ref, high_ref):
        for half, ref in enumerate((low_ref, high_ref)):
            for index in range(CHUNKS):
                value = ref[index].astype(F32) * FACTOR
                for k in range(3):
                    target, row, column = early[192 * half + 3 * index + k]
                    target[row : row + 16, column : column + 128] = value[16 * k : 16 * k + 16]
                start = 1024 * half + 16 * index
                column = start // 256 * 128
                expand_ref[start % 256 : start % 256 + 16, column : column + 128] = value[48:64]
                if half == 0 and index < 9:
                    for block in range(BLOCKS):
                        kernel_ref[index : index + 1, 128 * block : 128 * block + 128] = value[
                            64 + block : 65 + block
                        ]

    @pl.when(core == 0)
    def _():
        fill(mine_ref, other_ref)

    @pl.when(core == 1)
    def _():
        fill(other_ref, mine_ref)


def beside_rows(first, last):
    count = lax.axis_size("row")
    down = [(i, i + 1) for i in range(count - 1)]
    up = [(i + 1, i) for i in range(count - 1)]
    return lax.ppermute(last, "row", down), lax.ppermute(first, "row", up)


def beside_columns(first, last):
    axes = ("hi", "core")
    count = lax.axis_size("hi") * lax.axis_size("core")
    right = [(i, i + 1) for i in range(count - 1)]
    left = [(i + 1, i) for i in range(count - 1)]
    return lax.ppermute(last, axes, right), lax.ppermute(first, axes, left)


def across(values):
    return lax.all_to_all(values, ("row", "hi"), split_axis=0, concat_axis=0, tiled=True)


def sibling(values):
    return lax.ppermute(values, "core", [(0, 1), (1, 0)])


def shards(
    x_input,
    grad_output,
    in_scale,
    in_shift,
    w_expand,
    dw_kernel,
    w_project,
    gain_block,
    w_qkv_block,
    w_out_block,
    bias_block,
    gain_grid,
    w_qkv_grid,
    w_out_grid,
    bias_grid,
):
    core_flag = lax.axis_index("core").reshape(1).astype(jnp.int32)
    scale = in_scale.reshape(1, D)
    shift = in_shift.reshape(1, D)
    gain_block = gain_block.reshape(1, D)
    gain_grid = gain_grid.reshape(1, D)
    hidden = shape((BLOCKS, TOKENS, 128), BF16)
    hidden_vmem = pltpu.VMEM((BLOCKS, TOKENS, 128), BF16)
    tile = shape((ROWS, COLS, D), BF16)
    tokens = shape((TOKENS, D), BF16)
    tokens_vmem = pltpu.VMEM((TOKENS, D), BF16)
    edge_row = shape((144, D), BF16)
    edge_column = shape((ROWS, D), BF16)
    large = [
        x_input,
        w_expand,
        grad_output,
        w_project,
        w_qkv_block,
        w_out_block,
        w_qkv_grid,
        w_out_grid,
        dw_kernel,
    ]
    (
        x_input,
        w_expand,
        grad_output,
        w_project,
        w_qkv_block,
        w_out_block,
        w_qkv_grid,
        w_out_grid,
        dw_kernel,
        x_left,
        x_right,
    ) = call(
        load_kernel,
        large,
        [shape(v.shape, v.dtype) for v in large] + [edge_column, edge_column],
        [pltpu.SemaphoreType.DMA((len(large),)), pltpu.VMEM((2, ROWS, D), F32)],
        far=range(len(large)),
        keep=range(len(large) + 2),
        limit=4,
    )
    x_left, x_right = beside_columns(x_left, x_right)
    cube = shape((2, 64, 256), F32)
    cube_block, cube_grid = call(
        bias_kernel,
        [bias_block, bias_grid],
        [cube, cube],
        [pltpu.VMEM((2 * HEADS, 256), F32)],
        keep=(0, 1),
        limit=8,
    )
    x_first, x_last = call(
        x_edge_kernel,
        [x_input, x_left, x_right],
        [edge_row, edge_row],
        [],
        keep=(0, 1),
        limit=4,
    )
    x_top, x_bottom = beside_rows(x_first, x_last)
    (
        lifted,
        slope_pre,
        second,
        slope_conv,
        section_one,
        section_two,
        sendable,
        normed_block,
        joined,
        probs,
        mixture,
    ) = call(
        front_kernel,
        [
            x_input,
            x_top,
            x_bottom,
            x_left,
            x_right,
            scale,
            shift,
            w_expand,
            dw_kernel,
            w_project,
            gain_block,
            w_qkv_block,
            w_out_block,
            cube_block,
            gain_grid,
            grad_output,
        ],
        [
            hidden,
            hidden,
            hidden,
            hidden,
            tile,
            tile,
            shape((64, 32, D), BF16),
            tokens,
            shape((TOKENS, 3 * D), BF16),
            shape((32, 64, 256), F32),
            tokens,
        ],
        [
            pltpu.VMEM((BLOCKS, ROWS + 2, WIDE, 128), F32),
            pltpu.VMEM((ROWS, COLS, D), F32),
            pltpu.VMEM((ROWS, COLS, D), F32),
            hidden_vmem,
            hidden_vmem,
            hidden_vmem,
            tokens_vmem,
            tokens_vmem,
            pltpu.SemaphoreType.DMA((5,)),
        ],
        keep=(3, 4, 5, 6, 8, 9),
        far_out=(0, 1, 2, 7, 10),
        limit=24,
    )

    got = across(sendable).transpose(1, 0, 2).reshape(2, TOKENS, D)
    grad_groups, grid_total = call(
        grid_kernel,
        [got, w_qkv_grid, w_out_grid, cube_grid],
        [tokens, shape((2048, 128), F32)],
        [tokens_vmem, pltpu.VMEM((TOKENS, 3 * D), BF16)],
        keep=(0, 1),
        limit=8,
    )
    returned = across(grad_groups.reshape(16, 64, D).transpose(1, 0, 2)).reshape(ROWS, COLS, D)

    def block_half(parts, before):
        edge = [] if before else [shape((BLOCKS, ROWS, 128), BF16)] * 2
        half_vmem = pltpu.VMEM((TOKENS // 2, D), BF16)
        return call(
            functools.partial(block_kernel, parts),
            [
                returned,
                grad_output,
                section_two,
                section_one,
                joined,
                probs,
                slope_conv.reshape(BLOCKS, ROWS, COLS, 128),
                gain_grid,
                gain_block,
                w_qkv_block,
                w_out_block,
                w_project,
                normed_block,
                mixture,
            ]
            + before,
            [
                shape((ROWS, COLS // 2, D), BF16),
                shape((BLOCKS, ROWS, COLS // 2, 128), BF16),
                shape((2048, 128), F32),
            ]
            + edge,
            ([] if before else [pltpu.VMEM((2, BLOCKS, ROWS, 128), F32)])
            + [half_vmem, half_vmem, pltpu.SemaphoreType.DMA((4,))],
            far=(12, 13),
            keep=range(3 + len(edge)),
            limit=8,
            flops=4*10**9,
        )

    one_outer, inner_outer, block_total, left, right = block_half((0, 3), [])
    left, right = beside_columns(left, right)
    one_middle, inner_middle, block_total = block_half((1, 2), [block_total])
    edge_cells = shape((BLOCKS, 144, 128), BF16)
    first, last = call(
        inner_edge_kernel,
        [inner_outer, inner_middle, left, right],
        [edge_cells, edge_cells],
        [],
        keep=(0, 1),
        limit=4,
    )
    top, bottom = beside_rows(first, last)
    early = shape((3072, 128), BF16)
    grad_one, early_send, early_keep = call(
        total_kernel,
        [core_flag, one_outer, one_middle, second, block_total, grid_total],
        [tile, early, early],
        [pltpu.VMEM((6144, 128), F32), hidden_vmem, pltpu.SemaphoreType.DMA],
        smem=(0,),
        far=(3,),
        keep=range(3),
        limit=8,
        flops=3*10**9,
    )
    early_got = sibling(early_send)
    late = shape((CHUNKS, 24, 128), BF16)
    parts = shape((CHUNKS, CHUNK, 128), BF16)
    preact, late_send, late_keep = call(
        back_kernel,
        [
            core_flag,
            x_input,
            lifted,
            slope_pre,
            inner_outer,
            inner_middle,
            top,
            bottom,
            left,
            right,
            scale,
            shift,
            dw_kernel,
            early_keep,
        ],
        [hidden, late, late],
        [
            pltpu.VMEM((BLOCKS, ROWS + 2, WIDE, 128), F32),
            tokens_vmem,
            pltpu.VMEM((2048, 128), F32),
            pltpu.VMEM((9, BLOCKS, 128), F32),
            hidden_vmem,
            hidden_vmem,
            pltpu.SemaphoreType.DMA((BLOCKS, 2)),
        ],
        smem=(0,),
        far=(2, 3),
        keep=(0, 1, 2),
        limit=20,
        flops=10**10,
    )
    (grad_input,) = call(
        input_kernel, [preact, grad_one, w_expand, scale], [tokens], [], limit=8
    )

    (paired,) = call(
        pair_kernel,
        [early_keep, early_got, late_keep, sibling(late_send)],
        [parts],
        [],
        keep=(0,),
        limit=4,
    )
    (summed,) = call(sum_kernel, [across(paired)], [parts], [], keep=(0,), limit=4)
    mine = across(summed)
    totals = call(
        unpack_kernel,
        [core_flag, mine, sibling(mine)],
        [
            shape((D, E), F32),
            shape((9, E), F32),
            shape((E, D), F32),
            shape((D, 3 * D), F32),
            shape((D, D), F32),
            shape((D, 3 * D), F32),
            shape((D, D), F32),
        ],
        [],
        smem=(0,),
        limit=16,
    )
    return (grad_input.reshape(ROWS, COLS, D), *totals)


def solution(mesh):
    split = Mesh(mesh.devices.reshape(8, 8, 2), ("row", "hi", "core"))
    tile = P("row", ("hi", "core"), None)
    return jax.shard_map(
        shards,
        mesh=split,
        in_specs=(tile, tile) + (P(),) * 13,
        out_specs=(tile,) + (P(),) * 7,
        check_vma=False,
    )
```

```python
import functools

import jax
import jax.numpy as jnp
from jax import lax
from jax.experimental import pallas as pl
from jax.experimental.pallas import tpu as pltpu
from jax.sharding import Mesh
from jax.sharding import PartitionSpec as P

F32 = jnp.float32
BF16 = jnp.bfloat16
EPSILON = 1e-05
HEADS = 8
HEAD = 32
SCALE = HEAD ** (-0.5)
ROWS = 8
COLS = 128
TOKENS = ROWS * COLS
D = 256
E = 1024
BLOCKS = E // 128
LEFT = 8
WIDE = COLS + 2 * LEFT
GELU_1 = 0.7978845608028654
GELU_3 = 0.044715 * GELU_1


def dot(left, right, left_dim, right_dim):
    return lax.dot_general(
        left, right, (((left_dim,), (right_dim,)), ((), ())), preferred_element_type=F32
    )


def gelu_pair(values):
    square = values * values
    half = 0.5 + 0.5 * jnp.tanh(values * (GELU_1 + GELU_3 * square))
    value = values * half
    slope = half + value * (1.0 - half) * (2.0 * GELU_1 + (6.0 * GELU_3) * square)
    return value, slope


def norm_parts(values):
    centered = values - jnp.mean(values, axis=-1, keepdims=True)
    spread = jnp.mean(centered * centered, axis=-1, keepdims=True)
    inverse = lax.rsqrt(spread + EPSILON)
    return centered * inverse, inverse


def norm_back(values, gain, grad):
    unit, inverse = norm_parts(values)
    scaled = grad * gain
    mean_grad = jnp.mean(scaled, axis=-1, keepdims=True)
    mean_unit = jnp.mean(scaled * unit, axis=-1, keepdims=True)
    return inverse * (scaled - mean_grad - unit * mean_unit)


def four_windows(cells):
    return jnp.concatenate(
        [cells[:, 8 * m : 8 * m + 8, :].reshape(64, D) for m in range(4)], axis=0
    )


def from_four_windows(tokens):
    return jnp.concatenate(
        [tokens[64 * m : 64 * m + 64].reshape(8, 8, D) for m in range(4)], axis=1
    )


def load_kernel(x_in, x_ref, left_ref, right_ref, sem, ends):
    copy = pltpu.make_async_copy(x_in, x_ref, sem)
    copy.start()
    copy.wait()
    for row in range(ROWS):
        ends[0, row : row + 1, :] = x_ref[row, 0:16, :].astype(F32)[0:1]
        ends[1, row : row + 1, :] = x_ref[row, COLS - 16 : COLS, :].astype(F32)[15:16]
    left_ref[...] = ends[0].astype(BF16)
    right_ref[...] = ends[1].astype(BF16)


def with_corners(cells, left, right):
    rest = jnp.zeros((14, cells.shape[1]), F32)
    corners = jnp.concatenate([left, right, rest], axis=0).astype(BF16)
    return jnp.concatenate([cells, corners], axis=0)


def x_edge_kernel(x_ref, left_ref, right_ref, first_ref, last_ref):
    left = left_ref[...].astype(F32)
    right = right_ref[...].astype(F32)
    for row, target in ((0, first_ref), (ROWS - 1, last_ref)):
        target[...] = with_corners(x_ref[row], left[row : row + 1], right[row : row + 1])


def inner_edge_kernel(outer_ref, middle_ref, left_ref, right_ref, first_ref, last_ref):
    for block in range(BLOCKS):
        left = left_ref[block].astype(F32)
        right = right_ref[block].astype(F32)
        for row, target in ((0, first_ref), (ROWS - 1, last_ref)):
            cells = whole_row(outer_ref[block, row], middle_ref[block, row])
            target[block] = with_corners(cells, left[row : row + 1], right[row : row + 1])


def whole_row(outer, middle):
    axis = outer.ndim - 2
    first = lax.slice_in_dim(outer, 0, 32, axis=axis)
    last = lax.slice_in_dim(outer, 32, 64, axis=axis)
    return jnp.concatenate([first, middle, last], axis=axis)


def bias_kernel(block_ref, grid_ref, bias_block_ref, bias_grid_ref, table):
    source = lax.broadcasted_iota(jnp.int32, (256, 1024), 0)
    place = lax.broadcasted_iota(jnp.int32, (256, 1024), 1)
    wanted = 15 * (place % 128 // 8) + 7 + place % 8 - place // 128
    onehot = jnp.where(source == wanted, 1.0, 0.0).astype(BF16)
    table[...] = jnp.zeros((2 * HEADS, 256), F32)
    table[0:HEADS, 0:225] = block_ref[...]
    table[HEADS : 2 * HEADS, 0:225] = grid_ref[...]
    rest = table[...]
    spread = jnp.zeros((2 * HEADS, 1024), F32)
    for _ in range(3):
        part = rest.astype(BF16)
        spread = spread + dot(part, onehot, 1, 0)
        rest = rest - part.astype(F32)
    for which, bias_ref in enumerate((bias_block_ref, bias_grid_ref)):
        for head in range(HEADS):
            line = HEADS * which + head
            rows = jnp.concatenate(
                [spread[line : line + 1, 128 * e : 128 * e + 128] for e in range(8)], axis=0
            )
            for a_k in range(8):
                start = 8 * (7 - a_k)
                bias_ref[
                    head // 4, 8 * a_k : 8 * a_k + 8, 64 * (head % 4) : 64 * (head % 4) + 64
                ] = rows[:, start : start + 64]


def stacked(part, heads_mask):
    return jnp.concatenate([part] * 4, axis=0) * heads_mask


def pick(product):
    lane = lax.broadcasted_iota(jnp.int32, (64, 128), 1)
    low = jnp.where(lane < 32, product[0:64], product[64:128])
    high = jnp.where(lane < 96, product[128:192], product[192:256])
    return jnp.where(lane < 64, low, high)


def softmax_keys(scores):
    shifted = jnp.exp(scores - jnp.max(scores, axis=0, keepdims=True))
    return shifted * (1.0 / jnp.sum(shifted, axis=0, keepdims=True))


def half_of(joined, part, half, group):
    start = part * D + half * 128
    return joined[64 * group : 64 * group + 64, start : start + 128]


PAIRS = [(group, half) for group in range(4) for half in range(2)]


def quarter(parts):
    return jnp.concatenate(
        [jnp.concatenate(parts[2 * g : 2 * g + 2], axis=1) for g in range(4)], axis=0
    )


def attend(joined, bias_ref, heads_mask):
    scores = [
        dot(half_of(joined, 1, h, g), stacked(half_of(joined, 0, h, g), heads_mask), 1, 1)
        for g, h in PAIRS
    ]
    probs = [softmax_keys(s * SCALE + bias_ref[h]) for s, (_, h) in zip(scores, PAIRS)]
    products = [dot(p.astype(BF16), half_of(joined, 2, h, g), 0, 0) for p, (g, h) in zip(probs, PAIRS)]
    return probs, quarter([pick(p).astype(BF16) for p in products])


def attend_back(joined, probs, grad_mix, heads_mask):
    stacks = [stacked(half_of(grad_mix, 0, h, g), heads_mask) for g, h in PAIRS]
    grad_weights = [
        dot(half_of(joined, 2, h, g), stack, 1, 1).astype(BF16).astype(F32)
        for stack, (g, h) in zip(stacks, PAIRS)
    ]
    grad_values = [dot(p.astype(BF16), stack, 1, 0) for p, stack in zip(probs, stacks)]
    grad_scores = []
    for p, w in zip(probs, grad_weights):
        centre = jnp.sum(w * p, axis=0, keepdims=True)
        grad_scores.append((p * (w - centre) * SCALE).astype(BF16))
    grad_keys = [
        dot(s, stacked(half_of(joined, 0, h, g), heads_mask), 1, 0)
        for s, (g, h) in zip(grad_scores, PAIRS)
    ]
    grad_queries = [
        pick(dot(s, half_of(joined, 1, h, g), 0, 0)) for s, (g, h) in zip(grad_scores, PAIRS)
    ]
    return jnp.concatenate(
        [quarter(grad_queries), quarter(grad_keys), quarter(grad_values)], axis=1
    ).astype(BF16)


def heads_mask_of():
    row = lax.broadcasted_iota(jnp.int32, (256, 128), 0) // 64
    lane = lax.broadcasted_iota(jnp.int32, (256, 128), 1) // HEAD
    return jnp.where(row == lane, 1.0, 0.0).astype(BF16)


def attention_totals(total_ref, normed_ref, grad_joined_ref, mixture_ref, grad_ref):
    for part in range(3):
        total = dot(normed_ref[...], grad_joined_ref[:, D * part : D * part + D], 0, 0)
        for k in range(2):
            start = 256 * (2 * part + k)
            total_ref[start : start + 256, :] = total[:, 128 * k : 128 * k + 128]
    total = dot(mixture_ref[...], grad_ref[...], 0, 0)
    for k in range(2):
        total_ref[1536 + 256 * k : 1792 + 256 * k, :] = total[:, 128 * k : 128 * k + 128]


def edge_flags():
    row_index = lax.axis_index("row")
    col_index = 2 * lax.axis_index("hi") + lax.axis_index("core")
    flags = (row_index > 0, row_index < 7, col_index > 0, col_index < 15)
    return [jnp.where(flag, 1.0, 0.0).astype(F32) for flag in flags]


def shift_scale(tokens, scale_ref, shift_ref):
    return (tokens.astype(F32) * scale_ref[...] + shift_ref[...]).astype(BF16)


def copy_all(pairs, sems, first=0):
    copies = [
        pltpu.make_async_copy(source, target, sems.at[first + k])
        for k, (source, target) in enumerate(pairs)
    ]
    for copy in copies:
        copy.start()
    return copies


def wait_all(copies):
    for copy in copies:
        copy.wait()


def expand_kernel(
    x_ref,
    scale_ref,
    shift_ref,
    *refs,
):
    count = (len(refs) - 6) // 2
    sources, (lifted_out, slope_pre_out, lifted_ref) = refs[:count], refs[count : count + 3]
    targets, (slope_pre_ref, sems, load_sems) = refs[count + 3 : -3], refs[-3:]
    loads = copy_all(list(zip(sources, targets)), load_sems)
    w_expand_ref = targets[0]

    def stores(row):
        here = pl.ds(pl.multiple_of(row * COLS, COLS), COLS)
        return [
            pltpu.make_async_copy(source.at[:, here, :], target.at[:, here, :], sems.at[row, k])
            for k, (source, target) in enumerate(
                ((lifted_ref, lifted_out), (slope_pre_ref, slope_pre_out))
            )
        ]

    wait_all(loads[:1])

    @pl.loop(0, ROWS)
    def _(row):
        here = pl.ds(pl.multiple_of(row * COLS, COLS), COLS)
        shifted = shift_scale(x_ref[row], scale_ref, shift_ref)
        for pair in range(4):
            value, slope = gelu_pair(
                dot(shifted, w_expand_ref[:, 256 * pair : 256 * pair + 256], 1, 0)
            )
            value = value.astype(BF16)
            slope = slope.astype(BF16)
            for k in range(2):
                lanes = slice(128 * k, 128 * k + 128)
                lifted_ref[2 * pair + k, here, :] = value[:, lanes]
                slope_pre_ref[2 * pair + k, here, :] = slope[:, lanes]
        for copy in stores(row):
            copy.start()

    wait_all(loads[1:])
    for row in range(ROWS):
        wait_all(stores(row))


def convolve_rows(pad, block, pad_row, taps, second_ref, slope_conv_ref, row):
    for chunk in range(4):
        summed = None
        for t in range(9):
            start = LEFT - 1 + t % 3 + 32 * chunk
            term = taps[t] * pad[block, pad_row + t // 3, start : start + 32, :]
            summed = term if summed is None else summed + term
        value, slope = gelu_pair(summed)
        here = pl.ds(pl.multiple_of(row * COLS + 32 * chunk, 32), 32)
        second_ref[block, here, :] = value.astype(BF16)
        slope_conv_ref[block, here, :] = slope.astype(BF16)


def taps_of(dw_ref, block):
    lanes = pl.ds(pl.multiple_of(block * 128, 128), 128)
    return [dw_ref[t : t + 1, lanes] for t in range(9)]


def inner_rows_kernel(
    lifted_ref,
    left_ref,
    right_ref,
    scale_ref,
    shift_ref,
    w_expand_ref,
    dw_ref,
    second_out,
    second_ref,
    slope_conv_out,
    side_ref,
    pad,
    slope_conv_ref,
    sems,
):
    def stores(block):
        return [
            pltpu.make_async_copy(source.at[block], target.at[block], sems.at[block, k])
            for k, (source, target) in enumerate(
                ((second_ref, second_out), (slope_conv_ref, slope_conv_out))
            )
        ]

    inside = edge_flags()
    sides = jnp.concatenate([left_ref[...], right_ref[...]], axis=0)
    shifted = shift_scale(sides, scale_ref, shift_ref)
    place = lax.broadcasted_iota(jnp.int32, (16, 1), 0)
    flags = jnp.where(place < 8, inside[2], inside[3])
    for pair in range(4):
        value, _ = gelu_pair(dot(shifted, w_expand_ref[:, 256 * pair : 256 * pair + 256], 1, 0))
        value = value.astype(BF16).astype(F32) * flags
        for k in range(2):
            side_ref[2 * pair + k] = value[:, 128 * k : 128 * k + 128]

    @pl.loop(0, BLOCKS)
    def _(block):
        taps = taps_of(dw_ref, block)
        side = side_ref[block]
        for row in range(ROWS):
            pad[block, row, LEFT : LEFT + COLS, :] = lifted_ref[
                block, COLS * row : COLS * row + COLS, :
            ].astype(F32)
            pad[block, row, LEFT - 1 : LEFT, :] = side[row : row + 1]
            pad[block, row, LEFT + COLS : LEFT + COLS + 1, :] = side[8 + row : 9 + row]

        @pl.loop(0, ROWS - 2)
        def _(row):
            convolve_rows(pad, block, row, taps, second_ref, slope_conv_ref, row)

        for copy in stores(block):
            copy.start()

    for block in range(BLOCKS):
        wait_all(stores(block))


def front_kernel(
    x_ref,
    top_ref,
    bottom_ref,
    lifted_ref,
    side_ref,
    second_mid_ref,
    scale_ref,
    shift_ref,
    w_expand_ref,
    dw_ref,
    w_project_ref,
    gain_block_ref,
    w_qkv_ref,
    w_out_ref,
    bias,
    gain_grid_ref,
    grad_output_ref,
    second_out,
    slope_edge_out,
    section_one_out,
    section_two_out,
    send_ref,
    normed_block_out,
    joined_out,
    probs_out,
    mixture_out,
    pad,
    cells,
    outcome,
    second_ref,
    slope_edge_ref,
    section_one_ref,
    section_two_ref,
    normed_block_ref,
    joined_ref,
    probs_ref,
    mixture_ref,
    sems,
    part_sems,
):
    send_ref[:, 16:32, :] = grad_output_ref[...].reshape(64, 16, D)
    heads_mask = heads_mask_of()
    inside = edge_flags()
    for source, row, flag in ((top_ref, 0, inside[0]), (bottom_ref, 5, inside[1])):
        shifted = shift_scale(source[...], scale_ref, shift_ref)
        for pair in range(4):
            value, _ = gelu_pair(dot(shifted, w_expand_ref[:, 256 * pair : 256 * pair + 256], 1, 0))
            value = value.astype(BF16).astype(F32) * flag
            for k in range(2):
                block = 2 * pair + k
                part = value[:, 128 * k : 128 * k + 128]
                pad[block, row, LEFT : LEFT + COLS, :] = part[:COLS]
                pad[block, row, LEFT - 1 : LEFT, :] = part[COLS : COLS + 1] * inside[2]
                pad[block, row, LEFT + COLS : LEFT + COLS + 1, :] = (
                    part[COLS + 1 : COLS + 2] * inside[3]
                )

    @pl.loop(0, BLOCKS)
    def _(block):
        taps = taps_of(dw_ref, block)
        side = side_ref[block]
        for row, place in ((0, 1), (1, 2), (6, 3), (7, 4)):
            pad[block, place, LEFT : LEFT + COLS, :] = lifted_ref[
                block, COLS * row : COLS * row + COLS, :
            ].astype(F32)
            pad[block, place, LEFT - 1 : LEFT, :] = side[row : row + 1]
            pad[block, place, LEFT + COLS : LEFT + COLS + 1, :] = side[8 + row : 9 + row]
        for row in range(2):
            convolve_rows(pad, block, 3 * row, taps, second_ref, slope_edge_ref, row)

    stores = copy_all(((second_ref, second_out), (slope_edge_ref, slope_edge_out)), sems)
    for part in range(4):
        rows = slice(2 * part, 2 * part + 2)
        summed = x_ref[rows].reshape(256, D).astype(F32)
        for pair in range(4):
            pieces = []
            for block in (2 * pair, 2 * pair + 1):
                pieces.append(
                    jnp.concatenate(
                        [
                            second_ref[block, COLS * (row // 7) : COLS * (row // 7) + COLS, :]
                            if row in (0, 7)
                            else second_mid_ref[block, COLS * (row - 1) : COLS * row, :]
                            for row in (2 * part, 2 * part + 1)
                        ],
                        axis=0,
                    )
                )
            summed = summed + dot(
                jnp.concatenate(pieces, axis=1), w_project_ref[256 * pair : 256 * pair + 256, :], 1, 0
            )
        section_one = summed.astype(BF16)
        section_one_ref[rows] = section_one.reshape(2, COLS, D)
        cells[rows] = section_one.astype(F32).reshape(2, COLS, D)

    stores += copy_all([(section_one_ref, section_one_out)], sems, first=2)

    def part_stores(part):
        here = pl.ds(pl.multiple_of(part * 256, 256), 256)
        columns = pl.ds(pl.multiple_of(part * 32, 32), 32)
        eight = pl.ds(part * 8, 8)
        return [
            pltpu.make_async_copy(source, target, part_sems.at[part, k])
            for k, (source, target) in enumerate(
                (
                    (normed_block_ref.at[here, :], normed_block_out.at[here, :]),
                    (joined_ref.at[here, :], joined_out.at[here, :]),
                    (mixture_ref.at[here, :], mixture_out.at[here, :]),
                    (probs_ref.at[eight], probs_out.at[eight]),
                    (section_two_ref.at[:, columns, :], section_two_out.at[:, columns, :]),
                )
            )
        ]

    @pl.loop(0, 4)
    def _(part):
        here = pl.ds(pl.multiple_of(part * 256, 256), 256)
        columns = pl.ds(pl.multiple_of(part * 32, 32), 32)
        section_one = four_windows(cells[:, columns, :])
        normed = (norm_parts(section_one)[0] * gain_block_ref[...]).astype(BF16)
        normed_block_ref[here, :] = normed
        joined = dot(normed, w_qkv_ref[...], 1, 0).astype(BF16)
        joined_ref[here, :] = joined
        probs, mixture = attend(joined, bias, heads_mask)
        for index in range(8):
            probs_ref[part * 8 + index] = probs[index]
        mixture_ref[here, :] = mixture
        section_two = (section_one + dot(mixture, w_out_ref[...], 1, 0)).astype(BF16).astype(F32)
        section_two_ref[:, columns, :] = from_four_windows(section_two).astype(BF16)
        for copy in part_stores(part):
            copy.start()
        normed = norm_parts(section_two)[0] * gain_grid_ref[...]
        outcome[:, columns, :] = from_four_windows(normed)

    send_ref[:, 0:16, :] = outcome[...].astype(BF16).reshape(64, 16, D)
    wait_all(stores)
    for part in range(4):
        wait_all(part_stores(part))


def grid_kernel(
    got_ref,
    w_qkv_ref,
    w_out_ref,
    bias,
    grad_normed_ref,
    total_ref,
    mixture_ref,
    grad_joined_ref,
):
    heads_mask = heads_mask_of()
    normed_ref = got_ref.at[0]
    grad_ref = got_ref.at[1]

    @pl.loop(0, 4)
    def _(part):
        here = pl.ds(pl.multiple_of(part * 256, 256), 256)
        joined = dot(normed_ref[here, :], w_qkv_ref[...], 1, 0).astype(BF16)
        grad_mix = dot(grad_ref[here, :], w_out_ref[...], 1, 1).astype(BF16)
        probs, mixture = attend(joined, bias, heads_mask)
        mixture_ref[here, :] = mixture
        grad_joined = attend_back(joined, probs, grad_mix, heads_mask)
        grad_joined_ref[here, :] = grad_joined
        grad_normed_ref[here, :] = dot(grad_joined, w_qkv_ref[...], 1, 1).astype(BF16)

    attention_totals(total_ref, normed_ref, grad_joined_ref, mixture_ref, grad_ref)


def block_kernel(
    parts,
    returned_ref,
    grad_output_ref,
    section_two_in,
    section_one_in,
    joined_in,
    probs_in,
    slope_mid_in,
    slope_edge_in,
    normed_block_in,
    mixture_in,
    gain_grid_ref,
    gain_block_ref,
    w_qkv_ref,
    w_out_ref,
    w_project_ref,
    *rest,
):
    (
        section_two_ref,
        section_one_ref,
        joined_ref,
        probs_ref,
        slope_ref,
        normed_block_ref,
        mixture_ref,
        grad_one_ref,
        fetch_sems,
        sems,
    ) = rest[-10:]
    if len(rest) == 16:
        before_ref = None
        grad_one_out, inner_ref, total_ref, left_ref, right_ref, ends = rest[:-10]
    else:
        before_ref, grad_one_out, inner_ref, total_out, total_ref = rest[:-10]
    fetches = []
    stores = []
    for index, part in enumerate(parts):
        here = pl.ds(256 * part, 256)
        target = pl.ds(256 * index, 256)
        columns = pl.ds(32 * part, 32)
        to = pl.ds(32 * index, 32)
        fetches.append(
            copy_all(
                (
                    (section_two_in.at[:, columns, :], section_two_ref.at[:, to, :]),
                    (joined_in.at[here, :], joined_ref.at[target, :]),
                    (probs_in.at[pl.ds(8 * part, 8)], probs_ref.at[pl.ds(8 * index, 8)]),
                    (section_one_in.at[:, columns, :], section_one_ref.at[:, to, :]),
                    (
                        slope_mid_in.at[:, :, columns, :],
                        slope_ref.at[:, pl.ds(1, 6), to, :],
                    ),
                    (
                        slope_edge_in.at[:, pl.ds(0, 1), columns, :],
                        slope_ref.at[:, pl.ds(0, 1), to, :],
                    ),
                    (
                        slope_edge_in.at[:, pl.ds(1, 1), columns, :],
                        slope_ref.at[:, pl.ds(7, 1), to, :],
                    ),
                    (normed_block_in.at[here, :], normed_block_ref.at[target, :]),
                    (mixture_in.at[here, :], mixture_ref.at[target, :]),
                ),
                fetch_sems.at[index],
            )
        )
    heads_mask = heads_mask_of()
    all_windows = []
    all_joined = []
    for index, part in enumerate(parts):
        here = slice(256 * index, 256 * index + 256)
        columns = slice(32 * part, 32 * part + 32)
        out_columns = slice(32 * index, 32 * index + 32)

        def windows_of(ref, columns):
            return four_windows(ref[:, columns, :].astype(F32))

        wait_all(fetches[index][:1])
        grad_two = windows_of(grad_output_ref, columns) + norm_back(
            windows_of(section_two_ref, out_columns),
            gain_grid_ref[...],
            windows_of(returned_ref, columns),
        )
        grad_windows = grad_two.astype(BF16)
        grad_two = grad_windows.astype(F32)
        grad_mix = dot(grad_windows, w_out_ref[...], 1, 1).astype(BF16)
        wait_all(fetches[index][1:3])
        joined = joined_ref[here, :]
        probs = [probs_ref[index * 8 + k] for k in range(8)]
        grad_joined = attend_back(joined, probs, grad_mix, heads_mask)
        all_windows.append(grad_windows)
        all_joined.append(grad_joined)
        grad_normed = dot(grad_joined, w_qkv_ref[...], 1, 1).astype(BF16).astype(F32)
        wait_all(fetches[index][3:4])
        grad_one = grad_two + norm_back(
            windows_of(section_one_ref, out_columns), gain_block_ref[...], grad_normed
        )
        grad_one_ref[:, out_columns, :] = from_four_windows(grad_one).astype(BF16)
        stores += copy_all(
            [(grad_one_ref.at[:, out_columns, :], grad_one_out.at[:, out_columns, :])],
            sems,
            first=index,
        )
    for index in range(2):
        wait_all(fetches[index][7:])
    joined = jnp.concatenate(all_joined, axis=0)
    windows = jnp.concatenate(all_windows, axis=0)
    products = [
        (normed_block_ref, joined[:, D * part : D * part + D], 512 * part) for part in range(3)
    ]
    for left, right, start in products + [(mixture_ref, windows, 1536)]:
        total = dot(left[...], right, 0, 0)
        for k in range(2):
            place = slice(start + 256 * k, start + 256 * k + 256)
            value = total[:, 128 * k : 128 * k + 128]
            total_ref[place, :] = value if before_ref is None else before_ref[place, :] + value
    if before_ref is not None:
        stores += copy_all([(total_ref, total_out)], sems, first=2)
    for index, part in enumerate(parts):
        wait_all(fetches[index][4:7])
        out_columns = slice(32 * index, 32 * index + 32)
        grad_one = grad_one_ref[:, out_columns, :].reshape(256, D)
        for pair in range(4):
            through = dot(grad_one, w_project_ref[256 * pair : 256 * pair + 256, :], 1, 1)
            for k in range(2):
                block = 2 * pair + k
                slope = slope_ref[block, :, out_columns, :].astype(F32)
                inner = through[:, 128 * k : 128 * k + 128].reshape(ROWS, 32, 128) * slope
                inner_ref[block, :, out_columns, :] = inner.astype(BF16)
                if before_ref is None:
                    side, column = (0, 0) if part == 0 else (1, 31)
                    for row in range(ROWS):
                        ends[side, block, row : row + 1, :] = inner[row, column : column + 1]
    if before_ref is None:
        left_ref[...] = ends[0].astype(BF16)
        right_ref[...] = ends[1].astype(BF16)
    wait_all(stores)


def total_kernel(
    core_ref,
    outer_in,
    middle_in,
    second_mid_in,
    second_edge_in,
    block_total_in,
    grid_total_in,
    _,
    grad_one_ref,
    early_send_ref,
    early_keep_ref,
    total_ref,
    second_ref,
    sems,
):
    rows = (pl.ds(0, COLS), pl.ds(COLS, 6 * COLS), pl.ds(7 * COLS, COLS))
    fetches = copy_all(
        (
            (outer_in.at[:, pl.ds(0, 32), :], grad_one_ref.at[:, pl.ds(0, 32), :]),
            (outer_in.at[:, pl.ds(32, 32), :], grad_one_ref.at[:, pl.ds(96, 32), :]),
            (middle_in, grad_one_ref.at[:, pl.ds(32, 64), :]),
            (second_edge_in.at[:, pl.ds(0, COLS), :], second_ref.at[:, rows[0], :]),
            (second_mid_in, second_ref.at[:, rows[1], :]),
            (second_edge_in.at[:, pl.ds(COLS, COLS), :], second_ref.at[:, rows[2], :]),
            (block_total_in, total_ref.at[pl.ds(0, 2048), :]),
            (grid_total_in, total_ref.at[pl.ds(4096, 2048), :]),
        ),
        sems,
    )
    wait_all(fetches[:6])
    grad_one = grad_one_ref[...].reshape(TOKENS, D)
    for pair in range(4):
        joined = jnp.concatenate([second_ref[2 * pair], second_ref[2 * pair + 1]], axis=1)
        total = dot(joined, grad_one, 0, 0)
        for k in range(2):
            start = 2048 + 1024 * k + 256 * pair
            total_ref[start : start + 256, :] = total[:, 128 * k : 128 * k + 128]
    wait_all(fetches[6:])
    own = pl.ds(pl.multiple_of(core_ref[0] * 3072, 3072), 3072)
    other = pl.ds(pl.multiple_of((1 - core_ref[0]) * 3072, 3072), 3072)
    early_keep_ref[...] = total_ref[own, :].astype(BF16)
    early_send_ref[...] = total_ref[other, :].astype(BF16)


def back_rows(pad, block, pad_row, taps, lifted_ref, slope_pre_ref, preact_ref, row, totals):
    totals = list(totals)
    for chunk in range(4):
        here = pl.ds(pl.multiple_of(row * COLS + 32 * chunk, 32), 32)
        lifted = lifted_ref[block, here, :].astype(F32)
        summed = None
        for t in range(9):
            start = LEFT + 1 - t % 3 + 32 * chunk
            cells = pad[block, pad_row + 2 - t // 3, start : start + 32, :]
            term = taps[t] * cells
            summed = term if summed is None else summed + term
            totals[t] = totals[t] + jnp.sum((lifted * cells).reshape(4, 8, 128), axis=0)
        grad = summed * slope_pre_ref[block, here, :].astype(F32)
        preact_ref[block, here, :] = grad.astype(BF16)
    return tuple(totals)


def fill_row(pad, block, place, row, outer_ref, middle_ref, left, right):
    cells = whole_row(outer_ref[block, row], middle_ref[block, row])
    pad[block, place, LEFT : LEFT + COLS, :] = cells.astype(F32)
    pad[block, place, LEFT - 1 : LEFT, :] = left[row : row + 1]
    pad[block, place, LEFT + COLS : LEFT + COLS + 1, :] = right[row : row + 1]


def back_inner_kernel(
    lifted_in,
    slope_pre_in,
    outer_ref,
    middle_ref,
    left_ref,
    right_ref,
    dw_ref,
    preact_ref,
    taps_ref,
    pad,
    lifted_ref,
    slope_pre_ref,
    sems,
):
    rows = pl.ds(COLS, 6 * COLS)

    def fetches(block):
        return [
            pltpu.make_async_copy(
                source.at[block, rows, :], target.at[block], sems.at[block, k]
            )
            for k, (source, target) in enumerate(
                ((lifted_in, lifted_ref), (slope_pre_in, slope_pre_ref))
            )
        ]

    for block in range(BLOCKS):
        for copy in fetches(block):
            copy.start()

    @pl.loop(0, BLOCKS)
    def _(block):
        left = left_ref[block].astype(F32)
        right = right_ref[block].astype(F32)
        for row in range(ROWS):
            fill_row(pad, block, row, row, outer_ref, middle_ref, left, right)
        wait_all(fetches(block))
        taps = taps_of(dw_ref, block)

        def step(row, totals):
            return back_rows(
                pad, block, row, taps, lifted_ref, slope_pre_ref, preact_ref, row, totals
            )

        totals = lax.fori_loop(0, ROWS - 2, step, (jnp.zeros((8, 128), F32),) * 9)
        for t in range(9):
            taps_ref[t, pl.ds(block, 1), :] = jnp.sum(totals[t], axis=0, keepdims=True)


def back_kernel(
    core_ref,
    x_ref,
    lifted_in,
    slope_pre_in,
    outer_ref,
    middle_ref,
    top_ref,
    bottom_ref,
    left_ref,
    right_ref,
    scale_ref,
    shift_ref,
    dw_ref,
    preact_mid_ref,
    taps_mid_ref,
    _,
    preact_ref,
    late_send_ref,
    late_keep_ref,
    pad,
    lifted_ref,
    slope_pre_ref,
    shifted_ref,
    total_ref,
    taps_ref,
    sems,
):
    first, last = pl.ds(0, COLS), pl.ds(7 * COLS, COLS)
    second = pl.ds(COLS, COLS)
    fetches = copy_all(
        [
            (source.at[:, rows, :], target.at[:, place, :])
            for source, target in ((lifted_in, lifted_ref), (slope_pre_in, slope_pre_ref))
            for rows, place in ((first, first), (last, second))
        ],
        sems,
    )
    for place, row in enumerate((1, 2, 3, 4, 5, 6, 0, 7)):
        shifted_ref[COLS * place : COLS * place + COLS, :] = shift_scale(
            x_ref[row], scale_ref, shift_ref
        )
    wait_all(fetches)

    @pl.loop(0, BLOCKS)
    def _(block):
        left = left_ref[block].astype(F32)
        right = right_ref[block].astype(F32)
        for source, place in ((top_ref, 0), (bottom_ref, 5)):
            cells = source[block].astype(F32)
            pad[block, place, LEFT : LEFT + COLS, :] = cells[:COLS]
            pad[block, place, LEFT - 1 : LEFT, :] = cells[COLS : COLS + 1]
            pad[block, place, LEFT + COLS : LEFT + COLS + 1, :] = cells[COLS + 1 : COLS + 2]
        for row, place in ((0, 1), (1, 2), (6, 3), (7, 4)):
            fill_row(pad, block, place, row, outer_ref, middle_ref, left, right)
        taps = taps_of(dw_ref, block)
        totals = (jnp.zeros((8, 128), F32),) * 9
        for row in range(2):
            totals = back_rows(
                pad, block, 3 * row, taps, lifted_ref, slope_pre_ref, preact_ref, row, totals
            )
        for t in range(9):
            taps_ref[t, pl.ds(block, 1), :] = taps_mid_ref[t, pl.ds(block, 1), :] + jnp.sum(
                totals[t], axis=0, keepdims=True
            )

    for pair in range(4):
        pieces = [
            jnp.concatenate([preact_mid_ref[block], preact_ref[block]], axis=0)
            for block in (2 * pair, 2 * pair + 1)
        ]
        total = dot(shifted_ref[...], jnp.concatenate(pieces, axis=1), 0, 0)
        for k in range(2):
            start = 256 * (2 * pair + k)
            total_ref[start : start + 256, :] = total[:, 128 * k : 128 * k + 128]
    own = pl.ds(pl.multiple_of(core_ref[0] * 1024, 1024), 1024)
    other = pl.ds(pl.multiple_of((1 - core_ref[0]) * 1024, 1024), 1024)
    for target, rows in ((late_keep_ref, own), (late_send_ref, other)):
        large = total_ref[rows, :].reshape(CHUNKS, 16, 128)
        for index in range(CHUNKS):
            taps = taps_ref[index] if index < 9 else jnp.zeros((8, 128), F32)
            target[index] = jnp.concatenate([large[index], taps], axis=0).astype(BF16)


def input_kernel(
    preact_mid_ref, preact_edge_ref, grad_one_ref, w_expand_ref, scale_ref, grad_input_ref
):
    for rows, source, first in (
        ((0, 7), preact_edge_ref, 0),
        ((1, 2), preact_mid_ref, 0),
        ((3, 4), preact_mid_ref, 256),
        ((5, 6), preact_mid_ref, 512),
    ):
        summed = jnp.zeros((256, D), F32)
        for pair in range(4):
            joined = jnp.concatenate(
                [source[2 * pair + k, first : first + 256, :] for k in range(2)], axis=1
            )
            summed = summed + dot(joined, w_expand_ref[:, 256 * pair : 256 * pair + 256], 1, 1)
        summed = summed * scale_ref[...]
        for k, row in enumerate(rows):
            value = grad_one_ref[row].astype(F32) + summed[COLS * k : COLS * k + COLS]
            grad_input_ref[row] = value.astype(BF16)


VMEM = pl.BlockSpec(memory_space=pltpu.VMEM)
SMEM = pl.BlockSpec(memory_space=pltpu.SMEM)
HBM = pl.BlockSpec(memory_space=pltpu.HBM)


def shape(dims, kind):
    return jax.ShapeDtypeStruct(dims, kind)


def call(kernel, ins, outs, scratch, smem=(), far=(), far_out=(), keep=(), limit=16, flops=10**9):
    ins = [pltpu.with_memory_space_constraint(x, pltpu.HBM) if k in far else x for k, x in enumerate(ins)]
    specs = [SMEM if k in smem else HBM if k in far else VMEM for k in range(len(ins))]
    return pl.pallas_call(
        kernel,
        out_shape=[
            pltpu.VMEM(o.shape, o.dtype)
            if k in keep
            else pltpu.HBM(o.shape, o.dtype)
            if k in far_out
            else o
            for k, o in enumerate(outs)
        ],
        in_specs=specs,
        out_specs=[HBM if k in far_out else VMEM for k in range(len(outs))],
        scratch_shapes=scratch,
        compiler_params=pltpu.CompilerParams(vmem_limit_bytes=limit * 1024 * 1024),
        cost_estimate=pl.CostEstimate(flops=flops, bytes_accessed=flops // 100, transcendentals=0),
    )(*ins)


CHUNKS = 64
CHUNK = 72
FACTOR = float((64 * 2048) ** (-0.5))


def pair_kernel(early_keep_ref, early_got_ref, late_keep_ref, late_got_ref, parts_ref):
    early = early_keep_ref[...].astype(F32) + early_got_ref[...].astype(F32)
    early = early.reshape(CHUNKS, 48, 128)
    late = late_keep_ref[...].astype(F32) + late_got_ref[...].astype(F32)
    parts_ref[...] = jnp.concatenate([early, late], axis=1).astype(BF16)


def sum_kernel(got_ref, out_ref):
    def step(index, total):
        return total + got_ref[index].astype(F32)

    total = lax.fori_loop(0, CHUNKS, step, jnp.zeros((CHUNK, 128), F32), unroll=8)
    total = total.astype(BF16)
    for index in range(CHUNKS):
        out_ref[index] = total


def unpack_kernel(
    core_ref,
    mine_ref,
    other_ref,
    expand_ref,
    kernel_ref,
    project_ref,
    qkv_block_ref,
    out_block_ref,
    qkv_grid_ref,
    out_grid_ref,
):
    core = core_ref[0]

    targets = (
        [(qkv_block_ref, 0, 128 * k, 256) for k in range(6)]
        + [(out_block_ref, 0, 128 * k, 256) for k in range(2)]
        + [(project_ref, 0, 128 * k, 1024) for k in range(2)]
        + [(qkv_grid_ref, 0, 128 * k, 256) for k in range(6)]
        + [(out_grid_ref, 0, 128 * k, 256) for k in range(2)]
    )
    early = [
        (target, first + start, column)
        for target, first, column, count in targets
        for start in range(0, count, 16)
    ]

    def fill(low_ref, high_ref):
        for half, ref in enumerate((low_ref, high_ref)):
            for index in range(CHUNKS):
                value = ref[index].astype(F32) * FACTOR
                for k in range(3):
                    target, row, column = early[192 * half + 3 * index + k]
                    target[row : row + 16, column : column + 128] = value[16 * k : 16 * k + 16]
                start = 1024 * half + 16 * index
                column = start // 256 * 128
                expand_ref[start % 256 : start % 256 + 16, column : column + 128] = value[48:64]
                if half == 0 and index < 9:
                    for block in range(BLOCKS):
                        kernel_ref[index : index + 1, 128 * block : 128 * block + 128] = value[
                            64 + block : 65 + block
                        ]

    @pl.when(core == 0)
    def _():
        fill(mine_ref, other_ref)

    @pl.when(core == 1)
    def _():
        fill(other_ref, mine_ref)


def beside_rows(first, last):
    count = lax.axis_size("row")
    down = [(i, i + 1) for i in range(count - 1)]
    up = [(i + 1, i) for i in range(count - 1)]
    return lax.ppermute(last, "row", down), lax.ppermute(first, "row", up)


def beside_columns(first, last):
    axes = ("hi", "core")
    count = lax.axis_size("hi") * lax.axis_size("core")
    right = [(i, i + 1) for i in range(count - 1)]
    left = [(i + 1, i) for i in range(count - 1)]
    return lax.ppermute(last, axes, right), lax.ppermute(first, axes, left)


def across(values):
    return lax.all_to_all(values, ("row", "hi"), split_axis=0, concat_axis=0, tiled=True)


def sibling(values):
    return lax.ppermute(values, "core", [(0, 1), (1, 0)])


def shards(
    x_input,
    grad_output,
    in_scale,
    in_shift,
    w_expand,
    dw_kernel,
    w_project,
    gain_block,
    w_qkv_block,
    w_out_block,
    bias_block,
    gain_grid,
    w_qkv_grid,
    w_out_grid,
    bias_grid,
):
    core_flag = lax.axis_index("core").reshape(1).astype(jnp.int32)
    scale = in_scale.reshape(1, D)
    shift = in_shift.reshape(1, D)
    gain_block = gain_block.reshape(1, D)
    gain_grid = gain_grid.reshape(1, D)
    hidden = shape((BLOCKS, TOKENS, 128), BF16)
    hidden_mid = shape((BLOCKS, 6 * COLS, 128), BF16)
    hidden_edge = shape((BLOCKS, 2 * COLS, 128), BF16)
    hidden_vmem = pltpu.VMEM(hidden.shape, BF16)
    mid_vmem = pltpu.VMEM(hidden_mid.shape, BF16)
    edge_vmem = pltpu.VMEM(hidden_edge.shape, BF16)
    pad_inner = pltpu.VMEM((BLOCKS, ROWS, WIDE, 128), F32)
    pad_edge = pltpu.VMEM((BLOCKS, 6, WIDE, 128), F32)
    tile = shape((ROWS, COLS, D), BF16)
    tokens = shape((TOKENS, D), BF16)
    tokens_vmem = pltpu.VMEM((TOKENS, D), BF16)
    edge_row = shape((144, D), BF16)
    edge_column = shape((ROWS, D), BF16)
    dma = pltpu.SemaphoreType.DMA

    x_input, x_left, x_right = call(
        load_kernel,
        [x_input],
        [tile, edge_column, edge_column],
        [dma, pltpu.VMEM((2, ROWS, D), F32)],
        far=(0,),
        keep=range(3),
        limit=4,
    )
    x_left, x_right = beside_columns(x_left, x_right)
    later = [
        w_expand,
        dw_kernel,
        grad_output,
        w_project,
        w_qkv_block,
        w_out_block,
        w_qkv_grid,
        w_out_grid,
    ]
    (
        lifted_far,
        slope_pre,
        lifted,
        w_expand,
        dw_kernel,
        grad_output,
        w_project,
        w_qkv_block,
        w_out_block,
        w_qkv_grid,
        w_out_grid,
    ) = call(
        expand_kernel,
        [x_input, scale, shift] + later,
        [hidden, hidden, hidden] + [shape(v.shape, v.dtype) for v in later],
        [hidden_vmem, dma((ROWS, 2)), dma((len(later),))],
        far=range(3, 3 + len(later)),
        far_out=(0, 1),
        keep=range(2, 3 + len(later)),
        limit=8,
        flops=4 * 10**9,
    )
    x_first, x_last = call(
        x_edge_kernel,
        [x_input, x_left, x_right],
        [edge_row, edge_row],
        [],
        keep=(0, 1),
        limit=4,
    )
    x_top, x_bottom = beside_rows(x_first, x_last)
    second_mid_far, second_mid, slope_mid, side_lifted = call(
        inner_rows_kernel,
        [lifted, x_left, x_right, scale, shift, w_expand, dw_kernel],
        [hidden_mid, hidden_mid, hidden_mid, shape((BLOCKS, 16, 128), F32)],
        [pad_inner, mid_vmem, dma((BLOCKS, 2))],
        far_out=(0, 2),
        keep=(1, 3),
        limit=12,
        flops=4 * 10**9,
    )
    cube = shape((2, 64, 256), F32)
    cube_block, cube_grid = call(
        bias_kernel,
        [bias_block, bias_grid],
        [cube, cube],
        [pltpu.VMEM((2 * HEADS, 256), F32)],
        keep=(0, 1),
        limit=8,
    )
    (
        second_edge_far,
        slope_edge,
        section_one,
        section_two,
        sendable,
        normed_block,
        joined,
        probs,
        mixture,
    ) = call(
        front_kernel,
        [
            x_input,
            x_top,
            x_bottom,
            lifted,
            side_lifted,
            second_mid,
            scale,
            shift,
            w_expand,
            dw_kernel,
            w_project,
            gain_block,
            w_qkv_block,
            w_out_block,
            cube_block,
            gain_grid,
            grad_output,
        ],
        [
            hidden_edge,
            hidden_edge,
            tile,
            tile,
            shape((64, 32, D), BF16),
            tokens,
            shape((TOKENS, 3 * D), BF16),
            shape((32, 64, 256), F32),
            tokens,
        ],
        [
            pad_edge,
            pltpu.VMEM((ROWS, COLS, D), F32),
            pltpu.VMEM((ROWS, COLS, D), F32),
            edge_vmem,
            edge_vmem,
            pltpu.VMEM(tile.shape, BF16),
            pltpu.VMEM(tile.shape, BF16),
            tokens_vmem,
            pltpu.VMEM((TOKENS, 3 * D), BF16),
            pltpu.VMEM((32, 64, 256), F32),
            tokens_vmem,
            dma((3,)),
            dma((4, 5)),
        ],
        keep=(4,),
        far_out=(0, 1, 2, 3, 5, 6, 7, 8),
        limit=20,
    )

    got = across(sendable).transpose(1, 0, 2).reshape(2, TOKENS, D)
    grad_groups, grid_total = call(
        grid_kernel,
        [got, w_qkv_grid, w_out_grid, cube_grid],
        [tokens, shape((2048, 128), F32)],
        [tokens_vmem, pltpu.VMEM((TOKENS, 3 * D), BF16)],
        keep=(0, 1),
        limit=8,
    )
    returned = across(grad_groups.reshape(16, 64, D).transpose(1, 0, 2)).reshape(ROWS, COLS, D)

    def block_half(parts, before):
        edge = [] if before else [shape((BLOCKS, ROWS, 128), BF16)] * 2
        half_vmem = pltpu.VMEM((TOKENS // 2, D), BF16)
        half_tile = pltpu.VMEM((ROWS, COLS // 2, D), BF16)
        return call(
            functools.partial(block_kernel, parts),
            [
                returned,
                grad_output,
                section_two,
                section_one,
                joined,
                probs,
                slope_mid.reshape(BLOCKS, 6, COLS, 128),
                slope_edge.reshape(BLOCKS, 2, COLS, 128),
                normed_block,
                mixture,
                gain_grid,
                gain_block,
                w_qkv_block,
                w_out_block,
                w_project,
            ]
            + before,
            [
                shape((ROWS, COLS // 2, D), BF16),
                shape((BLOCKS, ROWS, COLS // 2, 128), BF16),
                shape((2048, 128), F32),
            ]
            + edge,
            ([] if before else [pltpu.VMEM((2, BLOCKS, ROWS, 128), F32)])
            + ([pltpu.VMEM((2048, 128), F32)] if before else [])
            + [
                half_tile,
                half_tile,
                pltpu.VMEM((TOKENS // 2, 3 * D), BF16),
                pltpu.VMEM((16, 64, 256), F32),
                pltpu.VMEM((BLOCKS, ROWS, COLS // 2, 128), BF16),
                half_vmem,
                half_vmem,
                half_tile,
                dma((2, 9)),
                dma((3,)),
            ],
            far=range(2, 10),
            far_out=(0, 2) if before else (0,),
            keep=(1,) if before else (1, 2, 3, 4),
            limit=12,
            flops=4*10**9,
        )

    one_outer, inner_outer, block_total, left, right = block_half((0, 3), [])
    left, right = beside_columns(left, right)
    one_middle, inner_middle, block_total = block_half((1, 2), [block_total])
    edge_cells = shape((BLOCKS, 144, 128), BF16)
    first, last = call(
        inner_edge_kernel,
        [inner_outer, inner_middle, left, right],
        [edge_cells, edge_cells],
        [],
        keep=(0, 1),
        limit=4,
    )
    top, bottom = beside_rows(first, last)
    early = shape((3072, 128), BF16)
    grad_one, early_send, early_keep = call(
        total_kernel,
        [
            core_flag,
            one_outer,
            one_middle,
            second_mid_far,
            second_edge_far,
            block_total,
            grid_total,
            first,
        ],
        [tile, early, early],
        [pltpu.VMEM((6144, 128), F32), hidden_vmem, dma((8,))],
        smem=(0,),
        far=range(1, 7),
        keep=range(3),
        limit=8,
        flops=3 * 10**9,
    )
    preact_mid, taps_mid = call(
        back_inner_kernel,
        [lifted_far, slope_pre, inner_outer, inner_middle, left, right, dw_kernel],
        [hidden_mid, shape((9, BLOCKS, 128), F32)],
        [pad_inner, mid_vmem, mid_vmem, dma((BLOCKS, 2))],
        far=(0, 1),
        keep=(0, 1),
        limit=12,
        flops=4 * 10**9,
    )
    early_got = sibling(early_send)
    late = shape((CHUNKS, 24, 128), BF16)
    parts = shape((CHUNKS, CHUNK, 128), BF16)
    preact_edge, late_send, late_keep = call(
        back_kernel,
        [
            core_flag,
            x_input,
            lifted_far,
            slope_pre,
            inner_outer,
            inner_middle,
            top,
            bottom,
            left,
            right,
            scale,
            shift,
            dw_kernel,
            preact_mid,
            taps_mid,
            early_keep,
        ],
        [hidden_edge, late, late],
        [
            pad_edge,
            edge_vmem,
            edge_vmem,
            tokens_vmem,
            pltpu.VMEM((2048, 128), F32),
            pltpu.VMEM((9, BLOCKS, 128), F32),
            dma((4,)),
        ],
        smem=(0,),
        far=(2, 3),
        keep=(0, 1, 2),
        limit=12,
        flops=4 * 10**9,
    )
    (grad_input,) = call(
        input_kernel, [preact_mid, preact_edge, grad_one, w_expand, scale], [tile], [], limit=8
    )

    (paired,) = call(
        pair_kernel,
        [early_keep, early_got, late_keep, sibling(late_send)],
        [parts],
        [],
        keep=(0,),
        limit=4,
    )
    (summed,) = call(sum_kernel, [across(paired)], [parts], [], keep=(0,), limit=4)
    mine = across(summed)
    totals = call(
        unpack_kernel,
        [core_flag, mine, sibling(mine)],
        [
            shape((D, E), F32),
            shape((9, E), F32),
            shape((E, D), F32),
            shape((D, 3 * D), F32),
            shape((D, D), F32),
            shape((D, 3 * D), F32),
            shape((D, D), F32),
        ],
        [],
        smem=(0,),
        limit=16,
    )
    return (grad_input, *totals)


def solution(mesh):
    split = Mesh(mesh.devices.reshape(8, 8, 2), ("row", "hi", "core"))
    tile = P("row", ("hi", "core"), None)
    return jax.shard_map(
        shards,
        mesh=split,
        in_specs=(tile, tile) + (P(),) * 13,
        out_specs=(tile,) + (P(),) * 7,
        check_vma=False,
    )
```

```python
import functools

import jax
import jax.numpy as jnp
from jax import lax
from jax.experimental import pallas as pl
from jax.experimental.pallas import tpu as pltpu
from jax.sharding import Mesh
from jax.sharding import PartitionSpec as P

F32 = jnp.float32
BF16 = jnp.bfloat16
EPSILON = 1e-05
HEADS = 8
HEAD = 32
SCALE = HEAD ** (-0.5)
ROWS = 8
COLS = 128
TOKENS = ROWS * COLS
D = 256
E = 1024
BLOCKS = E // 128
LEFT = 8
WIDE = COLS + 2 * LEFT
GELU_1 = 0.7978845608028654
GELU_3 = 0.044715 * GELU_1


def dot(left, right, left_dim, right_dim):
    return lax.dot_general(
        left, right, (((left_dim,), (right_dim,)), ((), ())), preferred_element_type=F32
    )


def gelu_pair(values):
    square = values * values
    half = 0.5 + 0.5 * jnp.tanh(values * (GELU_1 + GELU_3 * square))
    value = values * half
    slope = half + value * (1.0 - half) * (2.0 * GELU_1 + (6.0 * GELU_3) * square)
    return value, slope


def norm_parts(values):
    centered = values - jnp.mean(values, axis=-1, keepdims=True)
    spread = jnp.mean(centered * centered, axis=-1, keepdims=True)
    inverse = lax.rsqrt(spread + EPSILON)
    return centered * inverse, inverse


def norm_back(values, gain, grad):
    unit, inverse = norm_parts(values)
    scaled = grad * gain
    mean_grad = jnp.mean(scaled, axis=-1, keepdims=True)
    mean_unit = jnp.mean(scaled * unit, axis=-1, keepdims=True)
    return inverse * (scaled - mean_grad - unit * mean_unit)


def four_windows(cells):
    return jnp.concatenate(
        [cells[:, 8 * m : 8 * m + 8, :].reshape(64, D) for m in range(4)], axis=0
    )


def from_four_windows(tokens):
    return jnp.concatenate(
        [tokens[64 * m : 64 * m + 64].reshape(8, 8, D) for m in range(4)], axis=1
    )


def load_kernel(x_in, x_ref, near_ref, next_ref, sem, ends):
    copy = pltpu.make_async_copy(x_in, x_ref, sem)
    copy.start()
    copy.wait()
    for row in range(ROWS):
        ends[0, row : row + 1, :] = x_ref[row, 0:16, :].astype(F32)[0:1]
        ends[1, row : row + 1, :] = x_ref[row, COLS - 16 : COLS, :].astype(F32)[15:16]
    near, after = trade(ends[1], ends[0])
    near_ref[...] = near.astype(BF16)
    next_ref[...] = after.astype(BF16)


def with_corners(cells, left, right):
    rest = jnp.zeros((14, cells.shape[1]), F32)
    corners = jnp.concatenate([left, right, rest], axis=0).astype(BF16)
    return jnp.concatenate([cells, corners], axis=0)


def x_edge_kernel(x_ref, near_ref, next_ref, pair_ref, other_ref):
    right, left = trade(near_ref[...], next_ref[...])
    even = even_row()
    for last, target in ((even, pair_ref), (1 - even, other_ref)):
        target[...] = with_corners(x_ref[7 * last], edge_of(last, left), edge_of(last, right))


def inner_edge_kernel(outer_ref, middle_ref, near_ref, next_ref, pair_ref, other_ref):
    even = even_row()
    for block in range(BLOCKS):
        right, left = trade(near_ref[block], next_ref[block])
        for last, target in ((even, pair_ref), (1 - even, other_ref)):
            cells = whole_row(outer_ref[block, 7 * last], middle_ref[block, 7 * last])
            target[block] = with_corners(cells, edge_of(last, left), edge_of(last, right))


def whole_row(outer, middle):
    axis = outer.ndim - 2
    first = lax.slice_in_dim(outer, 0, 32, axis=axis)
    last = lax.slice_in_dim(outer, 32, 64, axis=axis)
    return jnp.concatenate([first, middle, last], axis=axis)


def bias_kernel(block_ref, grid_ref, bias_block_ref, bias_grid_ref, table):
    source = lax.broadcasted_iota(jnp.int32, (256, 1024), 0)
    place = lax.broadcasted_iota(jnp.int32, (256, 1024), 1)
    wanted = 15 * (place % 128 // 8) + 7 + place % 8 - place // 128
    onehot = jnp.where(source == wanted, 1.0, 0.0).astype(BF16)
    table[...] = jnp.zeros((2 * HEADS, 256), F32)
    table[0:HEADS, 0:225] = block_ref[...]
    table[HEADS : 2 * HEADS, 0:225] = grid_ref[...]
    rest = table[...]
    spread = jnp.zeros((2 * HEADS, 1024), F32)
    for _ in range(3):
        part = rest.astype(BF16)
        spread = spread + dot(part, onehot, 1, 0)
        rest = rest - part.astype(F32)
    for which, bias_ref in enumerate((bias_block_ref, bias_grid_ref)):
        for head in range(HEADS):
            line = HEADS * which + head
            rows = jnp.concatenate(
                [spread[line : line + 1, 128 * e : 128 * e + 128] for e in range(8)], axis=0
            )
            for a_k in range(8):
                start = 8 * (7 - a_k)
                bias_ref[
                    head // 4, 8 * a_k : 8 * a_k + 8, 64 * (head % 4) : 64 * (head % 4) + 64
                ] = rows[:, start : start + 64]


def stacked(part, heads_mask):
    return jnp.concatenate([part] * 4, axis=0) * heads_mask


def pick(product):
    lane = lax.broadcasted_iota(jnp.int32, (64, 128), 1)
    low = jnp.where(lane < 32, product[0:64], product[64:128])
    high = jnp.where(lane < 96, product[128:192], product[192:256])
    return jnp.where(lane < 64, low, high)


def softmax_keys(scores):
    shifted = jnp.exp(scores - jnp.max(scores, axis=0, keepdims=True))
    return shifted * (1.0 / jnp.sum(shifted, axis=0, keepdims=True))


def half_of(joined, part, half, group):
    start = part * D + half * 128
    return joined[64 * group : 64 * group + 64, start : start + 128]


PAIRS = [(group, half) for group in range(4) for half in range(2)]


def quarter(parts):
    return jnp.concatenate(
        [jnp.concatenate(parts[2 * g : 2 * g + 2], axis=1) for g in range(4)], axis=0
    )


def attend(joined, bias_ref, heads_mask):
    scores = [
        dot(half_of(joined, 1, h, g), stacked(half_of(joined, 0, h, g), heads_mask), 1, 1)
        for g, h in PAIRS
    ]
    probs = [softmax_keys(s * SCALE + bias_ref[h]) for s, (_, h) in zip(scores, PAIRS)]
    products = [dot(p.astype(BF16), half_of(joined, 2, h, g), 0, 0) for p, (g, h) in zip(probs, PAIRS)]
    return probs, quarter([pick(p).astype(BF16) for p in products])


def attend_back(joined, probs, grad_mix, heads_mask):
    stacks = [stacked(half_of(grad_mix, 0, h, g), heads_mask) for g, h in PAIRS]
    grad_weights = [
        dot(half_of(joined, 2, h, g), stack, 1, 1).astype(BF16).astype(F32)
        for stack, (g, h) in zip(stacks, PAIRS)
    ]
    grad_values = [dot(p.astype(BF16), stack, 1, 0) for p, stack in zip(probs, stacks)]
    grad_scores = []
    for p, w in zip(probs, grad_weights):
        centre = jnp.sum(w * p, axis=0, keepdims=True)
        grad_scores.append((p * (w - centre) * SCALE).astype(BF16))
    grad_keys = [
        dot(s, stacked(half_of(joined, 0, h, g), heads_mask), 1, 0)
        for s, (g, h) in zip(grad_scores, PAIRS)
    ]
    grad_queries = [
        pick(dot(s, half_of(joined, 1, h, g), 0, 0)) for s, (g, h) in zip(grad_scores, PAIRS)
    ]
    return jnp.concatenate(
        [quarter(grad_queries), quarter(grad_keys), quarter(grad_values)], axis=1
    ).astype(BF16)


def heads_mask_of():
    row = lax.broadcasted_iota(jnp.int32, (256, 128), 0) // 64
    lane = lax.broadcasted_iota(jnp.int32, (256, 128), 1) // HEAD
    return jnp.where(row == lane, 1.0, 0.0).astype(BF16)


def attention_totals(total_ref, normed_ref, grad_joined_ref, mixture_ref, grad_ref):
    for part in range(3):
        total = dot(normed_ref[...], grad_joined_ref[:, D * part : D * part + D], 0, 0)
        for k in range(2):
            start = 256 * (2 * part + k)
            total_ref[start : start + 256, :] = total[:, 128 * k : 128 * k + 128]
    total = dot(mixture_ref[...], grad_ref[...], 0, 0)
    for k in range(2):
        total_ref[1536 + 256 * k : 1792 + 256 * k, :] = total[:, 128 * k : 128 * k + 128]


def edge_flags():
    row_index = lax.axis_index("row")
    col_index = 2 * lax.axis_index("hi") + lax.axis_index("core")
    flags = (row_index > 0, row_index < 7, col_index > 0, col_index < 15)
    return [jnp.where(flag, 1.0, 0.0).astype(F32) for flag in flags]


def shift_scale(tokens, scale_ref, shift_ref):
    return (tokens.astype(F32) * scale_ref[...] + shift_ref[...]).astype(BF16)


def trade(first, second):
    here = jnp.where(lax.axis_index("core") == 0, 1.0, 0.0).astype(F32)
    first, second = first.astype(F32), second.astype(F32)
    there = 1.0 - here
    return first * here + second * there, first * there + second * here


def even_row():
    return 1 - lax.rem(lax.axis_index("row"), 2)


def edge_of(even, value):
    last = even.astype(F32)
    return value[7:8] * last + value[0:1] * (1.0 - last)


def copy_all(pairs, sems, first=0):
    copies = [
        pltpu.make_async_copy(source, target, sems.at[first + k])
        for k, (source, target) in enumerate(pairs)
    ]
    for copy in copies:
        copy.start()
    return copies


def wait_all(copies):
    for copy in copies:
        copy.wait()


def expand_kernel(
    x_ref,
    scale_ref,
    shift_ref,
    *refs,
):
    count = (len(refs) - 6) // 2
    sources, (lifted_out, slope_pre_out, lifted_ref) = refs[:count], refs[count : count + 3]
    targets, (slope_pre_ref, sems, load_sems) = refs[count + 3 : -3], refs[-3:]
    loads = copy_all([(sources[0], targets[0])], load_sems)
    w_expand_ref = targets[0]

    def stores(row):
        here = pl.ds(pl.multiple_of(row * COLS, COLS), COLS)
        return [
            pltpu.make_async_copy(source.at[:, here, :], target.at[:, here, :], sems.at[row, k])
            for k, (source, target) in enumerate(
                ((lifted_ref, lifted_out), (slope_pre_ref, slope_pre_out))
            )
        ]

    wait_all(loads)
    loads = copy_all(list(zip(sources[1:], targets[1:])), load_sems, first=1)

    @pl.loop(0, ROWS)
    def _(row):
        here = pl.ds(pl.multiple_of(row * COLS, COLS), COLS)
        shifted = shift_scale(x_ref[row], scale_ref, shift_ref)
        for pair in range(4):
            value, slope = gelu_pair(
                dot(shifted, w_expand_ref[:, 256 * pair : 256 * pair + 256], 1, 0)
            )
            value = value.astype(BF16)
            slope = slope.astype(BF16)
            for k in range(2):
                lanes = slice(128 * k, 128 * k + 128)
                lifted_ref[2 * pair + k, here, :] = value[:, lanes]
                slope_pre_ref[2 * pair + k, here, :] = slope[:, lanes]
        for copy in stores(row):
            copy.start()

    wait_all(loads)
    for row in range(ROWS):
        wait_all(stores(row))


def convolve_rows(pad, block, pad_row, taps, second_ref, slope_conv_ref, row):
    for chunk in range(4):
        summed = None
        for t in range(9):
            start = LEFT - 1 + t % 3 + 32 * chunk
            term = taps[t] * pad[block, pad_row + t // 3, start : start + 32, :]
            summed = term if summed is None else summed + term
        value, slope = gelu_pair(summed)
        here = pl.ds(pl.multiple_of(row * COLS + 32 * chunk, 32), 32)
        second_ref[block, here, :] = value.astype(BF16)
        slope_conv_ref[block, here, :] = slope.astype(BF16)


def taps_of(dw_ref, block):
    lanes = pl.ds(pl.multiple_of(block * 128, 128), 128)
    return [dw_ref[t : t + 1, lanes] for t in range(9)]


def inner_rows_kernel(
    lifted_ref,
    near_ref,
    next_ref,
    scale_ref,
    shift_ref,
    w_expand_ref,
    dw_ref,
    second_out,
    second_ref,
    slope_conv_out,
    side_ref,
    pad,
    slope_conv_ref,
    sems,
):
    def stores(block):
        return [
            pltpu.make_async_copy(source.at[block], target.at[block], sems.at[block, k])
            for k, (source, target) in enumerate(
                ((second_ref, second_out), (slope_conv_ref, slope_conv_out))
            )
        ]

    inside = edge_flags()
    right, left = trade(near_ref[...], next_ref[...])
    sides = jnp.concatenate([left, right], axis=0)
    shifted = shift_scale(sides, scale_ref, shift_ref)
    place = lax.broadcasted_iota(jnp.int32, (16, 1), 0)
    flags = jnp.where(place < 8, inside[2], inside[3])
    for pair in range(4):
        value, _ = gelu_pair(dot(shifted, w_expand_ref[:, 256 * pair : 256 * pair + 256], 1, 0))
        value = value.astype(BF16).astype(F32) * flags
        for k in range(2):
            side_ref[2 * pair + k] = value[:, 128 * k : 128 * k + 128]

    @pl.loop(0, BLOCKS)
    def _(block):
        taps = taps_of(dw_ref, block)
        side = side_ref[block]
        for row in range(ROWS):
            pad[block, row, LEFT : LEFT + COLS, :] = lifted_ref[
                block, COLS * row : COLS * row + COLS, :
            ].astype(F32)
            pad[block, row, LEFT - 1 : LEFT, :] = side[row : row + 1]
            pad[block, row, LEFT + COLS : LEFT + COLS + 1, :] = side[8 + row : 9 + row]

        for row in range(ROWS - 2):
            convolve_rows(pad, block, row, taps, second_ref, slope_conv_ref, row)

        for copy in stores(block):
            copy.start()

    for block in range(BLOCKS):
        wait_all(stores(block))


def front_kernel(
    x_ref,
    pair_ref,
    other_ref,
    lifted_ref,
    side_ref,
    second_mid_ref,
    scale_ref,
    shift_ref,
    w_expand_ref,
    dw_ref,
    w_project_ref,
    gain_block_ref,
    w_qkv_ref,
    w_out_ref,
    bias,
    gain_grid_ref,
    grad_output_ref,
    second_out,
    slope_edge_out,
    section_one_out,
    section_two_out,
    send_ref,
    normed_block_out,
    joined_out,
    probs_out,
    mixture_out,
    pad,
    cells,
    outcome,
    second_ref,
    slope_edge_ref,
    section_one_ref,
    section_two_ref,
    normed_block_ref,
    joined_ref,
    probs_ref,
    mixture_ref,
    sems,
    part_sems,
):
    send_ref[:, 16:32, :] = grad_output_ref[...].reshape(64, 16, D)
    heads_mask = heads_mask_of()
    inside = edge_flags()
    even = even_row()
    for source, below in ((pair_ref, even), (other_ref, 1 - even)):
        row = 5 * below
        flag = inside[1] * below.astype(F32) + inside[0] * (1 - below).astype(F32)
        shifted = shift_scale(source[...], scale_ref, shift_ref)
        for pair in range(4):
            value, _ = gelu_pair(dot(shifted, w_expand_ref[:, 256 * pair : 256 * pair + 256], 1, 0))
            value = value.astype(BF16).astype(F32) * flag
            for k in range(2):
                block = 2 * pair + k
                part = value[:, 128 * k : 128 * k + 128]
                pad[block, row, LEFT : LEFT + COLS, :] = part[:COLS]
                pad[block, row, LEFT - 1 : LEFT, :] = part[COLS : COLS + 1] * inside[2]
                pad[block, row, LEFT + COLS : LEFT + COLS + 1, :] = (
                    part[COLS + 1 : COLS + 2] * inside[3]
                )

    @pl.loop(0, BLOCKS)
    def _(block):
        taps = taps_of(dw_ref, block)
        side = side_ref[block]
        for row, place in ((0, 1), (1, 2), (6, 3), (7, 4)):
            pad[block, place, LEFT : LEFT + COLS, :] = lifted_ref[
                block, COLS * row : COLS * row + COLS, :
            ].astype(F32)
            pad[block, place, LEFT - 1 : LEFT, :] = side[row : row + 1]
            pad[block, place, LEFT + COLS : LEFT + COLS + 1, :] = side[8 + row : 9 + row]
        for row in range(2):
            convolve_rows(pad, block, 3 * row, taps, second_ref, slope_edge_ref, row)

    stores = copy_all(((second_ref, second_out), (slope_edge_ref, slope_edge_out)), sems)
    for part in range(4):
        rows = slice(2 * part, 2 * part + 2)
        summed = x_ref[rows].reshape(256, D).astype(F32)
        for pair in range(4):
            pieces = []
            for block in (2 * pair, 2 * pair + 1):
                pieces.append(
                    jnp.concatenate(
                        [
                            second_ref[block, COLS * (row // 7) : COLS * (row // 7) + COLS, :]
                            if row in (0, 7)
                            else second_mid_ref[block, COLS * (row - 1) : COLS * row, :]
                            for row in (2 * part, 2 * part + 1)
                        ],
                        axis=0,
                    )
                )
            summed = summed + dot(
                jnp.concatenate(pieces, axis=1), w_project_ref[256 * pair : 256 * pair + 256, :], 1, 0
            )
        section_one = summed.astype(BF16)
        section_one_ref[rows] = section_one.reshape(2, COLS, D)
        cells[rows] = section_one.astype(F32).reshape(2, COLS, D)

    stores += copy_all([(section_one_ref, section_one_out)], sems, first=2)

    def part_stores(part):
        here = pl.ds(part * 256, 256)
        columns = pl.ds(part * 32, 32)
        eight = pl.ds(part * 8, 8)
        return [
            pltpu.make_async_copy(source, target, part_sems.at[part, k])
            for k, (source, target) in enumerate(
                (
                    (normed_block_ref.at[here, :], normed_block_out.at[here, :]),
                    (joined_ref.at[here, :], joined_out.at[here, :]),
                    (mixture_ref.at[here, :], mixture_out.at[here, :]),
                    (probs_ref.at[eight], probs_out.at[eight]),
                    (section_two_ref.at[:, columns, :], section_two_out.at[:, columns, :]),
                )
            )
        ]

    for part in range(4):
        here = slice(256 * part, 256 * part + 256)
        columns = slice(32 * part, 32 * part + 32)
        section_one = four_windows(cells[:, columns, :])
        normed = (norm_parts(section_one)[0] * gain_block_ref[...]).astype(BF16)
        normed_block_ref[here, :] = normed
        joined = dot(normed, w_qkv_ref[...], 1, 0).astype(BF16)
        joined_ref[here, :] = joined
        probs, mixture = attend(joined, bias, heads_mask)
        for index in range(8):
            probs_ref[part * 8 + index] = probs[index]
        mixture_ref[here, :] = mixture
        section_two = (section_one + dot(mixture, w_out_ref[...], 1, 0)).astype(BF16).astype(F32)
        section_two_ref[:, columns, :] = from_four_windows(section_two).astype(BF16)
        for copy in part_stores(part):
            copy.start()
        normed = norm_parts(section_two)[0] * gain_grid_ref[...]
        outcome[:, columns, :] = from_four_windows(normed)

    send_ref[:, 0:16, :] = outcome[...].astype(BF16).reshape(64, 16, D)
    wait_all(stores)
    for part in range(4):
        wait_all(part_stores(part))


def grid_kernel(
    got_ref,
    w_qkv_ref,
    w_out_ref,
    bias,
    grad_normed_ref,
    total_ref,
    mixture_ref,
    grad_joined_ref,
):
    heads_mask = heads_mask_of()
    normed_ref = got_ref.at[0]
    grad_ref = got_ref.at[1]

    for part in range(4):
        here = slice(256 * part, 256 * part + 256)
        joined = dot(normed_ref[here, :], w_qkv_ref[...], 1, 0).astype(BF16)
        grad_mix = dot(grad_ref[here, :], w_out_ref[...], 1, 1).astype(BF16)
        probs, mixture = attend(joined, bias, heads_mask)
        mixture_ref[here, :] = mixture
        grad_joined = attend_back(joined, probs, grad_mix, heads_mask)
        grad_joined_ref[here, :] = grad_joined
        grad_normed_ref[here, :] = dot(grad_joined, w_qkv_ref[...], 1, 1).astype(BF16)

    attention_totals(total_ref, normed_ref, grad_joined_ref, mixture_ref, grad_ref)


def block_kernel(
    parts,
    returned_ref,
    grad_output_ref,
    section_two_in,
    section_one_in,
    joined_in,
    probs_in,
    slope_mid_in,
    slope_edge_in,
    normed_block_in,
    mixture_in,
    gain_grid_ref,
    gain_block_ref,
    w_qkv_ref,
    w_out_ref,
    w_project_ref,
    *rest,
):
    (
        section_two_ref,
        section_one_ref,
        joined_ref,
        probs_ref,
        slope_ref,
        normed_block_ref,
        mixture_ref,
        grad_one_ref,
        fetch_sems,
        sems,
    ) = rest[-10:]
    if len(rest) == 16:
        before_ref = None
        grad_one_out, inner_ref, total_ref, near_ref, next_ref, ends = rest[:-10]
    else:
        before_ref, grad_one_out, inner_ref, total_out, total_ref = rest[:-10]
    stores = []

    def fetch(index):
        part = parts[index]
        here = pl.ds(256 * part, 256)
        target = pl.ds(256 * index, 256)
        columns = pl.ds(32 * part, 32)
        to = pl.ds(32 * index, 32)
        return [
            pltpu.make_async_copy(source, goal, fetch_sems.at[index, k])
            for k, (source, goal) in enumerate(
                (
                    (section_two_in.at[:, columns, :], section_two_ref.at[:, to, :]),
                    (joined_in.at[here, :], joined_ref.at[target, :]),
                    (probs_in.at[pl.ds(8 * part, 8)], probs_ref.at[pl.ds(8 * index, 8)]),
                    (section_one_in.at[:, columns, :], section_one_ref.at[:, to, :]),
                    (
                        slope_mid_in.at[:, :, columns, :],
                        slope_ref.at[:, pl.ds(1, 6), to, :],
                    ),
                    (
                        slope_edge_in.at[:, pl.ds(0, 1), columns, :],
                        slope_ref.at[:, pl.ds(0, 1), to, :],
                    ),
                    (
                        slope_edge_in.at[:, pl.ds(1, 1), columns, :],
                        slope_ref.at[:, pl.ds(7, 1), to, :],
                    ),
                    (normed_block_in.at[here, :], normed_block_ref.at[target, :]),
                    (mixture_in.at[here, :], mixture_ref.at[target, :]),
                )
            )
        ]

    fetches = [fetch(0), fetch(1)]
    for copy in fetches[0][:3]:
        copy.start()
    heads_mask = heads_mask_of()
    all_windows = []
    all_joined = []
    for index, part in enumerate(parts):
        here = slice(256 * index, 256 * index + 256)
        columns = slice(32 * part, 32 * part + 32)
        out_columns = slice(32 * index, 32 * index + 32)

        def windows_of(ref, columns):
            return four_windows(ref[:, columns, :].astype(F32))

        wait_all(fetches[index][:1])
        if index == 0:
            for copy in fetches[0][3:] + fetches[1]:
                copy.start()
        grad_two = windows_of(grad_output_ref, columns) + norm_back(
            windows_of(section_two_ref, out_columns),
            gain_grid_ref[...],
            windows_of(returned_ref, columns),
        )
        grad_windows = grad_two.astype(BF16)
        grad_two = grad_windows.astype(F32)
        grad_mix = dot(grad_windows, w_out_ref[...], 1, 1).astype(BF16)
        wait_all(fetches[index][1:3])
        joined = joined_ref[here, :]
        probs = [probs_ref[index * 8 + k] for k in range(8)]
        grad_joined = attend_back(joined, probs, grad_mix, heads_mask)
        all_windows.append(grad_windows)
        all_joined.append(grad_joined)
        grad_normed = dot(grad_joined, w_qkv_ref[...], 1, 1).astype(BF16).astype(F32)
        wait_all(fetches[index][3:4])
        grad_one = grad_two + norm_back(
            windows_of(section_one_ref, out_columns), gain_block_ref[...], grad_normed
        )
        grad_one_ref[:, out_columns, :] = from_four_windows(grad_one).astype(BF16)
        stores += copy_all(
            [(grad_one_ref.at[:, out_columns, :], grad_one_out.at[:, out_columns, :])],
            sems,
            first=index,
        )
    for index in range(2):
        wait_all(fetches[index][7:])
    joined = jnp.concatenate(all_joined, axis=0)
    windows = jnp.concatenate(all_windows, axis=0)
    products = [
        (normed_block_ref, joined[:, D * part : D * part + D], 512 * part) for part in range(3)
    ]
    for left, right, start in products + [(mixture_ref, windows, 1536)]:
        total = dot(left[...], right, 0, 0)
        for k in range(2):
            place = slice(start + 256 * k, start + 256 * k + 256)
            value = total[:, 128 * k : 128 * k + 128]
            total_ref[place, :] = value if before_ref is None else before_ref[place, :] + value
    if before_ref is not None:
        stores += copy_all([(total_ref, total_out)], sems, first=2)
    for index, part in enumerate(parts):
        wait_all(fetches[index][4:7])
        out_columns = slice(32 * index, 32 * index + 32)
        grad_one = grad_one_ref[:, out_columns, :].reshape(256, D)
        for pair in range(4):
            through = dot(grad_one, w_project_ref[256 * pair : 256 * pair + 256, :], 1, 1)
            for k in range(2):
                block = 2 * pair + k
                slope = slope_ref[block, :, out_columns, :].astype(F32)
                inner = through[:, 128 * k : 128 * k + 128].reshape(ROWS, 32, 128) * slope
                inner_ref[block, :, out_columns, :] = inner.astype(BF16)
                if before_ref is None:
                    side, column = (0, 0) if part == 0 else (1, 31)
                    for row in range(ROWS):
                        ends[side, block, row : row + 1, :] = inner[row, column : column + 1]
    if before_ref is None:
        near, after = trade(ends[1], ends[0])
        near_ref[...] = near.astype(BF16)
        next_ref[...] = after.astype(BF16)
    wait_all(stores)


def total_kernel(
    core_ref,
    outer_in,
    middle_in,
    second_mid_in,
    second_edge_in,
    block_total_in,
    grid_total_in,
    _,
    grad_one_ref,
    early_send_ref,
    early_keep_ref,
    total_ref,
    second_ref,
    sems,
):
    rows = (pl.ds(0, COLS), pl.ds(COLS, 6 * COLS), pl.ds(7 * COLS, COLS))
    fetches = copy_all(
        (
            (outer_in.at[:, pl.ds(0, 32), :], grad_one_ref.at[:, pl.ds(0, 32), :]),
            (outer_in.at[:, pl.ds(32, 32), :], grad_one_ref.at[:, pl.ds(96, 32), :]),
            (middle_in, grad_one_ref.at[:, pl.ds(32, 64), :]),
            (second_edge_in.at[:, pl.ds(0, COLS), :], second_ref.at[:, rows[0], :]),
            (second_mid_in, second_ref.at[:, rows[1], :]),
            (second_edge_in.at[:, pl.ds(COLS, COLS), :], second_ref.at[:, rows[2], :]),
            (block_total_in, total_ref.at[pl.ds(0, 2048), :]),
            (grid_total_in, total_ref.at[pl.ds(4096, 2048), :]),
        ),
        sems,
    )
    wait_all(fetches[:6])
    grad_one = grad_one_ref[...].reshape(TOKENS, D)
    for pair in range(4):
        joined = jnp.concatenate([second_ref[2 * pair], second_ref[2 * pair + 1]], axis=1)
        total = dot(joined, grad_one, 0, 0)
        for k in range(2):
            start = 2048 + 1024 * k + 256 * pair
            total_ref[start : start + 256, :] = total[:, 128 * k : 128 * k + 128]
    wait_all(fetches[6:])
    own = pl.ds(pl.multiple_of(core_ref[0] * 3072, 3072), 3072)
    other = pl.ds(pl.multiple_of((1 - core_ref[0]) * 3072, 3072), 3072)
    early_keep_ref[...] = total_ref[own, :].astype(BF16)
    early_send_ref[...] = total_ref[other, :].astype(BF16)


def back_rows(pad, block, pad_row, taps, lifted_ref, slope_pre_ref, preact_ref, row, totals):
    totals = list(totals)
    for chunk in range(4):
        here = pl.ds(pl.multiple_of(row * COLS + 32 * chunk, 32), 32)
        lifted = lifted_ref[block, here, :].astype(F32)
        summed = None
        for t in range(9):
            start = LEFT + 1 - t % 3 + 32 * chunk
            cells = pad[block, pad_row + 2 - t // 3, start : start + 32, :]
            term = taps[t] * cells
            summed = term if summed is None else summed + term
            totals[t] = totals[t] + jnp.sum((lifted * cells).reshape(4, 8, 128), axis=0)
        grad = summed * slope_pre_ref[block, here, :].astype(F32)
        preact_ref[block, here, :] = grad.astype(BF16)
    return tuple(totals)


def fill_row(pad, block, place, row, outer_ref, middle_ref, left, right):
    cells = whole_row(outer_ref[block, row], middle_ref[block, row])
    pad[block, place, LEFT : LEFT + COLS, :] = cells.astype(F32)
    pad[block, place, LEFT - 1 : LEFT, :] = left[row : row + 1]
    pad[block, place, LEFT + COLS : LEFT + COLS + 1, :] = right[row : row + 1]


def back_inner_kernel(
    lifted_in,
    slope_pre_in,
    outer_ref,
    middle_ref,
    near_ref,
    next_ref,
    dw_ref,
    preact_ref,
    taps_ref,
    pad,
    lifted_ref,
    slope_pre_ref,
    sems,
):
    rows = pl.ds(COLS, 6 * COLS)

    def fetches(block):
        return [
            pltpu.make_async_copy(
                source.at[block, rows, :], target.at[block], sems.at[block, k]
            )
            for k, (source, target) in enumerate(
                ((lifted_in, lifted_ref), (slope_pre_in, slope_pre_ref))
            )
        ]

    for block in range(BLOCKS):
        for copy in fetches(block):
            copy.start()

    @pl.loop(0, BLOCKS)
    def _(block):
        right, left = trade(near_ref[block], next_ref[block])
        for row in range(ROWS):
            fill_row(pad, block, row, row, outer_ref, middle_ref, left, right)
        wait_all(fetches(block))
        taps = taps_of(dw_ref, block)

        def step(row, totals):
            return back_rows(
                pad, block, row, taps, lifted_ref, slope_pre_ref, preact_ref, row, totals
            )

        totals = lax.fori_loop(0, ROWS - 2, step, (jnp.zeros((8, 128), F32),) * 9)
        for t in range(9):
            taps_ref[t, pl.ds(block, 1), :] = jnp.sum(totals[t], axis=0, keepdims=True)


def back_kernel(
    core_ref,
    x_ref,
    lifted_in,
    slope_pre_in,
    outer_ref,
    middle_ref,
    pair_ref,
    other_ref,
    near_ref,
    next_ref,
    scale_ref,
    shift_ref,
    dw_ref,
    preact_mid_ref,
    taps_mid_ref,
    _,
    preact_ref,
    late_send_ref,
    late_keep_ref,
    pad,
    lifted_ref,
    slope_pre_ref,
    shifted_ref,
    total_ref,
    taps_ref,
    sems,
):
    first, last = pl.ds(0, COLS), pl.ds(7 * COLS, COLS)
    second = pl.ds(COLS, COLS)
    fetches = copy_all(
        [
            (source.at[:, rows, :], target.at[:, place, :])
            for source, target in ((lifted_in, lifted_ref), (slope_pre_in, slope_pre_ref))
            for rows, place in ((first, first), (last, second))
        ],
        sems,
    )
    for place, row in enumerate((1, 2, 3, 4, 5, 6, 0, 7)):
        shifted_ref[COLS * place : COLS * place + COLS, :] = shift_scale(
            x_ref[row], scale_ref, shift_ref
        )
    wait_all(fetches)
    even = even_row()

    @pl.loop(0, BLOCKS)
    def _(block):
        right, left = trade(near_ref[block], next_ref[block])
        for source, place in ((pair_ref, 5 * even), (other_ref, 5 - 5 * even)):
            cells = source[block].astype(F32)
            pad[block, place, LEFT : LEFT + COLS, :] = cells[:COLS]
            pad[block, place, LEFT - 1 : LEFT, :] = cells[COLS : COLS + 1]
            pad[block, place, LEFT + COLS : LEFT + COLS + 1, :] = cells[COLS + 1 : COLS + 2]
        for row, place in ((0, 1), (1, 2), (6, 3), (7, 4)):
            fill_row(pad, block, place, row, outer_ref, middle_ref, left, right)
        taps = taps_of(dw_ref, block)
        totals = (jnp.zeros((8, 128), F32),) * 9
        for row in range(2):
            totals = back_rows(
                pad, block, 3 * row, taps, lifted_ref, slope_pre_ref, preact_ref, row, totals
            )
        for t in range(9):
            taps_ref[t, pl.ds(block, 1), :] = taps_mid_ref[t, pl.ds(block, 1), :] + jnp.sum(
                totals[t], axis=0, keepdims=True
            )

    for pair in range(4):
        pieces = [
            jnp.concatenate([preact_mid_ref[block], preact_ref[block]], axis=0)
            for block in (2 * pair, 2 * pair + 1)
        ]
        total = dot(shifted_ref[...], jnp.concatenate(pieces, axis=1), 0, 0)
        for k in range(2):
            start = 256 * (2 * pair + k)
            total_ref[start : start + 256, :] = total[:, 128 * k : 128 * k + 128]
    own = pl.ds(pl.multiple_of(core_ref[0] * 1024, 1024), 1024)
    other = pl.ds(pl.multiple_of((1 - core_ref[0]) * 1024, 1024), 1024)
    for target, rows in ((late_keep_ref, own), (late_send_ref, other)):
        large = total_ref[rows, :].reshape(CHUNKS, 16, 128)
        for index in range(CHUNKS):
            taps = taps_ref[index] if index < 9 else jnp.zeros((8, 128), F32)
            target[index] = jnp.concatenate([large[index], taps], axis=0).astype(BF16)


def input_kernel(
    preact_mid_ref, preact_edge_ref, grad_one_ref, w_expand_ref, scale_ref, grad_input_ref
):
    for rows, source, first in (
        ((0, 7), preact_edge_ref, 0),
        ((1, 2), preact_mid_ref, 0),
        ((3, 4), preact_mid_ref, 256),
        ((5, 6), preact_mid_ref, 512),
    ):
        summed = jnp.zeros((256, D), F32)
        for pair in range(4):
            joined = jnp.concatenate(
                [source[2 * pair + k, first : first + 256, :] for k in range(2)], axis=1
            )
            summed = summed + dot(joined, w_expand_ref[:, 256 * pair : 256 * pair + 256], 1, 1)
        summed = summed * scale_ref[...]
        for k, row in enumerate(rows):
            value = grad_one_ref[row].astype(F32) + summed[COLS * k : COLS * k + COLS]
            grad_input_ref[row] = value.astype(BF16)


VMEM = pl.BlockSpec(memory_space=pltpu.VMEM)
SMEM = pl.BlockSpec(memory_space=pltpu.SMEM)
HBM = pl.BlockSpec(memory_space=pltpu.HBM)


def shape(dims, kind):
    return jax.ShapeDtypeStruct(dims, kind)


def call(kernel, ins, outs, scratch, smem=(), far=(), far_out=(), keep=(), limit=16, flops=10**9):
    ins = [pltpu.with_memory_space_constraint(x, pltpu.HBM) if k in far else x for k, x in enumerate(ins)]
    specs = [SMEM if k in smem else HBM if k in far else VMEM for k in range(len(ins))]
    return pl.pallas_call(
        kernel,
        out_shape=[
            pltpu.VMEM(o.shape, o.dtype)
            if k in keep
            else pltpu.HBM(o.shape, o.dtype)
            if k in far_out
            else o
            for k, o in enumerate(outs)
        ],
        in_specs=specs,
        out_specs=[HBM if k in far_out else VMEM for k in range(len(outs))],
        scratch_shapes=scratch,
        compiler_params=pltpu.CompilerParams(vmem_limit_bytes=limit * 1024 * 1024),
        cost_estimate=pl.CostEstimate(flops=flops, bytes_accessed=flops // 100, transcendentals=0),
    )(*ins)


CHUNKS = 64
CHUNK = 72
FACTOR = float((64 * 2048) ** (-0.5))


def pair_kernel(early_keep_ref, early_got_ref, late_keep_ref, late_got_ref, _, parts_ref):
    early = early_keep_ref[...].astype(F32) + early_got_ref[...].astype(F32)
    early = early.reshape(CHUNKS, 48, 128)
    late = late_keep_ref[...].astype(F32) + late_got_ref[...].astype(F32)
    parts_ref[...] = jnp.concatenate([early, late], axis=1).astype(BF16)


def sum_kernel(got_ref, out_ref):
    def step(index, total):
        return total + got_ref[index].astype(F32)

    total = lax.fori_loop(0, CHUNKS, step, jnp.zeros((CHUNK, 128), F32), unroll=8)
    total = total.astype(BF16)
    for index in range(CHUNKS):
        out_ref[index] = total


def unpack_half(half, parts_ref, targets):
    expand, kernel, project, qkv_block, out_block, qkv_grid, out_grid = targets
    blocks = (
        [(qkv_block, 128 * k, 256) for k in range(6)]
        + [(out_block, 128 * k, 256) for k in range(2)]
        + [(project, 128 * k, 1024) for k in range(2)]
        + [(qkv_grid, 128 * k, 256) for k in range(6)]
        + [(out_grid, 128 * k, 256) for k in range(2)]
    )
    places = [
        (target, start, column)
        for target, column, count in blocks
        for start in range(0, count, 16)
    ]
    for index in range(CHUNKS):
        value = parts_ref[index].astype(F32) * FACTOR
        for k in range(3):
            target, row, column = places[192 * half + 3 * index + k]
            target[row : row + 16, column : column + 128] = value[16 * k : 16 * k + 16]
        start = 1024 * half + 16 * index
        column = start // 256 * 128
        expand[start % 256 : start % 256 + 16, column : column + 128] = value[48:64]
        if half == 0 and index < 9:
            for block in range(BLOCKS):
                kernel[index : index + 1, 128 * block : 128 * block + 128] = value[
                    64 + block : 65 + block
                ]


def half_pieces(half, arrays):
    expand, kernel, project, qkv_block, out_block, qkv_grid, out_grid = arrays
    lanes = pl.ds(128 * half, 128)
    wide = pl.ds(512 * half, 512)
    pieces = [project.at[:, lanes], expand.at[:, wide]]
    return pieces + ([qkv_block, out_block, kernel] if half == 0 else [qkv_grid, out_grid])


def mine_kernel(core_ref, mine_ref, *targets):
    for half in range(2):

        @pl.when(core_ref[0] == half)
        def _():
            unpack_half(half, mine_ref, targets)


def other_kernel(core_ref, other_ref, *refs):
    done, outs, targets, sems = refs[:7], refs[7:14], refs[14:21], refs[21]
    for half in range(2):

        @pl.when(core_ref[0] == half)
        def _():
            copies = copy_all(zip(half_pieces(half, done), half_pieces(half, outs)), sems)
            unpack_half(1 - half, other_ref, targets)
            copies += copy_all(
                zip(half_pieces(1 - half, targets), half_pieces(1 - half, outs)), sems, first=5
            )
            wait_all(copies)


def beside_rows(pair, other):
    count = lax.axis_size("row")
    swaps = []
    for first in range(2):
        pairs = [(i, i + 1) for i in range(first, count - 1, 2)]
        swaps.append(pairs + [(j, i) for i, j in pairs])
    return lax.ppermute(pair, "row", swaps[0]), lax.ppermute(other, "row", swaps[1])


def beside_columns(near, after):
    axes = ("hi", "core")
    count = lax.axis_size("hi") * lax.axis_size("core")
    pairs = [(i, i + 1) for i in range(1, count - 1, 2)]
    swap = pairs + [(j, i) for i, j in pairs]
    return sibling(near), lax.ppermute(after, axes, swap)


def across(values):
    return lax.all_to_all(values, ("row", "hi"), split_axis=0, concat_axis=0, tiled=True)


def sibling(values):
    return lax.ppermute(values, "core", [(0, 1), (1, 0)])


def shards(
    x_input,
    grad_output,
    in_scale,
    in_shift,
    w_expand,
    dw_kernel,
    w_project,
    gain_block,
    w_qkv_block,
    w_out_block,
    bias_block,
    gain_grid,
    w_qkv_grid,
    w_out_grid,
    bias_grid,
):
    core_flag = lax.axis_index("core").reshape(1).astype(jnp.int32)
    scale = in_scale.reshape(1, D)
    shift = in_shift.reshape(1, D)
    gain_block = gain_block.reshape(1, D)
    gain_grid = gain_grid.reshape(1, D)
    hidden = shape((BLOCKS, TOKENS, 128), BF16)
    hidden_mid = shape((BLOCKS, 6 * COLS, 128), BF16)
    hidden_edge = shape((BLOCKS, 2 * COLS, 128), BF16)
    hidden_vmem = pltpu.VMEM(hidden.shape, BF16)
    mid_vmem = pltpu.VMEM(hidden_mid.shape, BF16)
    edge_vmem = pltpu.VMEM(hidden_edge.shape, BF16)
    pad_inner = pltpu.VMEM((BLOCKS, ROWS, WIDE, 128), F32)
    pad_edge = pltpu.VMEM((BLOCKS, 6, WIDE, 128), F32)
    tile = shape((ROWS, COLS, D), BF16)
    tokens = shape((TOKENS, D), BF16)
    tokens_vmem = pltpu.VMEM((TOKENS, D), BF16)
    edge_row = shape((144, D), BF16)
    edge_column = shape((ROWS, D), BF16)
    dma = pltpu.SemaphoreType.DMA

    x_input, x_left, x_right = call(
        load_kernel,
        [x_input],
        [tile, edge_column, edge_column],
        [dma, pltpu.VMEM((2, ROWS, D), F32)],
        far=(0,),
        keep=range(3),
        limit=4,
    )
    x_left, x_right = beside_columns(x_left, x_right)
    later = [
        w_expand,
        dw_kernel,
        grad_output,
        w_project,
        w_qkv_block,
        w_out_block,
        w_qkv_grid,
        w_out_grid,
    ]
    (
        lifted_far,
        slope_pre,
        lifted,
        w_expand,
        dw_kernel,
        grad_output,
        w_project,
        w_qkv_block,
        w_out_block,
        w_qkv_grid,
        w_out_grid,
    ) = call(
        expand_kernel,
        [x_input, scale, shift] + later,
        [hidden, hidden, hidden] + [shape(v.shape, v.dtype) for v in later],
        [hidden_vmem, dma((ROWS, 2)), dma((len(later),))],
        far=range(3, 3 + len(later)),
        far_out=(0, 1),
        keep=range(2, 3 + len(later)),
        limit=8,
        flops=4 * 10**9,
    )
    x_first, x_last = call(
        x_edge_kernel,
        [x_input, x_left, x_right],
        [edge_row, edge_row],
        [],
        keep=(0, 1),
        limit=4,
    )
    x_top, x_bottom = beside_rows(x_first, x_last)
    second_mid_far, second_mid, slope_mid, side_lifted = call(
        inner_rows_kernel,
        [lifted, x_left, x_right, scale, shift, w_expand, dw_kernel],
        [hidden_mid, hidden_mid, hidden_mid, shape((BLOCKS, 16, 128), F32)],
        [pad_inner, mid_vmem, dma((BLOCKS, 2))],
        far_out=(0, 2),
        keep=(1, 3),
        limit=12,
        flops=4 * 10**9,
    )
    cube = shape((2, 64, 256), F32)
    cube_block, cube_grid = call(
        bias_kernel,
        [bias_block, bias_grid],
        [cube, cube],
        [pltpu.VMEM((2 * HEADS, 256), F32)],
        keep=(0, 1),
        limit=8,
    )
    (
        second_edge_far,
        slope_edge,
        section_one,
        section_two,
        sendable,
        normed_block,
        joined,
        probs,
        mixture,
    ) = call(
        front_kernel,
        [
            x_input,
            x_top,
            x_bottom,
            lifted,
            side_lifted,
            second_mid,
            scale,
            shift,
            w_expand,
            dw_kernel,
            w_project,
            gain_block,
            w_qkv_block,
            w_out_block,
            cube_block,
            gain_grid,
            grad_output,
        ],
        [
            hidden_edge,
            hidden_edge,
            tile,
            tile,
            shape((64, 32, D), BF16),
            tokens,
            shape((TOKENS, 3 * D), BF16),
            shape((32, 64, 256), F32),
            tokens,
        ],
        [
            pad_edge,
            pltpu.VMEM((ROWS, COLS, D), F32),
            pltpu.VMEM((ROWS, COLS, D), F32),
            edge_vmem,
            edge_vmem,
            pltpu.VMEM(tile.shape, BF16),
            pltpu.VMEM(tile.shape, BF16),
            tokens_vmem,
            pltpu.VMEM((TOKENS, 3 * D), BF16),
            pltpu.VMEM((32, 64, 256), F32),
            tokens_vmem,
            dma((3,)),
            dma((4, 5)),
        ],
        keep=(4,),
        far_out=(0, 1, 2, 3, 5, 6, 7, 8),
        limit=20,
    )

    got = across(sendable).transpose(1, 0, 2).reshape(2, TOKENS, D)
    grad_groups, grid_total = call(
        grid_kernel,
        [got, w_qkv_grid, w_out_grid, cube_grid],
        [tokens, shape((2048, 128), F32)],
        [
            tokens_vmem,
            pltpu.VMEM((TOKENS, 3 * D), BF16),
        ],
        keep=(0, 1),
        limit=8,
    )
    returned = across(grad_groups.reshape(16, 64, D).transpose(1, 0, 2)).reshape(ROWS, COLS, D)

    def block_half(parts, before):
        edge = [] if before else [shape((BLOCKS, ROWS, 128), BF16)] * 2
        half_vmem = pltpu.VMEM((TOKENS // 2, D), BF16)
        half_tile = pltpu.VMEM((ROWS, COLS // 2, D), BF16)
        return call(
            functools.partial(block_kernel, parts),
            [
                returned,
                grad_output,
                section_two,
                section_one,
                joined,
                probs,
                slope_mid.reshape(BLOCKS, 6, COLS, 128),
                slope_edge.reshape(BLOCKS, 2, COLS, 128),
                normed_block,
                mixture,
                gain_grid,
                gain_block,
                w_qkv_block,
                w_out_block,
                w_project,
            ]
            + before,
            [
                shape((ROWS, COLS // 2, D), BF16),
                shape((BLOCKS, ROWS, COLS // 2, 128), BF16),
                shape((2048, 128), F32),
            ]
            + edge,
            ([] if before else [pltpu.VMEM((2, BLOCKS, ROWS, 128), F32)])
            + ([pltpu.VMEM((2048, 128), F32)] if before else [])
            + [
                half_tile,
                half_tile,
                pltpu.VMEM((TOKENS // 2, 3 * D), BF16),
                pltpu.VMEM((16, 64, 256), F32),
                pltpu.VMEM((BLOCKS, ROWS, COLS // 2, 128), BF16),
                half_vmem,
                half_vmem,
                half_tile,
                dma((2, 9)),
                dma((3,)),
            ],
            far=range(2, 10),
            far_out=(0, 2) if before else (0,),
            keep=(1,) if before else (1, 2, 3, 4),
            limit=12,
            flops=4*10**9,
        )

    one_outer, inner_outer, block_total, left, right = block_half((0, 3), [])
    left, right = beside_columns(left, right)
    one_middle, inner_middle, block_total = block_half((1, 2), [block_total])
    edge_cells = shape((BLOCKS, 144, 128), BF16)
    first, last = call(
        inner_edge_kernel,
        [inner_outer, inner_middle, left, right],
        [edge_cells, edge_cells],
        [],
        keep=(0, 1),
        limit=4,
    )
    top, bottom = beside_rows(first, last)
    early = shape((3072, 128), BF16)
    grad_one, early_send, early_keep = call(
        total_kernel,
        [
            core_flag,
            one_outer,
            one_middle,
            second_mid_far,
            second_edge_far,
            block_total,
            grid_total,
            first,
        ],
        [tile, early, early],
        [pltpu.VMEM((6144, 128), F32), hidden_vmem, dma((8,))],
        smem=(0,),
        far=range(1, 7),
        keep=range(3),
        limit=8,
        flops=3 * 10**9,
    )
    preact_mid, taps_mid = call(
        back_inner_kernel,
        [lifted_far, slope_pre, inner_outer, inner_middle, left, right, dw_kernel],
        [hidden_mid, shape((9, BLOCKS, 128), F32)],
        [pad_inner, mid_vmem, mid_vmem, dma((BLOCKS, 2))],
        far=(0, 1),
        keep=(0, 1),
        limit=12,
        flops=4 * 10**9,
    )
    early_got = sibling(early_send)
    late = shape((CHUNKS, 24, 128), BF16)
    parts = shape((CHUNKS, CHUNK, 128), BF16)
    preact_edge, late_send, late_keep = call(
        back_kernel,
        [
            core_flag,
            x_input,
            lifted_far,
            slope_pre,
            inner_outer,
            inner_middle,
            top,
            bottom,
            left,
            right,
            scale,
            shift,
            dw_kernel,
            preact_mid,
            taps_mid,
            early_keep,
        ],
        [hidden_edge, late, late],
        [
            pad_edge,
            edge_vmem,
            edge_vmem,
            tokens_vmem,
            pltpu.VMEM((2048, 128), F32),
            pltpu.VMEM((9, BLOCKS, 128), F32),
            dma((4,)),
        ],
        smem=(0,),
        far=(2, 3),
        keep=(0, 1, 2),
        limit=12,
        flops=4 * 10**9,
    )
    (grad_input,) = call(
        input_kernel, [preact_mid, preact_edge, grad_one, w_expand, scale], [tile], [], limit=8
    )

    (paired,) = call(
        pair_kernel,
        [early_keep, early_got, late_keep, sibling(late_send), grad_input],
        [parts],
        [],
        far=(4,),
        keep=(0,),
        limit=4,
    )
    (summed,) = call(sum_kernel, [across(paired)], [parts], [], keep=(0,), limit=4)
    mine = across(summed)
    sums = [
        shape((D, E), F32),
        shape((9, E), F32),
        shape((E, D), F32),
        shape((D, 3 * D), F32),
        shape((D, D), F32),
        shape((D, 3 * D), F32),
        shape((D, D), F32),
    ]
    done = call(
        mine_kernel,
        [core_flag, mine],
        sums,
        [],
        smem=(0,),
        keep=range(7),
        limit=4,
        flops=2 * 10**9,
    )
    totals = call(
        other_kernel,
        [core_flag, sibling(mine), *done],
        sums,
        [pltpu.VMEM(o.shape, F32) for o in sums] + [dma((10,))],
        smem=(0,),
        far_out=range(7),
        limit=10,
    )
    return (grad_input, *totals)


def solution(mesh):
    split = Mesh(mesh.devices.reshape(8, 8, 2), ("row", "hi", "core"))
    tile = P("row", ("hi", "core"), None)
    return jax.shard_map(
        shards,
        mesh=split,
        in_specs=(tile, tile) + (P(),) * 13,
        out_specs=(tile,) + (P(),) * 7,
        check_vma=False,
    )
```

```python
import functools

import jax
import jax.numpy as jnp
from jax import lax
from jax.experimental import pallas as pl
from jax.experimental.pallas import tpu as pltpu
from jax.sharding import Mesh
from jax.sharding import PartitionSpec as P

F32 = jnp.float32
BF16 = jnp.bfloat16
EPSILON = 1e-05
HEADS = 8
HEAD = 32
SCALE = HEAD ** (-0.5)
ROWS = 8
COLS = 128
TOKENS = ROWS * COLS
D = 256
E = 1024
BLOCKS = E // 128
LEFT = 8
WIDE = COLS + 2 * LEFT
GELU_1 = 0.7978845608028654
GELU_3 = 0.044715 * GELU_1


def dot(left, right, left_dim, right_dim):
    return lax.dot_general(
        left, right, (((left_dim,), (right_dim,)), ((), ())), preferred_element_type=F32
    )


def gelu_pair(values):
    square = values * values
    half = 0.5 + 0.5 * jnp.tanh(values * (GELU_1 + GELU_3 * square))
    value = values * half
    slope = half + value * (1.0 - half) * (2.0 * GELU_1 + (6.0 * GELU_3) * square)
    return value, slope


def norm_parts(values):
    centered = values - jnp.mean(values, axis=-1, keepdims=True)
    spread = jnp.mean(centered * centered, axis=-1, keepdims=True)
    inverse = lax.rsqrt(spread + EPSILON)
    return centered * inverse, inverse


def norm_back(values, gain, grad):
    unit, inverse = norm_parts(values)
    scaled = grad * gain
    mean_grad = jnp.mean(scaled, axis=-1, keepdims=True)
    mean_unit = jnp.mean(scaled * unit, axis=-1, keepdims=True)
    return inverse * (scaled - mean_grad - unit * mean_unit)


def four_windows(cells):
    return jnp.concatenate(
        [cells[:, 8 * m : 8 * m + 8, :].reshape(64, D) for m in range(4)], axis=0
    )


def from_four_windows(tokens):
    return jnp.concatenate(
        [tokens[64 * m : 64 * m + 64].reshape(8, 8, D) for m in range(4)], axis=1
    )


def load_kernel(x_in, w_expand_in, x_ref, w_expand_ref, near_ref, next_ref, sems, ends):
    copies = copy_all(((x_in, x_ref), (w_expand_in, w_expand_ref)), sems)
    copies[0].wait()
    for row in range(ROWS):
        ends[0, row : row + 1, :] = x_ref[row, 0:16, :].astype(F32)[0:1]
        ends[1, row : row + 1, :] = x_ref[row, COLS - 16 : COLS, :].astype(F32)[15:16]
    near, after = trade(ends[1], ends[0])
    near_ref[...] = near.astype(BF16)
    next_ref[...] = after.astype(BF16)
    copies[1].wait()


def with_corners(cells, left, right):
    rest = jnp.zeros((14, cells.shape[1]), F32)
    corners = jnp.concatenate([left, right, rest], axis=0).astype(BF16)
    return jnp.concatenate([cells, corners], axis=0)


def x_edge_kernel(x_ref, near_ref, next_ref, pair_ref, other_ref):
    right, left = trade(near_ref[...], next_ref[...])
    even = even_row()
    for last, target in ((even, pair_ref), (1 - even, other_ref)):
        target[...] = with_corners(x_ref[7 * last], edge_of(last, left), edge_of(last, right))


def inner_edge_kernel(outer_ref, middle_ref, near_ref, next_ref, pair_ref, other_ref):
    even = even_row()
    for block in range(BLOCKS):
        right, left = trade(near_ref[block], next_ref[block])
        for last, target in ((even, pair_ref), (1 - even, other_ref)):
            cells = whole_row(outer_ref[block, 7 * last], middle_ref[block, 7 * last])
            target[block] = with_corners(cells, edge_of(last, left), edge_of(last, right))


def whole_row(outer, middle):
    axis = outer.ndim - 2
    first = lax.slice_in_dim(outer, 0, 32, axis=axis)
    last = lax.slice_in_dim(outer, 32, 64, axis=axis)
    return jnp.concatenate([first, middle, last], axis=axis)


def bias_kernel(block_ref, grid_ref, bias_block_ref, bias_grid_ref, table):
    source = lax.broadcasted_iota(jnp.int32, (256, 1024), 0)
    place = lax.broadcasted_iota(jnp.int32, (256, 1024), 1)
    wanted = 15 * (place % 128 // 8) + 7 + place % 8 - place // 128
    onehot = jnp.where(source == wanted, 1.0, 0.0).astype(BF16)
    table[...] = jnp.zeros((2 * HEADS, 256), F32)
    table[0:HEADS, 0:225] = block_ref[...]
    table[HEADS : 2 * HEADS, 0:225] = grid_ref[...]
    rest = table[...]
    spread = jnp.zeros((2 * HEADS, 1024), F32)
    for _ in range(3):
        part = rest.astype(BF16)
        spread = spread + dot(part, onehot, 1, 0)
        rest = rest - part.astype(F32)
    for which, bias_ref in enumerate((bias_block_ref, bias_grid_ref)):
        for head in range(HEADS):
            line = HEADS * which + head
            rows = jnp.concatenate(
                [spread[line : line + 1, 128 * e : 128 * e + 128] for e in range(8)], axis=0
            )
            for a_k in range(8):
                start = 8 * (7 - a_k)
                bias_ref[
                    head // 4, 8 * a_k : 8 * a_k + 8, 64 * (head % 4) : 64 * (head % 4) + 64
                ] = rows[:, start : start + 64]


def stacked(part, heads_mask):
    return jnp.concatenate([part] * 4, axis=0) * heads_mask


def pick(product):
    lane = lax.broadcasted_iota(jnp.int32, (64, 128), 1)
    low = jnp.where(lane < 32, product[0:64], product[64:128])
    high = jnp.where(lane < 96, product[128:192], product[192:256])
    return jnp.where(lane < 64, low, high)


def softmax_keys(scores):
    shifted = jnp.exp(scores - jnp.max(scores, axis=0, keepdims=True))
    return shifted * (1.0 / jnp.sum(shifted, axis=0, keepdims=True))


def half_of(joined, part, half, group):
    start = part * D + half * 128
    return joined[64 * group : 64 * group + 64, start : start + 128]


PAIRS = [(group, half) for group in range(4) for half in range(2)]


def quarter(parts):
    return jnp.concatenate(
        [jnp.concatenate(parts[2 * g : 2 * g + 2], axis=1) for g in range(4)], axis=0
    )


def attend(joined, bias_ref, heads_mask):
    scores = [
        dot(half_of(joined, 1, h, g), stacked(half_of(joined, 0, h, g), heads_mask), 1, 1)
        for g, h in PAIRS
    ]
    probs = [softmax_keys(s * SCALE + bias_ref[h]) for s, (_, h) in zip(scores, PAIRS)]
    products = [dot(p.astype(BF16), half_of(joined, 2, h, g), 0, 0) for p, (g, h) in zip(probs, PAIRS)]
    return probs, quarter([pick(p).astype(BF16) for p in products])


def attend_back(joined, probs, grad_mix, heads_mask):
    stacks = [stacked(half_of(grad_mix, 0, h, g), heads_mask) for g, h in PAIRS]
    grad_weights = [
        dot(half_of(joined, 2, h, g), stack, 1, 1).astype(BF16).astype(F32)
        for stack, (g, h) in zip(stacks, PAIRS)
    ]
    grad_values = [dot(p.astype(BF16), stack, 1, 0) for p, stack in zip(probs, stacks)]
    grad_scores = []
    for p, w in zip(probs, grad_weights):
        centre = jnp.sum(w * p, axis=0, keepdims=True)
        grad_scores.append((p * (w - centre) * SCALE).astype(BF16))
    grad_keys = [
        dot(s, stacked(half_of(joined, 0, h, g), heads_mask), 1, 0)
        for s, (g, h) in zip(grad_scores, PAIRS)
    ]
    grad_queries = [
        pick(dot(s, half_of(joined, 1, h, g), 0, 0)) for s, (g, h) in zip(grad_scores, PAIRS)
    ]
    return jnp.concatenate(
        [quarter(grad_queries), quarter(grad_keys), quarter(grad_values)], axis=1
    ).astype(BF16)


def heads_mask_of():
    row = lax.broadcasted_iota(jnp.int32, (256, 128), 0) // 64
    lane = lax.broadcasted_iota(jnp.int32, (256, 128), 1) // HEAD
    return jnp.where(row == lane, 1.0, 0.0).astype(BF16)


def attention_totals(total_ref, normed_ref, grad_joined_ref, mixture_ref, grad_ref):
    for part in range(3):
        total = dot(normed_ref[...], grad_joined_ref[:, D * part : D * part + D], 0, 0)
        for k in range(2):
            start = 256 * (2 * part + k)
            total_ref[start : start + 256, :] = total[:, 128 * k : 128 * k + 128]
    total = dot(mixture_ref[...], grad_ref[...], 0, 0)
    for k in range(2):
        total_ref[1536 + 256 * k : 1792 + 256 * k, :] = total[:, 128 * k : 128 * k + 128]


def edge_flags():
    row_index = lax.axis_index("row")
    col_index = 2 * lax.axis_index("hi") + lax.axis_index("core")
    flags = (row_index > 0, row_index < 7, col_index > 0, col_index < 15)
    return [jnp.where(flag, 1.0, 0.0).astype(F32) for flag in flags]


def shift_scale(tokens, scale_ref, shift_ref):
    return (tokens.astype(F32) * scale_ref[...] + shift_ref[...]).astype(BF16)


def trade(first, second):
    here = jnp.where(lax.axis_index("core") == 0, 1.0, 0.0).astype(F32)
    first, second = first.astype(F32), second.astype(F32)
    there = 1.0 - here
    return first * here + second * there, first * there + second * here


def even_row():
    return 1 - lax.rem(lax.axis_index("row"), 2)


def edge_of(even, value):
    last = even.astype(F32)
    return value[7:8] * last + value[0:1] * (1.0 - last)


def copy_all(pairs, sems, first=0):
    copies = [
        pltpu.make_async_copy(source, target, sems.at[first + k])
        for k, (source, target) in enumerate(pairs)
    ]
    for copy in copies:
        copy.start()
    return copies


def wait_all(copies):
    for copy in copies:
        copy.wait()


def expand_kernel(
    x_ref,
    scale_ref,
    shift_ref,
    w_expand_ref,
    *refs,
):
    count = (len(refs) - 6) // 2
    sources, (lifted_out, slope_pre_out, lifted_ref) = refs[:count], refs[count : count + 3]
    targets, (slope_pre_ref, sems, load_sems) = refs[count + 3 : -3], refs[-3:]
    loads = copy_all(list(zip(sources, targets)), load_sems)

    def stores(row):
        here = pl.ds(row * COLS, COLS)
        return [
            pltpu.make_async_copy(source.at[:, here, :], target.at[:, here, :], sems.at[row, k])
            for k, (source, target) in enumerate(
                ((lifted_ref, lifted_out), (slope_pre_ref, slope_pre_out))
            )
        ]

    for row in range(ROWS):
        here = pl.ds(row * COLS, COLS)
        shifted = shift_scale(x_ref[row], scale_ref, shift_ref)
        for pair in range(4):
            value, slope = gelu_pair(
                dot(shifted, w_expand_ref[:, 256 * pair : 256 * pair + 256], 1, 0)
            )
            value = value.astype(BF16)
            slope = slope.astype(BF16)
            for k in range(2):
                lanes = slice(128 * k, 128 * k + 128)
                lifted_ref[2 * pair + k, here, :] = value[:, lanes]
                slope_pre_ref[2 * pair + k, here, :] = slope[:, lanes]
        for copy in stores(row):
            copy.start()

    wait_all(loads)
    for row in range(ROWS):
        wait_all(stores(row))


def convolve_rows(pad, block, pad_row, taps, second_ref, slope_conv_ref, row):
    for chunk in range(4):
        summed = None
        for t in range(9):
            start = LEFT - 1 + t % 3 + 32 * chunk
            term = taps[t] * pad[block, pad_row + t // 3, start : start + 32, :]
            summed = term if summed is None else summed + term
        value, slope = gelu_pair(summed)
        here = pl.ds(pl.multiple_of(row * COLS + 32 * chunk, 32), 32)
        second_ref[block, here, :] = value.astype(BF16)
        slope_conv_ref[block, here, :] = slope.astype(BF16)


def taps_of(dw_ref, block):
    lanes = pl.ds(pl.multiple_of(block * 128, 128), 128)
    return [dw_ref[t : t + 1, lanes] for t in range(9)]


def inner_rows_kernel(
    lifted_ref,
    near_ref,
    next_ref,
    scale_ref,
    shift_ref,
    w_expand_ref,
    dw_ref,
    second_out,
    second_ref,
    slope_conv_out,
    side_ref,
    pad,
    slope_conv_ref,
    sems,
):
    def stores(block):
        return [
            pltpu.make_async_copy(source.at[block], target.at[block], sems.at[block, k])
            for k, (source, target) in enumerate(
                ((second_ref, second_out), (slope_conv_ref, slope_conv_out))
            )
        ]

    inside = edge_flags()
    right, left = trade(near_ref[...], next_ref[...])
    sides = jnp.concatenate([left, right], axis=0)
    shifted = shift_scale(sides, scale_ref, shift_ref)
    place = lax.broadcasted_iota(jnp.int32, (16, 1), 0)
    flags = jnp.where(place < 8, inside[2], inside[3])
    for pair in range(4):
        value, _ = gelu_pair(dot(shifted, w_expand_ref[:, 256 * pair : 256 * pair + 256], 1, 0))
        value = value.astype(BF16).astype(F32) * flags
        for k in range(2):
            side_ref[2 * pair + k] = value[:, 128 * k : 128 * k + 128]

    @pl.loop(0, BLOCKS)
    def _(block):
        taps = taps_of(dw_ref, block)
        side = side_ref[block]
        for row in range(ROWS):
            pad[block, row, LEFT : LEFT + COLS, :] = lifted_ref[
                block, COLS * row : COLS * row + COLS, :
            ].astype(F32)
            pad[block, row, LEFT - 1 : LEFT, :] = side[row : row + 1]
            pad[block, row, LEFT + COLS : LEFT + COLS + 1, :] = side[8 + row : 9 + row]

        for row in range(ROWS - 2):
            convolve_rows(pad, block, row, taps, second_ref, slope_conv_ref, row)

        for copy in stores(block):
            copy.start()

    for block in range(BLOCKS):
        wait_all(stores(block))


def front_kernel(
    x_ref,
    pair_ref,
    other_ref,
    lifted_ref,
    side_ref,
    second_mid_ref,
    scale_ref,
    shift_ref,
    w_expand_ref,
    dw_ref,
    w_project_ref,
    gain_block_ref,
    w_qkv_ref,
    w_out_ref,
    bias,
    gain_grid_ref,
    grad_output_ref,
    second_out,
    slope_edge_out,
    section_one_out,
    section_two_out,
    send_ref,
    normed_block_out,
    joined_out,
    probs_out,
    mixture_out,
    pad,
    cells,
    outcome,
    second_ref,
    slope_edge_ref,
    section_one_ref,
    section_two_ref,
    normed_block_ref,
    joined_ref,
    probs_ref,
    mixture_ref,
    sems,
    part_sems,
):
    send_ref[:, 16:32, :] = grad_output_ref[...].reshape(64, 16, D)
    heads_mask = heads_mask_of()
    inside = edge_flags()
    even = even_row()
    for source, below in ((pair_ref, even), (other_ref, 1 - even)):
        row = 5 * below
        flag = inside[1] * below.astype(F32) + inside[0] * (1 - below).astype(F32)
        shifted = shift_scale(source[...], scale_ref, shift_ref)
        for pair in range(4):
            value, _ = gelu_pair(dot(shifted, w_expand_ref[:, 256 * pair : 256 * pair + 256], 1, 0))
            value = value.astype(BF16).astype(F32) * flag
            for k in range(2):
                block = 2 * pair + k
                part = value[:, 128 * k : 128 * k + 128]
                pad[block, row, LEFT : LEFT + COLS, :] = part[:COLS]
                pad[block, row, LEFT - 1 : LEFT, :] = part[COLS : COLS + 1] * inside[2]
                pad[block, row, LEFT + COLS : LEFT + COLS + 1, :] = (
                    part[COLS + 1 : COLS + 2] * inside[3]
                )

    @pl.loop(0, BLOCKS)
    def _(block):
        taps = taps_of(dw_ref, block)
        side = side_ref[block]
        for row, place in ((0, 1), (1, 2), (6, 3), (7, 4)):
            pad[block, place, LEFT : LEFT + COLS, :] = lifted_ref[
                block, COLS * row : COLS * row + COLS, :
            ].astype(F32)
            pad[block, place, LEFT - 1 : LEFT, :] = side[row : row + 1]
            pad[block, place, LEFT + COLS : LEFT + COLS + 1, :] = side[8 + row : 9 + row]
        for row in range(2):
            convolve_rows(pad, block, 3 * row, taps, second_ref, slope_edge_ref, row)

    stores = copy_all(((second_ref, second_out), (slope_edge_ref, slope_edge_out)), sems)
    for part in range(4):
        rows = slice(2 * part, 2 * part + 2)
        summed = x_ref[rows].reshape(256, D).astype(F32)
        for pair in range(4):
            pieces = []
            for block in (2 * pair, 2 * pair + 1):
                pieces.append(
                    jnp.concatenate(
                        [
                            second_ref[block, COLS * (row // 7) : COLS * (row // 7) + COLS, :]
                            if row in (0, 7)
                            else second_mid_ref[block, COLS * (row - 1) : COLS * row, :]
                            for row in (2 * part, 2 * part + 1)
                        ],
                        axis=0,
                    )
                )
            summed = summed + dot(
                jnp.concatenate(pieces, axis=1), w_project_ref[256 * pair : 256 * pair + 256, :], 1, 0
            )
        section_one = summed.astype(BF16)
        section_one_ref[rows] = section_one.reshape(2, COLS, D)
        cells[rows] = section_one.astype(F32).reshape(2, COLS, D)

    stores += copy_all([(section_one_ref, section_one_out)], sems, first=2)

    def part_stores(part):
        here = pl.ds(part * 256, 256)
        columns = pl.ds(part * 32, 32)
        eight = pl.ds(part * 8, 8)
        return [
            pltpu.make_async_copy(source, target, part_sems.at[part, k])
            for k, (source, target) in enumerate(
                (
                    (normed_block_ref.at[here, :], normed_block_out.at[here, :]),
                    (joined_ref.at[here, :], joined_out.at[here, :]),
                    (mixture_ref.at[here, :], mixture_out.at[here, :]),
                    (probs_ref.at[eight], probs_out.at[eight]),
                    (section_two_ref.at[:, columns, :], section_two_out.at[:, columns, :]),
                )
            )
        ]

    for part in range(4):
        here = slice(256 * part, 256 * part + 256)
        columns = slice(32 * part, 32 * part + 32)
        section_one = four_windows(cells[:, columns, :])
        normed = (norm_parts(section_one)[0] * gain_block_ref[...]).astype(BF16)
        normed_block_ref[here, :] = normed
        joined = dot(normed, w_qkv_ref[...], 1, 0).astype(BF16)
        joined_ref[here, :] = joined
        probs, mixture = attend(joined, bias, heads_mask)
        for index in range(8):
            probs_ref[part * 8 + index] = probs[index]
        mixture_ref[here, :] = mixture
        section_two = (section_one + dot(mixture, w_out_ref[...], 1, 0)).astype(BF16).astype(F32)
        section_two_ref[:, columns, :] = from_four_windows(section_two).astype(BF16)
        for copy in part_stores(part):
            copy.start()
        normed = norm_parts(section_two)[0] * gain_grid_ref[...]
        outcome[:, columns, :] = from_four_windows(normed)

    send_ref[:, 0:16, :] = outcome[...].astype(BF16).reshape(64, 16, D)
    wait_all(stores)
    for part in range(4):
        wait_all(part_stores(part))


def grid_kernel(
    got_ref,
    w_qkv_ref,
    w_out_ref,
    bias,
    grad_normed_ref,
    total_ref,
    mixture_ref,
    grad_joined_ref,
    groups_ref,
):
    heads_mask = heads_mask_of()
    for index in range(2):
        for part in range(4):
            cells = got_ref[:, 16 * index + 4 * part : 16 * index + 4 * part + 4, :].astype(F32)
            groups_ref[index, 256 * part : 256 * part + 256, :] = (
                cells.transpose(1, 0, 2).reshape(256, D).astype(BF16)
            )
    normed_ref = groups_ref.at[0]
    grad_ref = groups_ref.at[1]

    for part in range(4):
        here = slice(256 * part, 256 * part + 256)
        joined = dot(normed_ref[here, :], w_qkv_ref[...], 1, 0).astype(BF16)
        grad_mix = dot(grad_ref[here, :], w_out_ref[...], 1, 1).astype(BF16)
        probs, mixture = attend(joined, bias, heads_mask)
        mixture_ref[here, :] = mixture
        grad_joined = attend_back(joined, probs, grad_mix, heads_mask)
        grad_joined_ref[here, :] = grad_joined
        grad_normed_ref[here, :] = dot(grad_joined, w_qkv_ref[...], 1, 1).astype(BF16)

    attention_totals(total_ref, normed_ref, grad_joined_ref, mixture_ref, grad_ref)


def quarter_fetches(far, near, parts, sems, first):
    section_two, joined, probs, section_one, slope_mid, slope_edge, normed_block, mixture = far
    two_ref, joined_ref, probs_ref, one_ref, slope_ref, normed_ref, mixture_ref = near
    fetches = []
    for index, part in enumerate(parts):
        here, columns = pl.ds(256 * part, 256), pl.ds(32 * part, 32)
        goal, to = pl.ds(256 * index, 256), pl.ds(32 * index, 32)
        pairs = (
            (section_two.at[:, columns, :], two_ref.at[:, to, :]),
            (joined.at[here, :], joined_ref.at[goal, :]),
            (probs.at[pl.ds(8 * part, 8)], probs_ref.at[pl.ds(8 * index, 8)]),
            (section_one.at[:, columns, :], one_ref.at[:, to, :]),
            (slope_mid.at[:, :, columns, :], slope_ref.at[:, pl.ds(1, 6), to, :]),
            (slope_edge.at[:, pl.ds(0, 1), columns, :], slope_ref.at[:, pl.ds(0, 1), to, :]),
            (slope_edge.at[:, pl.ds(1, 1), columns, :], slope_ref.at[:, pl.ds(7, 1), to, :]),
            (normed_block.at[here, :], normed_ref.at[goal, :]),
            (mixture.at[here, :], mixture_ref.at[goal, :]),
        )
        fetches.append(
            [
                pltpu.make_async_copy(source, target, sems.at[first + 9 * index + k])
                for k, (source, target) in enumerate(pairs)
            ]
        )
    return fetches


def block_kernel(
    parts,
    returned_ref,
    grad_output_ref,
    section_two_in,
    joined_in,
    probs_in,
    section_one_in,
    slope_mid_in,
    slope_edge_in,
    normed_block_in,
    mixture_in,
    gain_grid_ref,
    gain_block_ref,
    w_qkv_ref,
    w_out_ref,
    w_project_ref,
    *rest,
):
    far = (
        section_two_in,
        joined_in,
        probs_in,
        section_one_in,
        slope_mid_in,
        slope_edge_in,
        normed_block_in,
        mixture_in,
    )
    stores = []
    ahead = []
    if parts[0] == 0:
        before_ref = None
        grad_one_out, inner_ref, total_ref, near_ref, next_ref = rest[:5]
        ahead_refs, (ends, grad_one_ref), near_refs = rest[5:12], rest[12:14], rest[14:21]
        sems, fetch_sems = rest[21:]
        fetches = quarter_fetches(far, near_refs, parts, fetch_sems, 0)
        ahead = quarter_fetches(far, ahead_refs, (1, 2), fetch_sems, 18)
        for copy in fetches[0][:3]:
            copy.start()
    else:
        before_ref, grad_one_out, inner_ref, total_out, total_ref, grad_one_ref, sems = rest
        near_refs = far[:7]
        fetches = [[], []]
    (
        section_two_ref,
        joined_ref,
        probs_ref,
        section_one_ref,
        slope_ref,
        normed_block_ref,
        mixture_ref,
    ) = near_refs
    heads_mask = heads_mask_of()
    all_windows = []
    all_joined = []
    for index, part in enumerate(parts):
        here = slice(256 * index, 256 * index + 256)
        columns = slice(32 * part, 32 * part + 32)
        out_columns = slice(32 * index, 32 * index + 32)

        def windows_of(ref, columns):
            return four_windows(ref[:, columns, :].astype(F32))

        wait_all(fetches[index][:1])
        if index == 0:
            for copy in fetches[0][3:] + fetches[1] + sum(ahead, []):
                copy.start()
        grad_two = windows_of(grad_output_ref, columns) + norm_back(
            windows_of(section_two_ref, out_columns),
            gain_grid_ref[...],
            windows_of(returned_ref, columns),
        )
        grad_windows = grad_two.astype(BF16)
        grad_two = grad_windows.astype(F32)
        grad_mix = dot(grad_windows, w_out_ref[...], 1, 1).astype(BF16)
        wait_all(fetches[index][1:3])
        joined = joined_ref[here, :]
        probs = [probs_ref[index * 8 + k] for k in range(8)]
        grad_joined = attend_back(joined, probs, grad_mix, heads_mask)
        all_windows.append(grad_windows)
        all_joined.append(grad_joined)
        grad_normed = dot(grad_joined, w_qkv_ref[...], 1, 1).astype(BF16).astype(F32)
        wait_all(fetches[index][3:4])
        grad_one = grad_two + norm_back(
            windows_of(section_one_ref, out_columns), gain_block_ref[...], grad_normed
        )
        grad_one_ref[:, out_columns, :] = from_four_windows(grad_one).astype(BF16)
        stores += copy_all(
            [(grad_one_ref.at[:, out_columns, :], grad_one_out.at[:, out_columns, :])],
            sems,
            first=index,
        )
    for index in range(2):
        wait_all(fetches[index][7:])
    joined = jnp.concatenate(all_joined, axis=0)
    windows = jnp.concatenate(all_windows, axis=0)
    products = [
        (normed_block_ref, joined[:, D * part : D * part + D], 512 * part) for part in range(3)
    ]
    for left, right, start in products + [(mixture_ref, windows, 1536)]:
        total = dot(left[...], right, 0, 0)
        for k in range(2):
            place = slice(start + 256 * k, start + 256 * k + 256)
            value = total[:, 128 * k : 128 * k + 128]
            total_ref[place, :] = value if before_ref is None else before_ref[place, :] + value
    if before_ref is not None:
        stores += copy_all([(total_ref, total_out)], sems, first=2)
    for index, part in enumerate(parts):
        wait_all(fetches[index][4:7])
        out_columns = slice(32 * index, 32 * index + 32)
        grad_one = grad_one_ref[:, out_columns, :].reshape(256, D)
        for pair in range(4):
            through = dot(grad_one, w_project_ref[256 * pair : 256 * pair + 256, :], 1, 1)
            for k in range(2):
                block = 2 * pair + k
                slope = slope_ref[block, :, out_columns, :].astype(F32)
                inner = through[:, 128 * k : 128 * k + 128].reshape(ROWS, 32, 128) * slope
                inner_ref[block, :, out_columns, :] = inner.astype(BF16)
                if before_ref is None:
                    side, column = (0, 0) if part == 0 else (1, 31)
                    for row in range(ROWS):
                        ends[side, block, row : row + 1, :] = inner[row, column : column + 1]
    if before_ref is None:
        near, after = trade(ends[1], ends[0])
        near_ref[...] = near.astype(BF16)
        next_ref[...] = after.astype(BF16)
    wait_all(stores + sum(ahead, []))


def total_kernel(
    core_ref,
    outer_in,
    middle_in,
    second_mid_in,
    second_edge_in,
    block_total_in,
    grid_total_in,
    _,
    grad_one_ref,
    early_send_ref,
    early_keep_ref,
    total_ref,
    second_ref,
    sems,
):
    rows = (pl.ds(0, COLS), pl.ds(COLS, 6 * COLS), pl.ds(7 * COLS, COLS))
    fetches = copy_all(
        (
            (outer_in.at[:, pl.ds(0, 32), :], grad_one_ref.at[:, pl.ds(0, 32), :]),
            (outer_in.at[:, pl.ds(32, 32), :], grad_one_ref.at[:, pl.ds(96, 32), :]),
            (middle_in, grad_one_ref.at[:, pl.ds(32, 64), :]),
            (second_edge_in.at[:, pl.ds(0, COLS), :], second_ref.at[:, rows[0], :]),
            (second_mid_in, second_ref.at[:, rows[1], :]),
            (second_edge_in.at[:, pl.ds(COLS, COLS), :], second_ref.at[:, rows[2], :]),
            (block_total_in, total_ref.at[pl.ds(0, 2048), :]),
            (grid_total_in, total_ref.at[pl.ds(4096, 2048), :]),
        ),
        sems,
    )
    wait_all(fetches[:6])
    grad_one = grad_one_ref[...].reshape(TOKENS, D)
    for pair in range(4):
        joined = jnp.concatenate([second_ref[2 * pair], second_ref[2 * pair + 1]], axis=1)
        total = dot(joined, grad_one, 0, 0)
        for k in range(2):
            start = 2048 + 1024 * k + 256 * pair
            total_ref[start : start + 256, :] = total[:, 128 * k : 128 * k + 128]
    wait_all(fetches[6:])
    own = pl.ds(pl.multiple_of(core_ref[0] * 3072, 3072), 3072)
    other = pl.ds(pl.multiple_of((1 - core_ref[0]) * 3072, 3072), 3072)
    early_keep_ref[...] = total_ref[own, :].astype(BF16)
    early_send_ref[...] = total_ref[other, :].astype(BF16)


def back_rows(pad, block, pad_row, taps, lifted_ref, slope_pre_ref, preact_ref, row, totals):
    totals = list(totals)
    for chunk in range(4):
        here = pl.ds(pl.multiple_of(row * COLS + 32 * chunk, 32), 32)
        lifted = lifted_ref[block, here, :].astype(F32)
        summed = None
        for t in range(9):
            start = LEFT + 1 - t % 3 + 32 * chunk
            cells = pad[block, pad_row + 2 - t // 3, start : start + 32, :]
            term = taps[t] * cells
            summed = term if summed is None else summed + term
            totals[t] = totals[t] + jnp.sum((lifted * cells).reshape(4, 8, 128), axis=0)
        grad = summed * slope_pre_ref[block, here, :].astype(F32)
        preact_ref[block, here, :] = grad.astype(BF16)
    return tuple(totals)


def fill_row(pad, block, place, row, outer_ref, middle_ref, left, right):
    cells = whole_row(outer_ref[block, row], middle_ref[block, row])
    pad[block, place, LEFT : LEFT + COLS, :] = cells.astype(F32)
    pad[block, place, LEFT - 1 : LEFT, :] = left[row : row + 1]
    pad[block, place, LEFT + COLS : LEFT + COLS + 1, :] = right[row : row + 1]


def back_inner_kernel(
    lifted_in,
    slope_pre_in,
    outer_ref,
    middle_ref,
    near_ref,
    next_ref,
    dw_ref,
    preact_ref,
    taps_ref,
    pad,
    lifted_ref,
    slope_pre_ref,
    sems,
):
    rows = pl.ds(COLS, 6 * COLS)

    def fetches(block):
        return [
            pltpu.make_async_copy(
                source.at[block, rows, :], target.at[block], sems.at[block, k]
            )
            for k, (source, target) in enumerate(
                ((lifted_in, lifted_ref), (slope_pre_in, slope_pre_ref))
            )
        ]

    for block in range(BLOCKS):
        for copy in fetches(block):
            copy.start()

    @pl.loop(0, BLOCKS)
    def _(block):
        right, left = trade(near_ref[block], next_ref[block])
        for row in range(ROWS):
            fill_row(pad, block, row, row, outer_ref, middle_ref, left, right)
        wait_all(fetches(block))
        taps = taps_of(dw_ref, block)

        def step(row, totals):
            return back_rows(
                pad, block, row, taps, lifted_ref, slope_pre_ref, preact_ref, row, totals
            )

        totals = lax.fori_loop(0, ROWS - 2, step, (jnp.zeros((8, 128), F32),) * 9)
        for t in range(9):
            taps_ref[t, pl.ds(block, 1), :] = jnp.sum(totals[t], axis=0, keepdims=True)


def back_kernel(
    core_ref,
    x_ref,
    lifted_in,
    slope_pre_in,
    outer_ref,
    middle_ref,
    pair_ref,
    other_ref,
    near_ref,
    next_ref,
    scale_ref,
    shift_ref,
    dw_ref,
    preact_mid_ref,
    taps_mid_ref,
    _,
    preact_ref,
    late_send_ref,
    late_keep_ref,
    pad,
    lifted_ref,
    slope_pre_ref,
    shifted_ref,
    total_ref,
    taps_ref,
    sems,
):
    first, last = pl.ds(0, COLS), pl.ds(7 * COLS, COLS)
    second = pl.ds(COLS, COLS)
    fetches = copy_all(
        [
            (source.at[:, rows, :], target.at[:, place, :])
            for source, target in ((lifted_in, lifted_ref), (slope_pre_in, slope_pre_ref))
            for rows, place in ((first, first), (last, second))
        ],
        sems,
    )
    for place, row in enumerate((1, 2, 3, 4, 5, 6, 0, 7)):
        shifted_ref[COLS * place : COLS * place + COLS, :] = shift_scale(
            x_ref[row], scale_ref, shift_ref
        )
    wait_all(fetches)
    even = even_row()

    @pl.loop(0, BLOCKS)
    def _(block):
        right, left = trade(near_ref[block], next_ref[block])
        for source, place in ((pair_ref, 5 * even), (other_ref, 5 - 5 * even)):
            cells = source[block].astype(F32)
            pad[block, place, LEFT : LEFT + COLS, :] = cells[:COLS]
            pad[block, place, LEFT - 1 : LEFT, :] = cells[COLS : COLS + 1]
            pad[block, place, LEFT + COLS : LEFT + COLS + 1, :] = cells[COLS + 1 : COLS + 2]
        for row, place in ((0, 1), (1, 2), (6, 3), (7, 4)):
            fill_row(pad, block, place, row, outer_ref, middle_ref, left, right)
        taps = taps_of(dw_ref, block)
        totals = (jnp.zeros((8, 128), F32),) * 9
        for row in range(2):
            totals = back_rows(
                pad, block, 3 * row, taps, lifted_ref, slope_pre_ref, preact_ref, row, totals
            )
        for t in range(9):
            taps_ref[t, pl.ds(block, 1), :] = taps_mid_ref[t, pl.ds(block, 1), :] + jnp.sum(
                totals[t], axis=0, keepdims=True
            )

    for pair in range(4):
        pieces = [
            jnp.concatenate([preact_mid_ref[block], preact_ref[block]], axis=0)
            for block in (2 * pair, 2 * pair + 1)
        ]
        total = dot(shifted_ref[...], jnp.concatenate(pieces, axis=1), 0, 0)
        for k in range(2):
            start = 256 * (2 * pair + k)
            total_ref[start : start + 256, :] = total[:, 128 * k : 128 * k + 128]
    own = pl.ds(pl.multiple_of(core_ref[0] * 1024, 1024), 1024)
    other = pl.ds(pl.multiple_of((1 - core_ref[0]) * 1024, 1024), 1024)
    for target, rows in ((late_keep_ref, own), (late_send_ref, other)):
        large = total_ref[rows, :].reshape(CHUNKS, 16, 128)
        for index in range(CHUNKS):
            taps = taps_ref[index] if index < 9 else jnp.zeros((8, 128), F32)
            target[index] = jnp.concatenate([large[index], taps], axis=0).astype(BF16)


def input_kernel(
    preact_mid_ref, preact_edge_ref, grad_one_ref, w_expand_ref, scale_ref, grad_input_ref
):
    for rows, source, first in (
        ((0, 7), preact_edge_ref, 0),
        ((1, 2), preact_mid_ref, 0),
        ((3, 4), preact_mid_ref, 256),
        ((5, 6), preact_mid_ref, 512),
    ):
        summed = jnp.zeros((256, D), F32)
        for pair in range(4):
            joined = jnp.concatenate(
                [source[2 * pair + k, first : first + 256, :] for k in range(2)], axis=1
            )
            summed = summed + dot(joined, w_expand_ref[:, 256 * pair : 256 * pair + 256], 1, 1)
        summed = summed * scale_ref[...]
        for k, row in enumerate(rows):
            value = grad_one_ref[row].astype(F32) + summed[COLS * k : COLS * k + COLS]
            grad_input_ref[row] = value.astype(BF16)


VMEM = pl.BlockSpec(memory_space=pltpu.VMEM)
SMEM = pl.BlockSpec(memory_space=pltpu.SMEM)
HBM = pl.BlockSpec(memory_space=pltpu.HBM)


def shape(dims, kind):
    return jax.ShapeDtypeStruct(dims, kind)


def call(kernel, ins, outs, scratch, smem=(), far=(), far_out=(), keep=(), limit=16, flops=10**9):
    ins = [pltpu.with_memory_space_constraint(x, pltpu.HBM) if k in far else x for k, x in enumerate(ins)]
    specs = [SMEM if k in smem else HBM if k in far else VMEM for k in range(len(ins))]
    return pl.pallas_call(
        kernel,
        out_shape=[
            pltpu.VMEM(o.shape, o.dtype)
            if k in keep
            else pltpu.HBM(o.shape, o.dtype)
            if k in far_out
            else o
            for k, o in enumerate(outs)
        ],
        in_specs=specs,
        out_specs=[HBM if k in far_out else VMEM for k in range(len(outs))],
        scratch_shapes=scratch,
        compiler_params=pltpu.CompilerParams(vmem_limit_bytes=limit * 1024 * 1024),
        cost_estimate=pl.CostEstimate(flops=flops, bytes_accessed=flops // 100, transcendentals=0),
    )(*ins)


CHUNKS = 64
CHUNK = 72
FACTOR = float((64 * 2048) ** (-0.5))


def pair_kernel(early_keep_ref, early_got_ref, late_keep_ref, late_got_ref, _, parts_ref):
    early = early_keep_ref[...].astype(F32) + early_got_ref[...].astype(F32)
    early = early.reshape(CHUNKS, 48, 128)
    late = late_keep_ref[...].astype(F32) + late_got_ref[...].astype(F32)
    parts_ref[...] = jnp.concatenate([early, late], axis=1).astype(BF16)


def sum_kernel(got_ref, out_ref):
    def step(index, total):
        return total + got_ref[index].astype(F32)

    total = lax.fori_loop(0, CHUNKS, step, jnp.zeros((CHUNK, 128), F32), unroll=8)
    total = total.astype(BF16)
    for index in range(CHUNKS):
        out_ref[index] = total


def unpack_half(half, parts_ref, targets):
    expand, kernel, project, qkv_block, out_block, qkv_grid, out_grid = targets
    blocks = (
        [(qkv_block, 128 * k, 256) for k in range(6)]
        + [(out_block, 128 * k, 256) for k in range(2)]
        + [(project, 128 * k, 1024) for k in range(2)]
        + [(qkv_grid, 128 * k, 256) for k in range(6)]
        + [(out_grid, 128 * k, 256) for k in range(2)]
    )
    places = [
        (target, start, column)
        for target, column, count in blocks
        for start in range(0, count, 16)
    ]
    for index in range(CHUNKS):
        value = parts_ref[index].astype(F32) * FACTOR
        for k in range(3):
            target, row, column = places[192 * half + 3 * index + k]
            target[row : row + 16, column : column + 128] = value[16 * k : 16 * k + 16]
        start = 1024 * half + 16 * index
        column = start // 256 * 128
        expand[start % 256 : start % 256 + 16, column : column + 128] = value[48:64]
        if half == 0 and index < 9:
            for block in range(BLOCKS):
                kernel[index : index + 1, 128 * block : 128 * block + 128] = value[
                    64 + block : 65 + block
                ]


def half_pieces(half, arrays):
    expand, kernel, project, qkv_block, out_block, qkv_grid, out_grid = arrays
    lanes = pl.ds(128 * half, 128)
    wide = pl.ds(512 * half, 512)
    pieces = [project.at[:, lanes], expand.at[:, wide]]
    return pieces + ([qkv_block, out_block, kernel] if half == 0 else [qkv_grid, out_grid])


def mine_kernel(core_ref, mine_ref, *targets):
    for half in range(2):

        @pl.when(core_ref[0] == half)
        def _():
            unpack_half(half, mine_ref, targets)


def other_kernel(core_ref, other_ref, *refs):
    done, outs, targets, sems = refs[:7], refs[7:14], refs[14:21], refs[21]
    for half in range(2):

        @pl.when(core_ref[0] == half)
        def _():
            copies = copy_all(zip(half_pieces(half, done), half_pieces(half, outs)), sems)
            unpack_half(1 - half, other_ref, targets)
            copies += copy_all(
                zip(half_pieces(1 - half, targets), half_pieces(1 - half, outs)), sems, first=5
            )
            wait_all(copies)


def beside_rows(pair, other):
    count = lax.axis_size("row")
    swaps = []
    for first in range(2):
        pairs = [(i, i + 1) for i in range(first, count - 1, 2)]
        swaps.append(pairs + [(j, i) for i, j in pairs])
    return lax.ppermute(pair, "row", swaps[0]), lax.ppermute(other, "row", swaps[1])


def beside_columns(near, after):
    axes = ("hi", "core")
    count = lax.axis_size("hi") * lax.axis_size("core")
    pairs = [(i, i + 1) for i in range(1, count - 1, 2)]
    swap = pairs + [(j, i) for i, j in pairs]
    return sibling(near), lax.ppermute(after, axes, swap)


def across(values):
    return lax.all_to_all(values, ("row", "hi"), split_axis=0, concat_axis=0, tiled=True)


def sibling(values):
    return lax.ppermute(values, "core", [(0, 1), (1, 0)])


def shards(
    x_input,
    grad_output,
    in_scale,
    in_shift,
    w_expand,
    dw_kernel,
    w_project,
    gain_block,
    w_qkv_block,
    w_out_block,
    bias_block,
    gain_grid,
    w_qkv_grid,
    w_out_grid,
    bias_grid,
):
    core_flag = lax.axis_index("core").reshape(1).astype(jnp.int32)
    scale = in_scale.reshape(1, D)
    shift = in_shift.reshape(1, D)
    gain_block = gain_block.reshape(1, D)
    gain_grid = gain_grid.reshape(1, D)
    hidden = shape((BLOCKS, TOKENS, 128), BF16)
    hidden_mid = shape((BLOCKS, 6 * COLS, 128), BF16)
    hidden_edge = shape((BLOCKS, 2 * COLS, 128), BF16)
    hidden_vmem = pltpu.VMEM(hidden.shape, BF16)
    mid_vmem = pltpu.VMEM(hidden_mid.shape, BF16)
    edge_vmem = pltpu.VMEM(hidden_edge.shape, BF16)
    pad_inner = pltpu.VMEM((BLOCKS, ROWS, WIDE, 128), F32)
    pad_edge = pltpu.VMEM((BLOCKS, 6, WIDE, 128), F32)
    tile = shape((ROWS, COLS, D), BF16)
    tokens = shape((TOKENS, D), BF16)
    tokens_vmem = pltpu.VMEM((TOKENS, D), BF16)
    edge_row = shape((144, D), BF16)
    edge_column = shape((ROWS, D), BF16)
    dma = pltpu.SemaphoreType.DMA

    x_input, w_expand, x_left, x_right = call(
        load_kernel,
        [x_input, w_expand],
        [tile, shape((D, E), BF16), edge_column, edge_column],
        [dma((2,)), pltpu.VMEM((2, ROWS, D), F32)],
        far=(0, 1),
        keep=range(4),
        limit=4,
    )
    x_left, x_right = beside_columns(x_left, x_right)
    later = [
        dw_kernel,
        grad_output,
        w_project,
        w_qkv_block,
        w_out_block,
        w_qkv_grid,
        w_out_grid,
    ]
    (
        lifted_far,
        slope_pre,
        lifted,
        dw_kernel,
        grad_output,
        w_project,
        w_qkv_block,
        w_out_block,
        w_qkv_grid,
        w_out_grid,
    ) = call(
        expand_kernel,
        [x_input, scale, shift, w_expand] + later,
        [hidden, hidden, hidden] + [shape(v.shape, v.dtype) for v in later],
        [hidden_vmem, dma((ROWS, 2)), dma((len(later),))],
        far=range(4, 4 + len(later)),
        far_out=(0, 1),
        keep=range(2, 3 + len(later)),
        limit=8,
        flops=4 * 10**9,
    )
    x_first, x_last = call(
        x_edge_kernel,
        [x_input, x_left, x_right],
        [edge_row, edge_row],
        [],
        keep=(0, 1),
        limit=4,
    )
    x_top, x_bottom = beside_rows(x_first, x_last)
    second_mid_far, second_mid, slope_mid, side_lifted = call(
        inner_rows_kernel,
        [lifted, x_left, x_right, scale, shift, w_expand, dw_kernel],
        [hidden_mid, hidden_mid, hidden_mid, shape((BLOCKS, 16, 128), F32)],
        [pad_inner, mid_vmem, dma((BLOCKS, 2))],
        far_out=(0, 2),
        keep=(1, 3),
        limit=12,
        flops=4 * 10**9,
    )
    cube = shape((2, 64, 256), F32)
    cube_block, cube_grid = call(
        bias_kernel,
        [bias_block, bias_grid],
        [cube, cube],
        [pltpu.VMEM((2 * HEADS, 256), F32)],
        keep=(0, 1),
        limit=8,
    )
    (
        second_edge_far,
        slope_edge,
        section_one,
        section_two,
        sendable,
        normed_block,
        joined,
        probs,
        mixture,
    ) = call(
        front_kernel,
        [
            x_input,
            x_top,
            x_bottom,
            lifted,
            side_lifted,
            second_mid,
            scale,
            shift,
            w_expand,
            dw_kernel,
            w_project,
            gain_block,
            w_qkv_block,
            w_out_block,
            cube_block,
            gain_grid,
            grad_output,
        ],
        [
            hidden_edge,
            hidden_edge,
            tile,
            tile,
            shape((64, 32, D), BF16),
            tokens,
            shape((TOKENS, 3 * D), BF16),
            shape((32, 64, 256), F32),
            tokens,
        ],
        [
            pad_edge,
            pltpu.VMEM((ROWS, COLS, D), F32),
            pltpu.VMEM((ROWS, COLS, D), F32),
            edge_vmem,
            edge_vmem,
            pltpu.VMEM(tile.shape, BF16),
            pltpu.VMEM(tile.shape, BF16),
            tokens_vmem,
            pltpu.VMEM((TOKENS, 3 * D), BF16),
            pltpu.VMEM((32, 64, 256), F32),
            tokens_vmem,
            dma((3,)),
            dma((4, 5)),
        ],
        keep=(4,),
        far_out=(0, 1, 2, 3, 5, 6, 7, 8),
        limit=20,
    )

    got = across(sendable)
    grad_groups, grid_total = call(
        grid_kernel,
        [got, w_qkv_grid, w_out_grid, cube_grid],
        [tokens, shape((2048, 128), F32)],
        [
            tokens_vmem,
            pltpu.VMEM((TOKENS, 3 * D), BF16),
            pltpu.VMEM((2, TOKENS, D), BF16),
        ],
        keep=(0, 1),
        limit=8,
    )
    returned = across(grad_groups.reshape(16, 64, D).transpose(1, 0, 2)).reshape(ROWS, COLS, D)

    half_tile = shape((ROWS, COLS // 2, D), BF16)
    half_inner = shape((BLOCKS, ROWS, COLS // 2, 128), BF16)
    block_total = shape((2048, 128), F32)
    half_read = [
        half_tile,
        shape((TOKENS // 2, 3 * D), BF16),
        shape((16, 64, 256), F32),
        half_tile,
        half_inner,
        shape((TOKENS // 2, D), BF16),
        shape((TOKENS // 2, D), BF16),
    ]
    half_scratch = [pltpu.VMEM(o.shape, o.dtype) for o in half_read]
    weights = [gain_grid, gain_block, w_qkv_block, w_out_block, w_project]
    one_outer, inner_outer, first_total, near, after, *ahead = call(
        functools.partial(block_kernel, (0, 3)),
        [
            returned,
            grad_output,
            section_two,
            joined,
            probs,
            section_one,
            slope_mid.reshape(BLOCKS, 6, COLS, 128),
            slope_edge.reshape(BLOCKS, 2, COLS, 128),
            normed_block,
            mixture,
            *weights,
        ],
        [half_tile, half_inner, block_total]
        + [shape((BLOCKS, ROWS, 128), BF16)] * 2
        + half_read,
        [pltpu.VMEM((2, BLOCKS, ROWS, 128), F32), half_scratch[0]]
        + half_scratch
        + [dma((3,)), dma((36,))],
        far=range(2, 10),
        far_out=(0,),
        keep=range(1, 12),
        limit=12,
        flops=4 * 10**9,
    )
    left, right = beside_columns(near, after)
    one_middle, inner_middle, block_total = call(
        functools.partial(block_kernel, (1, 2)),
        [returned, grad_output, *ahead, ahead[0], *weights, first_total],
        [half_tile, half_inner, block_total],
        [pltpu.VMEM((2048, 128), F32), half_scratch[0], dma((3,))],
        far_out=(0, 2),
        keep=(1,),
        limit=10,
        flops=4 * 10**9,
    )
    edge_cells = shape((BLOCKS, 144, 128), BF16)
    first, last = call(
        inner_edge_kernel,
        [inner_outer, inner_middle, left, right],
        [edge_cells, edge_cells],
        [],
        keep=(0, 1),
        limit=4,
    )
    top, bottom = beside_rows(first, last)
    early = shape((3072, 128), BF16)
    grad_one, early_send, early_keep = call(
        total_kernel,
        [
            core_flag,
            one_outer,
            one_middle,
            second_mid_far,
            second_edge_far,
            block_total,
            grid_total,
            first,
        ],
        [tile, early, early],
        [pltpu.VMEM((6144, 128), F32), hidden_vmem, dma((8,))],
        smem=(0,),
        far=range(1, 7),
        keep=range(3),
        limit=8,
        flops=3 * 10**9,
    )
    preact_mid, taps_mid = call(
        back_inner_kernel,
        [lifted_far, slope_pre, inner_outer, inner_middle, left, right, dw_kernel],
        [hidden_mid, shape((9, BLOCKS, 128), F32)],
        [pad_inner, mid_vmem, mid_vmem, dma((BLOCKS, 2))],
        far=(0, 1),
        keep=(0, 1),
        limit=12,
        flops=4 * 10**9,
    )
    early_got = sibling(early_send)
    late = shape((CHUNKS, 24, 128), BF16)
    parts = shape((CHUNKS, CHUNK, 128), BF16)
    preact_edge, late_send, late_keep = call(
        back_kernel,
        [
            core_flag,
            x_input,
            lifted_far,
            slope_pre,
            inner_outer,
            inner_middle,
            top,
            bottom,
            left,
            right,
            scale,
            shift,
            dw_kernel,
            preact_mid,
            taps_mid,
            early_keep,
        ],
        [hidden_edge, late, late],
        [
            pad_edge,
            edge_vmem,
            edge_vmem,
            tokens_vmem,
            pltpu.VMEM((2048, 128), F32),
            pltpu.VMEM((9, BLOCKS, 128), F32),
            dma((4,)),
        ],
        smem=(0,),
        far=(2, 3),
        keep=(0, 1, 2),
        limit=12,
        flops=4 * 10**9,
    )
    (grad_input,) = call(
        input_kernel, [preact_mid, preact_edge, grad_one, w_expand, scale], [tile], [], limit=8
    )

    (paired,) = call(
        pair_kernel,
        [early_keep, early_got, late_keep, sibling(late_send), grad_input],
        [parts],
        [],
        far=(4,),
        keep=(0,),
        limit=4,
    )
    (summed,) = call(sum_kernel, [across(paired)], [parts], [], keep=(0,), limit=4)
    mine = across(summed)
    sums = [
        shape((D, E), F32),
        shape((9, E), F32),
        shape((E, D), F32),
        shape((D, 3 * D), F32),
        shape((D, D), F32),
        shape((D, 3 * D), F32),
        shape((D, D), F32),
    ]
    done = call(
        mine_kernel,
        [core_flag, mine],
        sums,
        [],
        smem=(0,),
        keep=range(7),
        limit=4,
        flops=2 * 10**9,
    )
    totals = call(
        other_kernel,
        [core_flag, sibling(mine), *done],
        sums,
        [pltpu.VMEM(o.shape, F32) for o in sums] + [dma((10,))],
        smem=(0,),
        far_out=range(7),
        limit=10,
    )
    return (grad_input, *totals)


def solution(mesh):
    split = Mesh(mesh.devices.reshape(8, 8, 2), ("row", "hi", "core"))
    tile = P("row", ("hi", "core"), None)
    return jax.shard_map(
        shards,
        mesh=split,
        in_specs=(tile, tile) + (P(),) * 13,
        out_specs=(tile,) + (P(),) * 7,
        check_vma=False,
    )
```

```python
import functools

import jax
import jax.numpy as jnp
from jax import lax
from jax.experimental import pallas as pl
from jax.experimental.pallas import tpu as pltpu
from jax.sharding import Mesh
from jax.sharding import PartitionSpec as P

F32 = jnp.float32
BF16 = jnp.bfloat16
EPSILON = 1e-05
HEADS = 8
HEAD = 32
SCALE = HEAD ** (-0.5)
ROWS = 8
COLS = 128
TOKENS = ROWS * COLS
D = 256
E = 1024
BLOCKS = E // 128
LEFT = 8
WIDE = COLS + 2 * LEFT
GELU_1 = 0.7978845608028654
GELU_3 = 0.044715 * GELU_1


def dot(left, right, left_dim, right_dim):
    return lax.dot_general(
        left, right, (((left_dim,), (right_dim,)), ((), ())), preferred_element_type=F32
    )


def gelu_pair(values):
    square = values * values
    half = 0.5 + 0.5 * jnp.tanh(values * (GELU_1 + GELU_3 * square))
    value = values * half
    slope = half + value * (1.0 - half) * (2.0 * GELU_1 + (6.0 * GELU_3) * square)
    return value, slope


def norm_parts(values):
    centered = values - jnp.mean(values, axis=-1, keepdims=True)
    spread = jnp.mean(centered * centered, axis=-1, keepdims=True)
    inverse = lax.rsqrt(spread + EPSILON)
    return centered * inverse, inverse


def norm_back(values, gain, grad):
    unit, inverse = norm_parts(values)
    scaled = grad * gain
    mean_grad = jnp.mean(scaled, axis=-1, keepdims=True)
    mean_unit = jnp.mean(scaled * unit, axis=-1, keepdims=True)
    return inverse * (scaled - mean_grad - unit * mean_unit)


def four_windows(cells):
    return jnp.concatenate(
        [cells[:, 8 * m : 8 * m + 8, :].reshape(64, D) for m in range(4)], axis=0
    )


def from_four_windows(tokens):
    return jnp.concatenate(
        [tokens[64 * m : 64 * m + 64].reshape(8, 8, D) for m in range(4)], axis=1
    )


def load_kernel(x_in, w_expand_in, x_ref, w_expand_ref, near_ref, next_ref, sems, ends):
    copies = copy_all(((x_in, x_ref), (w_expand_in, w_expand_ref)), sems)
    copies[0].wait()
    for row in range(ROWS):
        ends[0, row : row + 1, :] = x_ref[row, 0:16, :].astype(F32)[0:1]
        ends[1, row : row + 1, :] = x_ref[row, COLS - 16 : COLS, :].astype(F32)[15:16]
    near, after = trade(ends[1], ends[0])
    near_ref[...] = near.astype(BF16)
    next_ref[...] = after.astype(BF16)
    copies[1].wait()


def with_corners(cells, left, right):
    rest = jnp.zeros((14, cells.shape[1]), F32)
    corners = jnp.concatenate([left, right, rest], axis=0).astype(BF16)
    return jnp.concatenate([cells, corners], axis=0)


def x_edge_kernel(x_ref, near_ref, next_ref, pair_ref, other_ref):
    right, left = trade(near_ref[...], next_ref[...])
    even = even_row()
    for last, target in ((even, pair_ref), (1 - even, other_ref)):
        target[...] = with_corners(x_ref[7 * last], edge_of(last, left), edge_of(last, right))


def inner_edge_kernel(outer_ref, middle_ref, near_ref, next_ref, pair_ref, other_ref):
    even = even_row()
    for block in range(BLOCKS):
        right, left = trade(near_ref[block], next_ref[block])
        for last, target in ((even, pair_ref), (1 - even, other_ref)):
            cells = whole_row(outer_ref[block, 7 * last], middle_ref[block, 7 * last])
            target[block] = with_corners(cells, edge_of(last, left), edge_of(last, right))


def whole_row(outer, middle):
    axis = outer.ndim - 2
    first = lax.slice_in_dim(outer, 0, 32, axis=axis)
    last = lax.slice_in_dim(outer, 32, 64, axis=axis)
    return jnp.concatenate([first, middle, last], axis=axis)


def bias_kernel(block_ref, grid_ref, bias_block_ref, bias_grid_ref, table):
    source = lax.broadcasted_iota(jnp.int32, (256, 1024), 0)
    place = lax.broadcasted_iota(jnp.int32, (256, 1024), 1)
    wanted = 15 * (place % 128 // 8) + 7 + place % 8 - place // 128
    onehot = jnp.where(source == wanted, 1.0, 0.0).astype(BF16)
    table[...] = jnp.zeros((2 * HEADS, 256), F32)
    table[0:HEADS, 0:225] = block_ref[...]
    table[HEADS : 2 * HEADS, 0:225] = grid_ref[...]
    rest = table[...]
    spread = jnp.zeros((2 * HEADS, 1024), F32)
    for _ in range(3):
        part = rest.astype(BF16)
        spread = spread + dot(part, onehot, 1, 0)
        rest = rest - part.astype(F32)
    for which, bias_ref in enumerate((bias_block_ref, bias_grid_ref)):
        for head in range(HEADS):
            line = HEADS * which + head
            rows = jnp.concatenate(
                [spread[line : line + 1, 128 * e : 128 * e + 128] for e in range(8)], axis=0
            )
            for a_k in range(8):
                start = 8 * (7 - a_k)
                bias_ref[
                    head // 4, 8 * a_k : 8 * a_k + 8, 64 * (head % 4) : 64 * (head % 4) + 64
                ] = rows[:, start : start + 64]


def stacked(part, heads_mask):
    return jnp.concatenate([part] * 4, axis=0) * heads_mask


def pick(product):
    lane = lax.broadcasted_iota(jnp.int32, (64, 128), 1)
    low = jnp.where(lane < 32, product[0:64], product[64:128])
    high = jnp.where(lane < 96, product[128:192], product[192:256])
    return jnp.where(lane < 64, low, high)


def softmax_keys(scores):
    shifted = jnp.exp(scores - jnp.max(scores, axis=0, keepdims=True))
    return shifted * (1.0 / jnp.sum(shifted, axis=0, keepdims=True))


def half_of(joined, part, half, group):
    start = part * D + half * 128
    return joined[64 * group : 64 * group + 64, start : start + 128]


PAIRS = [(group, half) for group in range(4) for half in range(2)]


def quarter(parts):
    return jnp.concatenate(
        [jnp.concatenate(parts[2 * g : 2 * g + 2], axis=1) for g in range(4)], axis=0
    )


def attend(joined, bias_ref, heads_mask):
    scores = [
        dot(half_of(joined, 1, h, g), stacked(half_of(joined, 0, h, g), heads_mask), 1, 1)
        for g, h in PAIRS
    ]
    probs = [softmax_keys(s * SCALE + bias_ref[h]) for s, (_, h) in zip(scores, PAIRS)]
    products = [dot(p.astype(BF16), half_of(joined, 2, h, g), 0, 0) for p, (g, h) in zip(probs, PAIRS)]
    return probs, quarter([pick(p).astype(BF16) for p in products])


def attend_back(joined, probs, grad_mix, heads_mask):
    stacks = [stacked(half_of(grad_mix, 0, h, g), heads_mask) for g, h in PAIRS]
    grad_weights = [
        dot(half_of(joined, 2, h, g), stack, 1, 1).astype(BF16).astype(F32)
        for stack, (g, h) in zip(stacks, PAIRS)
    ]
    grad_values = [dot(p.astype(BF16), stack, 1, 0) for p, stack in zip(probs, stacks)]
    grad_scores = []
    for p, w in zip(probs, grad_weights):
        centre = jnp.sum(w * p, axis=0, keepdims=True)
        grad_scores.append((p * (w - centre) * SCALE).astype(BF16))
    grad_keys = [
        dot(s, stacked(half_of(joined, 0, h, g), heads_mask), 1, 0)
        for s, (g, h) in zip(grad_scores, PAIRS)
    ]
    grad_queries = [
        pick(dot(s, half_of(joined, 1, h, g), 0, 0)) for s, (g, h) in zip(grad_scores, PAIRS)
    ]
    return jnp.concatenate(
        [quarter(grad_queries), quarter(grad_keys), quarter(grad_values)], axis=1
    ).astype(BF16)


def heads_mask_of():
    row = lax.broadcasted_iota(jnp.int32, (256, 128), 0) // 64
    lane = lax.broadcasted_iota(jnp.int32, (256, 128), 1) // HEAD
    return jnp.where(row == lane, 1.0, 0.0).astype(BF16)


def attention_totals(total_ref, normed_ref, grad_joined_ref, mixture_ref, grad_ref):
    for part in range(3):
        total = dot(normed_ref[...], grad_joined_ref[:, D * part : D * part + D], 0, 0)
        for k in range(2):
            start = 256 * (2 * part + k)
            total_ref[start : start + 256, :] = total[:, 128 * k : 128 * k + 128].astype(BF16)
    total = dot(mixture_ref[...], grad_ref[...], 0, 0)
    for k in range(2):
        total_ref[1536 + 256 * k : 1792 + 256 * k, :] = total[:, 128 * k : 128 * k + 128].astype(BF16)


def edge_flags():
    row_index = lax.axis_index("row")
    col_index = 2 * lax.axis_index("hi") + lax.axis_index("core")
    flags = (row_index > 0, row_index < 7, col_index > 0, col_index < 15)
    return [jnp.where(flag, 1.0, 0.0).astype(F32) for flag in flags]


def shift_scale(tokens, scale_ref, shift_ref):
    return (tokens.astype(F32) * scale_ref[...] + shift_ref[...]).astype(BF16)


def trade(first, second):
    here = jnp.where(lax.axis_index("core") == 0, 1.0, 0.0).astype(F32)
    first, second = first.astype(F32), second.astype(F32)
    there = 1.0 - here
    return first * here + second * there, first * there + second * here


def even_row():
    return 1 - lax.rem(lax.axis_index("row"), 2)


def edge_of(even, value):
    last = even.astype(F32)
    return value[7:8] * last + value[0:1] * (1.0 - last)


def copy_all(pairs, sems, first=0):
    copies = [
        pltpu.make_async_copy(source, target, sems.at[first + k])
        for k, (source, target) in enumerate(pairs)
    ]
    for copy in copies:
        copy.start()
    return copies


def wait_all(copies):
    for copy in copies:
        copy.wait()


def expand_kernel(
    x_ref,
    scale_ref,
    shift_ref,
    w_expand_ref,
    *refs,
):
    count = (len(refs) - 6) // 2
    sources, (lifted_out, slope_pre_out, lifted_ref) = refs[:count], refs[count : count + 3]
    targets, (slope_pre_ref, sems, load_sems) = refs[count + 3 : -3], refs[-3:]
    loads = copy_all(list(zip(sources, targets)), load_sems)

    def stores(row):
        here = pl.ds(row * COLS, COLS)
        return [
            pltpu.make_async_copy(source.at[:, here, :], target.at[:, here, :], sems.at[row, k])
            for k, (source, target) in enumerate(
                ((lifted_ref, lifted_out), (slope_pre_ref, slope_pre_out))
            )
        ]

    for row in range(ROWS):
        here = pl.ds(row * COLS, COLS)
        shifted = shift_scale(x_ref[row], scale_ref, shift_ref)
        for pair in range(4):
            value, slope = gelu_pair(
                dot(shifted, w_expand_ref[:, 256 * pair : 256 * pair + 256], 1, 0)
            )
            value = value.astype(BF16)
            slope = slope.astype(BF16)
            for k in range(2):
                lanes = slice(128 * k, 128 * k + 128)
                lifted_ref[2 * pair + k, here, :] = value[:, lanes]
                slope_pre_ref[2 * pair + k, here, :] = slope[:, lanes]
        for copy in stores(row):
            copy.start()

    wait_all(loads)
    for row in range(ROWS):
        wait_all(stores(row))


def convolve_rows(pad, block, pad_row, taps, second_ref, slope_conv_ref, row):
    for chunk in range(4):
        summed = None
        for t in range(9):
            start = LEFT - 1 + t % 3 + 32 * chunk
            term = taps[t] * pad[block, pad_row + t // 3, start : start + 32, :]
            summed = term if summed is None else summed + term
        value, slope = gelu_pair(summed)
        here = pl.ds(pl.multiple_of(row * COLS + 32 * chunk, 32), 32)
        second_ref[block, here, :] = value.astype(BF16)
        slope_conv_ref[block, here, :] = slope.astype(BF16)


def taps_of(dw_ref, block):
    lanes = pl.ds(pl.multiple_of(block * 128, 128), 128)
    return [dw_ref[t : t + 1, lanes] for t in range(9)]


def inner_rows_kernel(
    lifted_ref,
    near_ref,
    next_ref,
    scale_ref,
    shift_ref,
    w_expand_ref,
    dw_ref,
    second_out,
    second_ref,
    slope_conv_out,
    side_ref,
    pad,
    slope_conv_ref,
    sems,
):
    def stores(block):
        return [
            pltpu.make_async_copy(source.at[block], target.at[block], sems.at[block, k])
            for k, (source, target) in enumerate(
                ((second_ref, second_out), (slope_conv_ref, slope_conv_out))
            )
        ]

    inside = edge_flags()
    right, left = trade(near_ref[...], next_ref[...])
    sides = jnp.concatenate([left, right], axis=0)
    shifted = shift_scale(sides, scale_ref, shift_ref)
    place = lax.broadcasted_iota(jnp.int32, (16, 1), 0)
    flags = jnp.where(place < 8, inside[2], inside[3])
    for pair in range(4):
        value, _ = gelu_pair(dot(shifted, w_expand_ref[:, 256 * pair : 256 * pair + 256], 1, 0))
        value = value.astype(BF16).astype(F32) * flags
        for k in range(2):
            side_ref[2 * pair + k] = value[:, 128 * k : 128 * k + 128]

    @pl.loop(0, BLOCKS)
    def _(block):
        taps = taps_of(dw_ref, block)
        side = side_ref[block]
        for row in range(ROWS):
            pad[block, row, LEFT : LEFT + COLS, :] = lifted_ref[
                block, COLS * row : COLS * row + COLS, :
            ].astype(F32)
            pad[block, row, LEFT - 1 : LEFT, :] = side[row : row + 1]
            pad[block, row, LEFT + COLS : LEFT + COLS + 1, :] = side[8 + row : 9 + row]

        for row in range(ROWS - 2):
            convolve_rows(pad, block, row, taps, second_ref, slope_conv_ref, row)

        for copy in stores(block):
            copy.start()

    for block in range(BLOCKS):
        wait_all(stores(block))


def front_kernel(
    x_ref,
    pair_ref,
    other_ref,
    lifted_ref,
    side_ref,
    second_mid_ref,
    scale_ref,
    shift_ref,
    w_expand_ref,
    dw_ref,
    w_project_ref,
    gain_block_ref,
    w_qkv_ref,
    w_out_ref,
    bias,
    gain_grid_ref,
    grad_output_ref,
    second_out,
    slope_edge_out,
    section_one_out,
    section_two_out,
    send_ref,
    normed_block_out,
    joined_out,
    probs_out,
    mixture_out,
    pad,
    cells,
    outcome,
    second_ref,
    slope_edge_ref,
    section_one_ref,
    section_two_ref,
    normed_block_ref,
    joined_ref,
    probs_ref,
    mixture_ref,
    sems,
    part_sems,
):
    send_ref[:, 16:32, :] = grad_output_ref[...].reshape(64, 16, D)
    heads_mask = heads_mask_of()
    inside = edge_flags()
    even = even_row()
    for source, below in ((pair_ref, even), (other_ref, 1 - even)):
        row = 5 * below
        flag = inside[1] * below.astype(F32) + inside[0] * (1 - below).astype(F32)
        shifted = shift_scale(source[...], scale_ref, shift_ref)
        for pair in range(4):
            value, _ = gelu_pair(dot(shifted, w_expand_ref[:, 256 * pair : 256 * pair + 256], 1, 0))
            value = value.astype(BF16).astype(F32) * flag
            for k in range(2):
                block = 2 * pair + k
                part = value[:, 128 * k : 128 * k + 128]
                pad[block, row, LEFT : LEFT + COLS, :] = part[:COLS]
                pad[block, row, LEFT - 1 : LEFT, :] = part[COLS : COLS + 1] * inside[2]
                pad[block, row, LEFT + COLS : LEFT + COLS + 1, :] = (
                    part[COLS + 1 : COLS + 2] * inside[3]
                )

    @pl.loop(0, BLOCKS)
    def _(block):
        taps = taps_of(dw_ref, block)
        side = side_ref[block]
        for row, place in ((0, 1), (1, 2), (6, 3), (7, 4)):
            pad[block, place, LEFT : LEFT + COLS, :] = lifted_ref[
                block, COLS * row : COLS * row + COLS, :
            ].astype(F32)
            pad[block, place, LEFT - 1 : LEFT, :] = side[row : row + 1]
            pad[block, place, LEFT + COLS : LEFT + COLS + 1, :] = side[8 + row : 9 + row]
        for row in range(2):
            convolve_rows(pad, block, 3 * row, taps, second_ref, slope_edge_ref, row)

    stores = copy_all(((second_ref, second_out), (slope_edge_ref, slope_edge_out)), sems)
    for part in range(4):
        rows = slice(2 * part, 2 * part + 2)
        summed = x_ref[rows].reshape(256, D).astype(F32)
        for pair in range(4):
            pieces = []
            for block in (2 * pair, 2 * pair + 1):
                pieces.append(
                    jnp.concatenate(
                        [
                            second_ref[block, COLS * (row // 7) : COLS * (row // 7) + COLS, :]
                            if row in (0, 7)
                            else second_mid_ref[block, COLS * (row - 1) : COLS * row, :]
                            for row in (2 * part, 2 * part + 1)
                        ],
                        axis=0,
                    )
                )
            summed = summed + dot(
                jnp.concatenate(pieces, axis=1), w_project_ref[256 * pair : 256 * pair + 256, :], 1, 0
            )
        section_one = summed.astype(BF16)
        section_one_ref[rows] = section_one.reshape(2, COLS, D)
        cells[rows] = section_one.astype(F32).reshape(2, COLS, D)

    stores += copy_all([(section_one_ref, section_one_out)], sems, first=2)

    def part_stores(part):
        here = pl.ds(part * 256, 256)
        columns = pl.ds(part * 32, 32)
        eight = pl.ds(part * 8, 8)
        return [
            pltpu.make_async_copy(source, target, part_sems.at[part, k])
            for k, (source, target) in enumerate(
                (
                    (normed_block_ref.at[here, :], normed_block_out.at[here, :]),
                    (joined_ref.at[here, :], joined_out.at[here, :]),
                    (mixture_ref.at[here, :], mixture_out.at[here, :]),
                    (probs_ref.at[eight], probs_out.at[eight]),
                    (section_two_ref.at[:, columns, :], section_two_out.at[:, columns, :]),
                )
            )
        ]

    for part in range(4):
        here = slice(256 * part, 256 * part + 256)
        columns = slice(32 * part, 32 * part + 32)
        section_one = four_windows(cells[:, columns, :])
        normed = (norm_parts(section_one)[0] * gain_block_ref[...]).astype(BF16)
        normed_block_ref[here, :] = normed
        joined = dot(normed, w_qkv_ref[...], 1, 0).astype(BF16)
        joined_ref[here, :] = joined
        probs, mixture = attend(joined, bias, heads_mask)
        for index in range(8):
            probs_ref[part * 8 + index] = probs[index]
        mixture_ref[here, :] = mixture
        section_two = (section_one + dot(mixture, w_out_ref[...], 1, 0)).astype(BF16).astype(F32)
        section_two_ref[:, columns, :] = from_four_windows(section_two).astype(BF16)
        for copy in part_stores(part):
            copy.start()
        normed = norm_parts(section_two)[0] * gain_grid_ref[...]
        outcome[:, columns, :] = from_four_windows(normed)

    send_ref[:, 0:16, :] = outcome[...].astype(BF16).reshape(64, 16, D)
    wait_all(stores)
    for part in range(4):
        wait_all(part_stores(part))


def grid_kernel(
    got_ref,
    w_qkv_ref,
    w_out_ref,
    bias,
    grad_normed_ref,
    total_ref,
    mixture_ref,
    grad_joined_ref,
    groups_ref,
    ordered,
):
    heads_mask = heads_mask_of()
    for index in range(2):
        for part in range(4):
            cells = got_ref[:, 16 * index + 4 * part : 16 * index + 4 * part + 4, :].astype(F32)
            groups_ref[index, 256 * part : 256 * part + 256, :] = (
                cells.transpose(1, 0, 2).reshape(256, D).astype(BF16)
            )
    normed_ref = groups_ref.at[0]
    grad_ref = groups_ref.at[1]

    for part in range(4):
        here = slice(256 * part, 256 * part + 256)
        joined = dot(normed_ref[here, :], w_qkv_ref[...], 1, 0).astype(BF16)
        grad_mix = dot(grad_ref[here, :], w_out_ref[...], 1, 1).astype(BF16)
        probs, mixture = attend(joined, bias, heads_mask)
        mixture_ref[here, :] = mixture
        grad_joined = attend_back(joined, probs, grad_mix, heads_mask)
        grad_joined_ref[here, :] = grad_joined
        grad_normed = dot(grad_joined, w_qkv_ref[...], 1, 1).reshape(4, 64, D)
        ordered[:, 4 * part : 4 * part + 4, :] = grad_normed.transpose(1, 0, 2)

    attention_totals(total_ref, normed_ref, grad_joined_ref, mixture_ref, grad_ref)
    grad_normed_ref[...] = ordered[...].astype(BF16)


def quarter_fetches(far, near, parts, sems, first):
    section_two, joined, probs, section_one, slope_mid, slope_edge, normed_block, mixture = far
    two_ref, joined_ref, probs_ref, one_ref, slope_ref, normed_ref, mixture_ref = near
    fetches = []
    for index, part in enumerate(parts):
        here, columns = pl.ds(256 * part, 256), pl.ds(32 * part, 32)
        goal, to = pl.ds(256 * index, 256), pl.ds(32 * index, 32)
        pairs = (
            (section_two.at[:, columns, :], two_ref.at[:, to, :]),
            (joined.at[here, :], joined_ref.at[goal, :]),
            (probs.at[pl.ds(8 * part, 8)], probs_ref.at[pl.ds(8 * index, 8)]),
            (section_one.at[:, columns, :], one_ref.at[:, to, :]),
            (slope_mid.at[:, :, columns, :], slope_ref.at[:, pl.ds(1, 6), to, :]),
            (slope_edge.at[:, pl.ds(0, 1), columns, :], slope_ref.at[:, pl.ds(0, 1), to, :]),
            (slope_edge.at[:, pl.ds(1, 1), columns, :], slope_ref.at[:, pl.ds(7, 1), to, :]),
            (normed_block.at[here, :], normed_ref.at[goal, :]),
            (mixture.at[here, :], mixture_ref.at[goal, :]),
        )
        fetches.append(
            [
                pltpu.make_async_copy(source, target, sems.at[first + 9 * index + k])
                for k, (source, target) in enumerate(pairs)
            ]
        )
    return fetches


def block_kernel(
    parts,
    returned_ref,
    grad_output_ref,
    section_two_in,
    joined_in,
    probs_in,
    section_one_in,
    slope_mid_in,
    slope_edge_in,
    normed_block_in,
    mixture_in,
    gain_grid_ref,
    gain_block_ref,
    w_qkv_ref,
    w_out_ref,
    w_project_ref,
    *rest,
):
    far = (
        section_two_in,
        joined_in,
        probs_in,
        section_one_in,
        slope_mid_in,
        slope_edge_in,
        normed_block_in,
        mixture_in,
    )
    stores = []
    ahead = []
    if parts[0] == 0:
        before_ref = None
        grad_one_out, inner_ref, total_ref, near_ref, next_ref = rest[:5]
        ahead_refs, (ends, grad_one_ref), near_refs = rest[5:12], rest[12:14], rest[14:21]
        sems, fetch_sems = rest[21:]
        fetches = quarter_fetches(far, near_refs, parts, fetch_sems, 0)
        ahead = quarter_fetches(far, ahead_refs, (1, 2), fetch_sems, 18)
        for copy in fetches[0][:3]:
            copy.start()
    else:
        before_ref, grad_one_out, inner_ref, total_out, total_ref, grad_one_ref, sems = rest
        near_refs = far[:7]
        fetches = [[], []]
    (
        section_two_ref,
        joined_ref,
        probs_ref,
        section_one_ref,
        slope_ref,
        normed_block_ref,
        mixture_ref,
    ) = near_refs
    heads_mask = heads_mask_of()
    all_windows = []
    all_joined = []
    for index, part in enumerate(parts):
        here = slice(256 * index, 256 * index + 256)
        columns = slice(32 * part, 32 * part + 32)
        out_columns = slice(32 * index, 32 * index + 32)

        def windows_of(ref, columns):
            return four_windows(ref[:, columns, :].astype(F32))

        wait_all(fetches[index][:1])
        if index == 0:
            for copy in fetches[0][3:] + fetches[1] + sum(ahead, []):
                copy.start()
        grad_two = windows_of(grad_output_ref, columns) + norm_back(
            windows_of(section_two_ref, out_columns),
            gain_grid_ref[...],
            windows_of(returned_ref, columns),
        )
        grad_windows = grad_two.astype(BF16)
        grad_two = grad_windows.astype(F32)
        grad_mix = dot(grad_windows, w_out_ref[...], 1, 1).astype(BF16)
        wait_all(fetches[index][1:3])
        joined = joined_ref[here, :]
        probs = [probs_ref[index * 8 + k] for k in range(8)]
        grad_joined = attend_back(joined, probs, grad_mix, heads_mask)
        all_windows.append(grad_windows)
        all_joined.append(grad_joined)
        grad_normed = dot(grad_joined, w_qkv_ref[...], 1, 1).astype(BF16).astype(F32)
        wait_all(fetches[index][3:4])
        grad_one = grad_two + norm_back(
            windows_of(section_one_ref, out_columns), gain_block_ref[...], grad_normed
        )
        grad_one_ref[:, out_columns, :] = from_four_windows(grad_one).astype(BF16)
        stores += copy_all(
            [(grad_one_ref.at[:, out_columns, :], grad_one_out.at[:, out_columns, :])],
            sems,
            first=index,
        )
    for index in range(2):
        wait_all(fetches[index][7:])
    joined = jnp.concatenate(all_joined, axis=0)
    windows = jnp.concatenate(all_windows, axis=0)
    products = [
        (normed_block_ref, joined[:, D * part : D * part + D], 512 * part) for part in range(3)
    ]
    for left, right, start in products + [(mixture_ref, windows, 1536)]:
        total = dot(left[...], right, 0, 0)
        for k in range(2):
            place = slice(start + 256 * k, start + 256 * k + 256)
            value = total[:, 128 * k : 128 * k + 128]
            if before_ref is None:
                total_ref[place, :] = value
            else:
                total_ref[place, :] = (before_ref[place, :] + value).astype(BF16)
    if before_ref is not None:
        stores += copy_all([(total_ref, total_out)], sems, first=2)
    for index, part in enumerate(parts):
        wait_all(fetches[index][4:7])
        out_columns = slice(32 * index, 32 * index + 32)
        grad_one = grad_one_ref[:, out_columns, :].reshape(256, D)
        for pair in range(4):
            through = dot(grad_one, w_project_ref[256 * pair : 256 * pair + 256, :], 1, 1)
            for k in range(2):
                block = 2 * pair + k
                slope = slope_ref[block, :, out_columns, :].astype(F32)
                inner = through[:, 128 * k : 128 * k + 128].reshape(ROWS, 32, 128) * slope
                inner_ref[block, :, out_columns, :] = inner.astype(BF16)
                if before_ref is None:
                    side, column = (0, 0) if part == 0 else (1, 31)
                    for row in range(ROWS):
                        ends[side, block, row : row + 1, :] = inner[row, column : column + 1]
    if before_ref is None:
        near, after = trade(ends[1], ends[0])
        near_ref[...] = near.astype(BF16)
        next_ref[...] = after.astype(BF16)
    wait_all(stores + sum(ahead, []))


def total_kernel(
    core_ref,
    outer_in,
    middle_in,
    second_mid_in,
    second_edge_in,
    block_total_in,
    grid_total_in,
    _,
    grad_one_ref,
    early_send_ref,
    early_keep_ref,
    total_ref,
    second_ref,
    sems,
):
    rows = (pl.ds(0, COLS), pl.ds(COLS, 6 * COLS), pl.ds(7 * COLS, COLS))
    fetches = copy_all(
        (
            (outer_in.at[:, pl.ds(0, 32), :], grad_one_ref.at[:, pl.ds(0, 32), :]),
            (outer_in.at[:, pl.ds(32, 32), :], grad_one_ref.at[:, pl.ds(96, 32), :]),
            (middle_in, grad_one_ref.at[:, pl.ds(32, 64), :]),
            (second_edge_in.at[:, pl.ds(0, COLS), :], second_ref.at[:, rows[0], :]),
            (second_mid_in, second_ref.at[:, rows[1], :]),
            (second_edge_in.at[:, pl.ds(COLS, COLS), :], second_ref.at[:, rows[2], :]),
            (block_total_in, total_ref.at[pl.ds(0, 2048), :]),
            (grid_total_in, total_ref.at[pl.ds(4096, 2048), :]),
        ),
        sems,
    )
    wait_all(fetches[:6])
    grad_one = grad_one_ref[...].reshape(TOKENS, D)
    for pair in range(4):
        joined = jnp.concatenate([second_ref[2 * pair], second_ref[2 * pair + 1]], axis=1)
        total = dot(joined, grad_one, 0, 0)
        for k in range(2):
            start = 2048 + 1024 * k + 256 * pair
            total_ref[start : start + 256, :] = total[:, 128 * k : 128 * k + 128].astype(BF16)
    wait_all(fetches[6:])
    own = pl.ds(pl.multiple_of(core_ref[0] * 3072, 3072), 3072)
    other = pl.ds(pl.multiple_of((1 - core_ref[0]) * 3072, 3072), 3072)
    early_keep_ref[...] = total_ref[own, :]
    early_send_ref[...] = total_ref[other, :]


def back_rows(pad, block, pad_row, taps, lifted_ref, slope_pre_ref, preact_ref, row, totals):
    totals = list(totals)
    for chunk in range(4):
        here = pl.ds(pl.multiple_of(row * COLS + 32 * chunk, 32), 32)
        lifted = lifted_ref[block, here, :].astype(F32)
        summed = None
        for t in range(9):
            start = LEFT + 1 - t % 3 + 32 * chunk
            cells = pad[block, pad_row + 2 - t // 3, start : start + 32, :]
            term = taps[t] * cells
            summed = term if summed is None else summed + term
            totals[t] = totals[t] + jnp.sum((lifted * cells).reshape(4, 8, 128), axis=0)
        grad = summed * slope_pre_ref[block, here, :].astype(F32)
        preact_ref[block, here, :] = grad.astype(BF16)
    return tuple(totals)


def fill_row(pad, block, place, row, outer_ref, middle_ref, left, right):
    cells = whole_row(outer_ref[block, row], middle_ref[block, row])
    pad[block, place, LEFT : LEFT + COLS, :] = cells.astype(F32)
    pad[block, place, LEFT - 1 : LEFT, :] = left[row : row + 1]
    pad[block, place, LEFT + COLS : LEFT + COLS + 1, :] = right[row : row + 1]


def back_inner_kernel(
    lifted_in,
    slope_pre_in,
    outer_ref,
    middle_ref,
    near_ref,
    next_ref,
    dw_ref,
    preact_ref,
    taps_ref,
    pad,
    lifted_ref,
    slope_pre_ref,
    sems,
):
    rows = pl.ds(COLS, 6 * COLS)

    def fetches(block):
        return [
            pltpu.make_async_copy(
                source.at[block, rows, :], target.at[block], sems.at[block, k]
            )
            for k, (source, target) in enumerate(
                ((lifted_in, lifted_ref), (slope_pre_in, slope_pre_ref))
            )
        ]

    for block in range(BLOCKS):
        for copy in fetches(block):
            copy.start()

    @pl.loop(0, BLOCKS)
    def _(block):
        right, left = trade(near_ref[block], next_ref[block])
        for row in range(ROWS):
            fill_row(pad, block, row, row, outer_ref, middle_ref, left, right)
        wait_all(fetches(block))
        taps = taps_of(dw_ref, block)

        def step(row, totals):
            return back_rows(
                pad, block, row, taps, lifted_ref, slope_pre_ref, preact_ref, row, totals
            )

        totals = lax.fori_loop(0, ROWS - 2, step, (jnp.zeros((8, 128), F32),) * 9)
        for t in range(9):
            taps_ref[t, pl.ds(block, 1), :] = jnp.sum(totals[t], axis=0, keepdims=True)


def back_kernel(
    core_ref,
    x_ref,
    lifted_in,
    slope_pre_in,
    outer_ref,
    middle_ref,
    pair_ref,
    other_ref,
    near_ref,
    next_ref,
    scale_ref,
    shift_ref,
    dw_ref,
    preact_mid_ref,
    taps_mid_ref,
    _,
    preact_ref,
    late_send_ref,
    late_keep_ref,
    pad,
    lifted_ref,
    slope_pre_ref,
    shifted_ref,
    total_ref,
    taps_ref,
    sems,
):
    first, last = pl.ds(0, COLS), pl.ds(7 * COLS, COLS)
    second = pl.ds(COLS, COLS)
    fetches = copy_all(
        [
            (source.at[:, rows, :], target.at[:, place, :])
            for source, target in ((lifted_in, lifted_ref), (slope_pre_in, slope_pre_ref))
            for rows, place in ((first, first), (last, second))
        ],
        sems,
    )
    for place, row in enumerate((1, 2, 3, 4, 5, 6, 0, 7)):
        shifted_ref[COLS * place : COLS * place + COLS, :] = shift_scale(
            x_ref[row], scale_ref, shift_ref
        )
    wait_all(fetches)
    even = even_row()

    @pl.loop(0, BLOCKS)
    def _(block):
        right, left = trade(near_ref[block], next_ref[block])
        for source, place in ((pair_ref, 5 * even), (other_ref, 5 - 5 * even)):
            cells = source[block].astype(F32)
            pad[block, place, LEFT : LEFT + COLS, :] = cells[:COLS]
            pad[block, place, LEFT - 1 : LEFT, :] = cells[COLS : COLS + 1]
            pad[block, place, LEFT + COLS : LEFT + COLS + 1, :] = cells[COLS + 1 : COLS + 2]
        for row, place in ((0, 1), (1, 2), (6, 3), (7, 4)):
            fill_row(pad, block, place, row, outer_ref, middle_ref, left, right)
        taps = taps_of(dw_ref, block)
        totals = (jnp.zeros((8, 128), F32),) * 9
        for row in range(2):
            totals = back_rows(
                pad, block, 3 * row, taps, lifted_ref, slope_pre_ref, preact_ref, row, totals
            )
        for t in range(9):
            taps_ref[t, pl.ds(block, 1), :] = taps_mid_ref[t, pl.ds(block, 1), :] + jnp.sum(
                totals[t], axis=0, keepdims=True
            )

    for pair in range(4):
        pieces = [
            jnp.concatenate([preact_mid_ref[block], preact_ref[block]], axis=0)
            for block in (2 * pair, 2 * pair + 1)
        ]
        total = dot(shifted_ref[...], jnp.concatenate(pieces, axis=1), 0, 0)
        for k in range(2):
            start = 256 * (2 * pair + k)
            total_ref[start : start + 256, :] = total[:, 128 * k : 128 * k + 128]
    own = pl.ds(pl.multiple_of(core_ref[0] * 1024, 1024), 1024)
    other = pl.ds(pl.multiple_of((1 - core_ref[0]) * 1024, 1024), 1024)
    for target, rows in ((late_keep_ref, own), (late_send_ref, other)):
        large = total_ref[rows, :].reshape(CHUNKS, 16, 128)
        for index in range(CHUNKS):
            taps = taps_ref[index] if index < 9 else jnp.zeros((8, 128), F32)
            target[index] = jnp.concatenate([large[index], taps], axis=0).astype(BF16)


def input_kernel(
    preact_mid_ref, preact_edge_ref, grad_one_ref, w_expand_ref, scale_ref, grad_input_ref
):
    for rows, source, first in (
        ((0, 7), preact_edge_ref, 0),
        ((1, 2), preact_mid_ref, 0),
        ((3, 4), preact_mid_ref, 256),
        ((5, 6), preact_mid_ref, 512),
    ):
        summed = jnp.zeros((256, D), F32)
        for pair in range(4):
            joined = jnp.concatenate(
                [source[2 * pair + k, first : first + 256, :] for k in range(2)], axis=1
            )
            summed = summed + dot(joined, w_expand_ref[:, 256 * pair : 256 * pair + 256], 1, 1)
        summed = summed * scale_ref[...]
        for k, row in enumerate(rows):
            value = grad_one_ref[row].astype(F32) + summed[COLS * k : COLS * k + COLS]
            grad_input_ref[row] = value.astype(BF16)


VMEM = pl.BlockSpec(memory_space=pltpu.VMEM)
SMEM = pl.BlockSpec(memory_space=pltpu.SMEM)
HBM = pl.BlockSpec(memory_space=pltpu.HBM)


def shape(dims, kind):
    return jax.ShapeDtypeStruct(dims, kind)


def call(kernel, ins, outs, scratch, smem=(), far=(), far_out=(), keep=(), limit=16, flops=10**9):
    ins = [pltpu.with_memory_space_constraint(x, pltpu.HBM) if k in far else x for k, x in enumerate(ins)]
    specs = [SMEM if k in smem else HBM if k in far else VMEM for k in range(len(ins))]
    return pl.pallas_call(
        kernel,
        out_shape=[
            pltpu.VMEM(o.shape, o.dtype)
            if k in keep
            else pltpu.HBM(o.shape, o.dtype)
            if k in far_out
            else o
            for k, o in enumerate(outs)
        ],
        in_specs=specs,
        out_specs=[HBM if k in far_out else VMEM for k in range(len(outs))],
        scratch_shapes=scratch,
        compiler_params=pltpu.CompilerParams(vmem_limit_bytes=limit * 1024 * 1024),
        cost_estimate=pl.CostEstimate(flops=flops, bytes_accessed=flops // 100, transcendentals=0),
    )(*ins)


CHUNKS = 64
CHUNK = 72
FACTOR = float((64 * 2048) ** (-0.5))


def pair_kernel(early_keep_ref, early_got_ref, late_keep_ref, late_got_ref, _, parts_ref):
    early = early_keep_ref[...].astype(F32) + early_got_ref[...].astype(F32)
    early = early.reshape(CHUNKS, 48, 128)
    late = late_keep_ref[...].astype(F32) + late_got_ref[...].astype(F32)
    parts_ref[...] = jnp.concatenate([early, late], axis=1).astype(BF16)


def sum_kernel(got_ref, out_ref):
    def step(index, total):
        return total + got_ref[index].astype(F32)

    total = lax.fori_loop(0, CHUNKS, step, jnp.zeros((CHUNK, 128), F32), unroll=8)
    total = total.astype(BF16)
    for index in range(CHUNKS):
        out_ref[index] = total


def unpack_half(half, parts_ref, targets):
    expand, kernel, project, qkv_block, out_block, qkv_grid, out_grid = targets
    blocks = (
        [(qkv_block, 128 * k, 256) for k in range(6)]
        + [(out_block, 128 * k, 256) for k in range(2)]
        + [(project, 128 * k, 1024) for k in range(2)]
        + [(qkv_grid, 128 * k, 256) for k in range(6)]
        + [(out_grid, 128 * k, 256) for k in range(2)]
    )
    places = [
        (target, start, column)
        for target, column, count in blocks
        for start in range(0, count, 16)
    ]
    for index in range(CHUNKS):
        value = parts_ref[index].astype(F32) * FACTOR
        for k in range(3):
            target, row, column = places[192 * half + 3 * index + k]
            target[row : row + 16, column : column + 128] = value[16 * k : 16 * k + 16]
        start = 1024 * half + 16 * index
        column = start // 256 * 128
        expand[start % 256 : start % 256 + 16, column : column + 128] = value[48:64]
        if half == 0 and index < 9:
            for block in range(BLOCKS):
                kernel[index : index + 1, 128 * block : 128 * block + 128] = value[
                    64 + block : 65 + block
                ]


def half_pieces(half, arrays):
    expand, kernel, project, qkv_block, out_block, qkv_grid, out_grid = arrays
    lanes = pl.ds(128 * half, 128)
    wide = pl.ds(512 * half, 512)
    pieces = [project.at[:, lanes], expand.at[:, wide]]
    return pieces + ([qkv_block, out_block, kernel] if half == 0 else [qkv_grid, out_grid])


def mine_kernel(core_ref, mine_ref, *targets):
    for half in range(2):

        @pl.when(core_ref[0] == half)
        def _():
            unpack_half(half, mine_ref, targets)


def other_kernel(core_ref, other_ref, *refs):
    done, outs, targets, sems = refs[:7], refs[7:14], refs[14:21], refs[21]
    for half in range(2):

        @pl.when(core_ref[0] == half)
        def _():
            copies = copy_all(zip(half_pieces(half, done), half_pieces(half, outs)), sems)
            unpack_half(1 - half, other_ref, targets)
            copies += copy_all(
                zip(half_pieces(1 - half, targets), half_pieces(1 - half, outs)), sems, first=5
            )
            wait_all(copies)


def beside_rows(pair, other):
    count = lax.axis_size("row")
    swaps = []
    for first in range(2):
        pairs = [(i, i + 1) for i in range(first, count - 1, 2)]
        swaps.append(pairs + [(j, i) for i, j in pairs])
    return lax.ppermute(pair, "row", swaps[0]), lax.ppermute(other, "row", swaps[1])


def beside_columns(near, after):
    axes = ("hi", "core")
    count = lax.axis_size("hi") * lax.axis_size("core")
    pairs = [(i, i + 1) for i in range(1, count - 1, 2)]
    swap = pairs + [(j, i) for i, j in pairs]
    return sibling(near), lax.ppermute(after, axes, swap)


def across(values):
    return lax.all_to_all(values, ("row", "hi"), split_axis=0, concat_axis=0, tiled=True)


def sibling(values):
    return lax.ppermute(values, "core", [(0, 1), (1, 0)])


def shards(
    x_input,
    grad_output,
    in_scale,
    in_shift,
    w_expand,
    dw_kernel,
    w_project,
    gain_block,
    w_qkv_block,
    w_out_block,
    bias_block,
    gain_grid,
    w_qkv_grid,
    w_out_grid,
    bias_grid,
):
    core_flag = lax.axis_index("core").reshape(1).astype(jnp.int32)
    scale = in_scale.reshape(1, D)
    shift = in_shift.reshape(1, D)
    gain_block = gain_block.reshape(1, D)
    gain_grid = gain_grid.reshape(1, D)
    hidden = shape((BLOCKS, TOKENS, 128), BF16)
    hidden_mid = shape((BLOCKS, 6 * COLS, 128), BF16)
    hidden_edge = shape((BLOCKS, 2 * COLS, 128), BF16)
    hidden_vmem = pltpu.VMEM(hidden.shape, BF16)
    mid_vmem = pltpu.VMEM(hidden_mid.shape, BF16)
    edge_vmem = pltpu.VMEM(hidden_edge.shape, BF16)
    pad_inner = pltpu.VMEM((BLOCKS, ROWS, WIDE, 128), F32)
    pad_edge = pltpu.VMEM((BLOCKS, 6, WIDE, 128), F32)
    tile = shape((ROWS, COLS, D), BF16)
    tokens = shape((TOKENS, D), BF16)
    tokens_vmem = pltpu.VMEM((TOKENS, D), BF16)
    edge_row = shape((144, D), BF16)
    edge_column = shape((ROWS, D), BF16)
    dma = pltpu.SemaphoreType.DMA

    x_input, w_expand, x_left, x_right = call(
        load_kernel,
        [x_input, w_expand],
        [tile, shape((D, E), BF16), edge_column, edge_column],
        [dma((2,)), pltpu.VMEM((2, ROWS, D), F32)],
        far=(0, 1),
        keep=range(4),
        limit=4,
    )
    x_left, x_right = beside_columns(x_left, x_right)
    later = [
        dw_kernel,
        grad_output,
        w_project,
        w_qkv_block,
        w_out_block,
        w_qkv_grid,
        w_out_grid,
    ]
    (
        lifted_far,
        slope_pre,
        lifted,
        dw_kernel,
        grad_output,
        w_project,
        w_qkv_block,
        w_out_block,
        w_qkv_grid,
        w_out_grid,
    ) = call(
        expand_kernel,
        [x_input, scale, shift, w_expand] + later,
        [hidden, hidden, hidden] + [shape(v.shape, v.dtype) for v in later],
        [hidden_vmem, dma((ROWS, 2)), dma((len(later),))],
        far=range(4, 4 + len(later)),
        far_out=(0, 1),
        keep=range(2, 3 + len(later)),
        limit=8,
        flops=4 * 10**9,
    )
    x_first, x_last = call(
        x_edge_kernel,
        [x_input, x_left, x_right],
        [edge_row, edge_row],
        [],
        keep=(0, 1),
        limit=4,
    )
    x_top, x_bottom = beside_rows(x_first, x_last)
    second_mid_far, second_mid, slope_mid, side_lifted = call(
        inner_rows_kernel,
        [lifted, x_left, x_right, scale, shift, w_expand, dw_kernel],
        [hidden_mid, hidden_mid, hidden_mid, shape((BLOCKS, 16, 128), F32)],
        [pad_inner, mid_vmem, dma((BLOCKS, 2))],
        far_out=(0, 2),
        keep=(1, 3),
        limit=12,
        flops=4 * 10**9,
    )
    cube = shape((2, 64, 256), F32)
    cube_block, cube_grid = call(
        bias_kernel,
        [bias_block, bias_grid],
        [cube, cube],
        [pltpu.VMEM((2 * HEADS, 256), F32)],
        keep=(0, 1),
        limit=8,
    )
    (
        second_edge_far,
        slope_edge,
        section_one,
        section_two,
        sendable,
        normed_block,
        joined,
        probs,
        mixture,
    ) = call(
        front_kernel,
        [
            x_input,
            x_top,
            x_bottom,
            lifted,
            side_lifted,
            second_mid,
            scale,
            shift,
            w_expand,
            dw_kernel,
            w_project,
            gain_block,
            w_qkv_block,
            w_out_block,
            cube_block,
            gain_grid,
            grad_output,
        ],
        [
            hidden_edge,
            hidden_edge,
            tile,
            tile,
            shape((64, 32, D), BF16),
            tokens,
            shape((TOKENS, 3 * D), BF16),
            shape((32, 64, 256), F32),
            tokens,
        ],
        [
            pad_edge,
            pltpu.VMEM((ROWS, COLS, D), F32),
            pltpu.VMEM((ROWS, COLS, D), F32),
            edge_vmem,
            edge_vmem,
            pltpu.VMEM(tile.shape, BF16),
            pltpu.VMEM(tile.shape, BF16),
            tokens_vmem,
            pltpu.VMEM((TOKENS, 3 * D), BF16),
            pltpu.VMEM((32, 64, 256), F32),
            tokens_vmem,
            dma((3,)),
            dma((4, 5)),
        ],
        keep=(4,),
        far_out=(0, 1, 2, 3, 5, 6, 7, 8),
        limit=20,
    )

    got = across(sendable)
    grad_groups, grid_total = call(
        grid_kernel,
        [got, w_qkv_grid, w_out_grid, cube_grid],
        [shape((64, 16, D), BF16), shape((2048, 128), BF16)],
        [
            tokens_vmem,
            pltpu.VMEM((TOKENS, 3 * D), BF16),
            pltpu.VMEM((2, TOKENS, D), BF16),
            pltpu.VMEM((64, 16, D), F32),
        ],
        keep=(0, 1),
        limit=8,
    )
    returned = across(grad_groups).reshape(ROWS, COLS, D)

    half_tile = shape((ROWS, COLS // 2, D), BF16)
    half_inner = shape((BLOCKS, ROWS, COLS // 2, 128), BF16)
    block_total = shape((2048, 128), F32)
    half_read = [
        half_tile,
        shape((TOKENS // 2, 3 * D), BF16),
        shape((16, 64, 256), F32),
        half_tile,
        half_inner,
        shape((TOKENS // 2, D), BF16),
        shape((TOKENS // 2, D), BF16),
    ]
    half_scratch = [pltpu.VMEM(o.shape, o.dtype) for o in half_read]
    weights = [gain_grid, gain_block, w_qkv_block, w_out_block, w_project]
    one_outer, inner_outer, first_total, near, after, *ahead = call(
        functools.partial(block_kernel, (0, 3)),
        [
            returned,
            grad_output,
            section_two,
            joined,
            probs,
            section_one,
            slope_mid.reshape(BLOCKS, 6, COLS, 128),
            slope_edge.reshape(BLOCKS, 2, COLS, 128),
            normed_block,
            mixture,
            *weights,
        ],
        [half_tile, half_inner, block_total]
        + [shape((BLOCKS, ROWS, 128), BF16)] * 2
        + half_read,
        [pltpu.VMEM((2, BLOCKS, ROWS, 128), F32), half_scratch[0]]
        + half_scratch
        + [dma((3,)), dma((36,))],
        far=range(2, 10),
        far_out=(0,),
        keep=range(1, 12),
        limit=12,
        flops=4 * 10**9,
    )
    left, right = beside_columns(near, after)
    one_middle, inner_middle, block_total = call(
        functools.partial(block_kernel, (1, 2)),
        [returned, grad_output, *ahead, ahead[0], *weights, first_total],
        [half_tile, half_inner, shape((2048, 128), BF16)],
        [pltpu.VMEM((2048, 128), BF16), half_scratch[0], dma((3,))],
        far_out=(0, 2),
        keep=(1,),
        limit=10,
        flops=4 * 10**9,
    )
    edge_cells = shape((BLOCKS, 144, 128), BF16)
    first, last = call(
        inner_edge_kernel,
        [inner_outer, inner_middle, left, right],
        [edge_cells, edge_cells],
        [],
        keep=(0, 1),
        limit=4,
    )
    top, bottom = beside_rows(first, last)
    early = shape((3072, 128), BF16)
    grad_one, early_send, early_keep = call(
        total_kernel,
        [
            core_flag,
            one_outer,
            one_middle,
            second_mid_far,
            second_edge_far,
            block_total,
            grid_total,
            first,
        ],
        [tile, early, early],
        [pltpu.VMEM((6144, 128), BF16), hidden_vmem, dma((8,))],
        smem=(0,),
        far=range(1, 7),
        keep=range(3),
        limit=8,
        flops=3 * 10**9,
    )
    preact_mid, taps_mid = call(
        back_inner_kernel,
        [lifted_far, slope_pre, inner_outer, inner_middle, left, right, dw_kernel],
        [hidden_mid, shape((9, BLOCKS, 128), F32)],
        [pad_inner, mid_vmem, mid_vmem, dma((BLOCKS, 2))],
        far=(0, 1),
        keep=(0, 1),
        limit=12,
        flops=4 * 10**9,
    )
    early_got = sibling(early_send)
    late = shape((CHUNKS, 24, 128), BF16)
    parts = shape((CHUNKS, CHUNK, 128), BF16)
    preact_edge, late_send, late_keep = call(
        back_kernel,
        [
            core_flag,
            x_input,
            lifted_far,
            slope_pre,
            inner_outer,
            inner_middle,
            top,
            bottom,
            left,
            right,
            scale,
            shift,
            dw_kernel,
            preact_mid,
            taps_mid,
            early_keep,
        ],
        [hidden_edge, late, late],
        [
            pad_edge,
            edge_vmem,
            edge_vmem,
            tokens_vmem,
            pltpu.VMEM((2048, 128), F32),
            pltpu.VMEM((9, BLOCKS, 128), F32),
            dma((4,)),
        ],
        smem=(0,),
        far=(2, 3),
        keep=(0, 1, 2),
        limit=12,
        flops=4 * 10**9,
    )
    (grad_input,) = call(
        input_kernel, [preact_mid, preact_edge, grad_one, w_expand, scale], [tile], [], limit=8
    )

    (paired,) = call(
        pair_kernel,
        [early_keep, early_got, late_keep, sibling(late_send), grad_input],
        [parts],
        [],
        far=(4,),
        keep=(0,),
        limit=4,
    )
    (summed,) = call(sum_kernel, [across(paired)], [parts], [], keep=(0,), limit=4)
    mine = across(summed)
    sums = [
        shape((D, E), F32),
        shape((9, E), F32),
        shape((E, D), F32),
        shape((D, 3 * D), F32),
        shape((D, D), F32),
        shape((D, 3 * D), F32),
        shape((D, D), F32),
    ]
    done = call(
        mine_kernel,
        [core_flag, mine],
        sums,
        [],
        smem=(0,),
        keep=range(7),
        limit=4,
        flops=2 * 10**9,
    )
    totals = call(
        other_kernel,
        [core_flag, sibling(mine), *done],
        sums,
        [pltpu.VMEM(o.shape, F32) for o in sums] + [dma((10,))],
        smem=(0,),
        far_out=range(7),
        limit=10,
    )
    return (grad_input, *totals)


def solution(mesh):
    split = Mesh(mesh.devices.reshape(8, 8, 2), ("row", "hi", "core"))
    tile = P("row", ("hi", "core"), None)
    return jax.shard_map(
        shards,
        mesh=split,
        in_specs=(tile, tile) + (P(),) * 13,
        out_specs=(tile,) + (P(),) * 7,
        check_vma=False,
    )
```
